32 devices in a mesh: dp: 8 (over y, x, core), mp: 4 (over z).
Axes of the slice: x: 2, y: 2, z: 4, core: 2. Of those that a mesh axis runs over, the one named last changes fastest.
Arguments:
- inputs: float32 [64, 14, 14, 320], P('dp'), may hold values from -60 to 60
- conv_weight: float32 [2, 9, 320], replicated, may hold values from -2 to 2
- batch_gain: float32 [2, 320], replicated, may hold values from 0.25 to 1.75
- batch_bias: float32 [2, 320], replicated, may hold values from -3 to 3
- mix_width: bfloat16 [2, 14, 14], replicated, may hold values from -1.5 to 1.5
- mix_height: bfloat16 [2, 14, 14], replicated, may hold values from -1.5 to 1.5
- unite_weight: bfloat16 [2, 960, 320], P(None, 'dp'), may hold values from -0.1875 to 0.1875
- layer_gain: float32 [2, 320], replicated, may hold values from 0.25 to 1.75
- up_weight: bfloat16 [2, 320, 1280], P(None, 'dp', 'mp'), may hold values from -0.3125 to 0.3125
- up_bias: float32 [2, 1280], replicated, may hold values from -3 to 3
- down_weight: bfloat16 [2, 320, 1280], P(None, 'dp', 'mp'), may hold values from -0.25 to 0.25
- cotangent: float32 [64, 14, 14, 320], P('dp'), may hold values from -6 to 6
Outputs:
- output: float32 [64, 14, 14, 320], P('dp')
- input_grad: float32 [64, 14, 14, 320], P('dp')
- kernel_grad: float32 [2, 9, 320], replicated
- scale_grad: float32 [2, 320], replicated
- offset_grad: float32 [2, 320], replicated
- width_grad: float32 [2, 14, 14], replicated
- height_grad: float32 [2, 14, 14], replicated
- unite_grad: float32 [2, 960, 320], P(None, 'dp')
- gain_grad: float32 [2, 320], replicated
- up_grad: float32 [2, 320, 1280], P(None, 'dp', 'mp')
- bias_grad: float32 [2, 1280], P(None, 'mp')
- down_grad: float32 [2, 320, 1280], P(None, 'dp', 'mp')
- stream_rms: float32 [2, 3], replicated
The draws below stay inside these ranges and needn't reach their ends.
All inputs are finite; a program needn't handle non-finite values.
Results may differ from the reference program's by a relative error of at most 0.015.
Values may be sent and summed in bfloat16 or wider, within the bound.
No kernel may reach another device: no remote copies, remote signals or barrier semaphores. Data moves between devices by JAX's collectives and lax.ppermute only.
A program may use at most 128 MiB of HBM per device.

```python
import math
import jax
import jax.numpy as jnp
from jax import lax

D = 320
HID = 1280
SIDE = 14
LAYERS = 2
IMAGES = 64


def draw_inputs(key, part):
    key = jax.random.fold_in(key, 7)
    subkeys = jax.random.split(key, 3)
    position = jnp.arange(IMAGES, dtype=jnp.float32) / max(IMAGES - 1, 1)
    image_scale = (3.0 ** position)[:, None, None, None]
    channel_scale = jnp.exp(jax.random.uniform(subkeys[1], (D,), jnp.float32, math.log(0.3), math.log(3.0)))
    cell_scale = jax.random.uniform(subkeys[2], (IMAGES, SIDE, SIDE, 1), jnp.float32, 0.6, 1.4)
    noise_part = jnp.clip(jax.random.normal(subkeys[0], (IMAGES, SIDE, SIDE, D), jnp.float32), -4.0, 4.0)
    return noise_part * cell_scale * channel_scale * image_scale


def steps_of(stream_key, shape, cuts, low, largest):
    loudness = 1.0
    for dim, blocks in cuts:
        draws = jax.random.uniform(jax.random.fold_in(jax.random.fold_in(stream_key, 6), dim), (blocks,), jnp.float32, low / len(cuts), largest / len(cuts))
        loudness = loudness * jnp.repeat(jnp.exp(draws), shape[dim] // blocks).reshape((-1,) + (1,) * (len(shape) - 1 - dim))
    return loudness


def bell_draw(stream_key, extent, scale, reach, cuts=(), held_as=jnp.bfloat16):
    values = scale * jax.random.normal(stream_key, extent, jnp.float32)
    if cuts:
        values = values * steps_of(stream_key, extent, cuts, -0.22, 0.18)
    return jnp.clip(values, -reach, reach).astype(held_as)


def setup_inputs(seed: int = 0) -> dict:
    arg_keys = jax.random.split(jax.random.key(seed), 13)
    return {
        "inputs": draw_inputs(jax.random.fold_in(arg_keys[12], 71), 0),
        "conv_weight": bell_draw(arg_keys[1], (LAYERS, 9, D), 0.33, 2.0, (), jnp.float32),
        "batch_gain": jnp.clip(1.0 + 0.15 * jax.random.normal(arg_keys[2], (LAYERS, D), jnp.float32), 0.25, 1.75),
        "batch_bias": bell_draw(arg_keys[3], (LAYERS, D), 0.5, 3.0, (), jnp.float32),
        "mix_width": bell_draw(arg_keys[4], (LAYERS, SIDE, SIDE), SIDE ** -0.5, 1.5),
        "mix_height": bell_draw(arg_keys[5], (LAYERS, SIDE, SIDE), SIDE ** -0.5, 1.5),
        "unite_weight": bell_draw(arg_keys[6], (LAYERS, 3 * D, D), (3 * D) ** -0.5, 0.1875, ((1, 8),)),
        "layer_gain": jnp.clip(1.0 + 0.15 * jax.random.normal(arg_keys[7], (LAYERS, D), jnp.float32), 0.25, 1.75),
        "up_weight": bell_draw(arg_keys[8], (LAYERS, D, HID), D ** -0.5, 0.3125, ((1, 8), (2, 4))),
        "up_bias": bell_draw(arg_keys[9], (LAYERS, HID), 0.5, 3.0, (), jnp.float32),
        "down_weight": bell_draw(arg_keys[10], (LAYERS, D, HID), (HID // 2) ** -0.5, 0.25, ((1, 8), (2, 4))),
        "cotangent": bell_draw(arg_keys[11], (IMAGES, SIDE, SIDE, D), 1.0, 6.0, ((0, 8),), jnp.float32),
    }


EPSILON = 1e-05
HIGHEST_PRECISION = lax.Precision.HIGHEST

@jax.custom_vjp
def low(v):
    return lax.optimization_barrier(v.astype(jnp.bfloat16)).astype(jnp.float32)

@jax.custom_vjp
def low_back(v):
    return v

def low_keep(v):
    return (low(v), None)

def low_pass(kept, grad):
    return (grad,)

def back_keep(v):
    return (v, None)

def back_low(kept, grad):
    return (low(grad),)
low.defvjp(low_keep, low_pass)
low_back.defvjp(back_keep, back_low)

def depthwise(stream, kernel):
    map_side = stream.shape[1]
    padded = jnp.pad(stream, ((0, 0), (1, 1), (1, 1), (0, 0)))
    summed = jnp.zeros_like(stream)
    for row_shift in range(3):
        for col_shift in range(3):
            summed = summed + padded[:, row_shift:row_shift + map_side, col_shift:col_shift + map_side, :] * kernel[3 * row_shift + col_shift]
    return summed

def layer_norm(rows, gain):
    center = lax.optimization_barrier(jnp.mean(rows, axis=-1, keepdims=True))
    deviate = rows - center
    spread = lax.optimization_barrier(jnp.mean(deviate * deviate, axis=-1, keepdims=True))
    return deviate * lax.rsqrt(spread + EPSILON) * gain

def root_square(values):
    return jnp.sqrt(jnp.mean(values * values))

def block(stream, params):
    kernel, bn_scale, bn_shift, mixer_w, mixer_h, unite_proj, norm_gain, up_proj, up_shift, down_proj = params
    features = stream.shape[-1]
    convolved = depthwise(stream, kernel)
    center = lax.optimization_barrier(jnp.mean(convolved, axis=(0, 1, 2)))
    spread = lax.optimization_barrier(jnp.mean(jnp.square(convolved - center), axis=(0, 1, 2)))
    normed = (convolved - center) * lax.rsqrt(spread + EPSILON)
    branch = low(normed * bn_scale + bn_shift)
    along_w = low(low_back(jnp.einsum('vw,nhwc->nhvc', mixer_w, branch, precision=HIGHEST_PRECISION)))
    along_h = low(low_back(jnp.einsum('vh,nhwc->nvwc', mixer_h, branch, precision=HIGHEST_PRECISION)))
    joined = jnp.concatenate([branch, along_w, along_h], axis=-1).reshape(-1, 3 * features)
    united_out = low_back(jnp.dot(joined, unite_proj, precision=HIGHEST_PRECISION))
    residual = stream.reshape(-1, features) + united_out
    normal_rows = low(layer_norm(residual, norm_gain))
    hidden_pre = low_back(jnp.dot(normal_rows, up_proj, precision=HIGHEST_PRECISION) + up_shift)
    hidden = low(jax.nn.gelu(hidden_pre, approximate=False))
    mlp_out = low_back(jnp.dot(hidden, down_proj.T, precision=HIGHEST_PRECISION))
    result = residual + mlp_out
    measures = jnp.stack([root_square(united_out), root_square(mlp_out), root_square(result)])
    return (result.reshape(stream.shape), measures)

def reference(inputs, conv_weight, batch_gain, batch_bias, mix_width, mix_height, unite_weight, layer_gain, up_weight, up_bias, down_weight, cotangent):
    params = tuple((tensor.astype(jnp.float32) for tensor in (conv_weight, batch_gain, batch_bias, mix_width, mix_height, unite_weight, layer_gain, up_weight, up_bias, down_weight)))

    def forward(stream, weights):
        measure_list = []
        for layer_index in range(LAYERS):
            stream, measures = block(stream, tuple((tensor[layer_index] for tensor in weights)))
            measure_list.append(measures)
        return (stream, jnp.stack(measure_list))
    output, pullback, stream_rms = jax.vjp(forward, inputs, params, has_aux=True)
    input_grad, weight_grads = pullback(cotangent)
    return (output, input_grad, weight_grads[0], weight_grads[1], weight_grads[2], weight_grads[3], weight_grads[4], weight_grads[5], weight_grads[6], weight_grads[7], weight_grads[8], weight_grads[9], stream_rms)
```

```python
import functools

import jax
import jax.numpy as jnp
from jax import lax
from jax.experimental import pallas as pl
from jax.experimental.pallas import tpu as pltpu
from jax.sharding import PartitionSpec as P

EPSILON = 1e-05
WIDE = 16
VMEM_LIMIT = 50 * 1024 * 1024
F32 = jnp.float32
BF16 = jnp.bfloat16


def dot(left, right):
    return lax.dot_general(left, right, (((1,), (0,)), ((), ())), preferred_element_type=F32)


def dot_cols(left, right):
    return lax.dot_general(left, right, (((1,), (1,)), ((), ())), preferred_element_type=F32)


def dot_rows(left, right):
    return lax.dot_general(left, right, (((0,), (0,)), ((), ())), preferred_element_type=F32)


def valid_rows(rows, side):
    return lax.broadcasted_iota(jnp.int32, (rows, 1), 0) % WIDE < side


def three_shifts(image):
    rows, features = image.shape
    empty = jnp.zeros((WIDE, features), image.dtype)
    padded = jnp.concatenate([empty, image, empty], axis=0)
    total = rows + 2 * WIDE
    return pltpu.roll(padded, 1, 0), padded, pltpu.roll(padded, total - 1, 0)


def convolve(image, taps, side):
    rows = image.shape[0]
    shifted = three_shifts(image)
    summed = None
    for i in range(3):
        for j in range(3):
            term = shifted[j][WIDE * i : WIDE * i + rows] * taps[3 * i + j : 3 * i + j + 1]
            summed = term if summed is None else summed + term
    return jnp.where(valid_rows(rows, side), summed, 0.0)


def local_moments(conv_ref, moments_ref, images, side):
    rows = side * WIDE
    count = images * side * side
    total = None
    for n in range(images):
        part = jnp.sum(conv_ref[n * rows : (n + 1) * rows, :], axis=0, keepdims=True)
        total = part if total is None else total + part
    mean = total / count
    squares = None
    for n in range(images):
        deviate = jnp.where(
            valid_rows(rows, side), conv_ref[n * rows : (n + 1) * rows, :] - mean, 0.0
        )
        part = jnp.sum(deviate * deviate, axis=0, keepdims=True)
        squares = part if squares is None else squares + part
    moments_ref[0:1, :] = mean
    moments_ref[1:2, :] = squares


def whole_moments(gathered_ref, count):
    devices = gathered_ref.shape[0]
    means = gathered_ref[:, 0, :]
    squares = gathered_ref[:, 1, :]
    center = jnp.sum(means, axis=0, keepdims=True) / devices
    apart = means - center
    spread = (
        jnp.sum(squares, axis=0, keepdims=True)
        + jnp.sum(apart * apart, axis=0, keepdims=True) * count
    ) / (count * devices)
    return center, lax.rsqrt(spread + EPSILON)


def mixing_matrices(mix_w, mix_h, side):
    cells = side * WIDE
    row = lax.broadcasted_iota(jnp.int32, (cells, side), 0)
    col = lax.broadcasted_iota(jnp.int32, (cells, side), 1)
    at_w = (row % WIDE == col).astype(BF16)
    at_h = (row // WIDE == col).astype(BF16)
    out = lax.broadcasted_iota(jnp.int32, (cells, cells), 0)
    inp = lax.broadcasted_iota(jnp.int32, (cells, cells), 1)
    same_h = out // WIDE == inp // WIDE
    same_w = (out % WIDE == inp % WIDE) & (out % WIDE < side)

    def spread(picks, mix, keep, flip):
        left = (dot_cols if flip else dot)(picks, mix).astype(BF16)
        return jnp.where(keep, dot_cols(left, picks), 0.0).astype(BF16)

    forward = jnp.concatenate(
        [spread(at_w, mix_w, same_h, False), spread(at_h, mix_h, same_w, False)], axis=0
    )
    backward = jnp.concatenate(
        [spread(at_w, mix_w, same_h, True), spread(at_h, mix_h, same_w, True)], axis=1
    )
    return forward, backward


def by_image(maps_ref, all_ref):
    side, _, held, features = maps_ref.shape
    empty = jnp.zeros((WIDE - side, held, features), F32)
    for h in range(side):
        lines = jnp.concatenate([maps_ref[h], empty], axis=0)
        all_ref[:, h * WIDE : (h + 1) * WIDE, :] = jnp.swapaxes(lines, 0, 1)


def first_kernel(
    place_ref,
    stream_ref,
    taps_ref,
    mix_w_ref,
    mix_h_ref,
    own_ref,
    conv_ref,
    moments_ref,
    forward_ref,
    backward_ref,
    all_ref,
    *,
    images,
    side,
):
    rows = side * WIDE
    by_image(stream_ref, all_ref)
    for n in range(images):
        own_ref[n * rows : (n + 1) * rows, :] = all_ref[place_ref[0] * images + n]
    taps = taps_ref[0]
    for n in range(images):
        conv_ref[n * rows : (n + 1) * rows, :] = convolve(
            own_ref[n * rows : (n + 1) * rows, :], taps, side
        )
    local_moments(conv_ref, moments_ref, images, side)
    for layer in range(mix_w_ref.shape[0]):
        forward, backward = mixing_matrices(mix_w_ref[layer], mix_h_ref[layer], side)
        forward_ref[layer] = forward
        backward_ref[layer] = backward


def unpack_mlp(packed_ref, up_ref, down_ref):
    shards, both, _ = packed_ref.shape
    half = both // 2
    ups, downs = [], []
    for s in range(shards):
        piece = packed_ref[s].astype(F32)
        ups.append(piece[:half])
        downs.append(piece[half:])
    up_ref[...] = jnp.concatenate(ups, axis=0).astype(BF16)
    down_ref[...] = jnp.concatenate(downs, axis=0).astype(BF16)


def forward_image(
    conv,
    stream,
    center,
    inv_std,
    bn_gain,
    bn_bias,
    mixing,
    unite_ref,
    norm_gain,
    up_ref,
    up_bias,
    down_ref,
    side,
):
    rows, features = conv.shape
    valid = valid_rows(rows, side)
    ahat = (conv - center) * inv_std
    branch = jnp.where(valid, ahat * bn_gain + bn_bias, 0.0).astype(BF16)
    along = dot(mixing, branch).astype(BF16)
    along_w, along_h = along[:rows], along[rows:]
    united = (
        dot(branch, unite_ref[0:features, :])
        + dot(along_w, unite_ref[features : 2 * features, :])
        + dot(along_h, unite_ref[2 * features :, :])
    )
    resid = stream + united
    mid = jnp.sum(resid, axis=-1, keepdims=True) / features
    deviate = resid - mid
    spread = jnp.sum(deviate * deviate, axis=-1, keepdims=True) / features
    inv_norm = lax.rsqrt(spread + EPSILON)
    uhat = deviate * inv_norm
    normal = (uhat * norm_gain).astype(BF16)
    pre = dot(normal, up_ref[...]) + up_bias
    below = 0.5 + 0.5 * lax.erf(pre * (0.5**0.5))
    slope = below + pre * (jnp.exp(-0.5 * pre * pre) * 0.3989422804014327)
    hidden = (pre * below).astype(BF16)
    mlp = jnp.where(valid, dot_cols(hidden, down_ref[...]), 0.0)
    result = resid + mlp
    squares = jnp.concatenate(
        [jnp.sum(v * v, axis=0, keepdims=True) for v in (united, mlp, result)], axis=0
    )
    return dict(
        ahat=ahat,
        branch=branch,
        along_w=along_w,
        along_h=along_h,
        uhat=uhat,
        inv_norm=inv_norm,
        normal=normal,
        slope=slope,
        hidden=hidden,
        result=result,
        squares=squares,
    )


def backward_image(
    grad, ahat, branch, uhat, inv_norm, slope, mixing_back, unite_ref, norm_gain, up_ref, down_ref
):
    rows, features = grad.shape
    grad_low = grad.astype(BF16)
    gh = dot(grad_low, down_ref[...])
    gpre = (gh * slope).astype(BF16)
    bias = jnp.sum(gpre.astype(F32), axis=0, keepdims=True)
    gn = dot_cols(gpre, up_ref[...])
    gain = jnp.sum(gn * uhat, axis=0, keepdims=True)
    q = gn * norm_gain
    mean_q = jnp.sum(q, axis=-1, keepdims=True) / features
    mean_qu = jnp.sum(q * uhat, axis=-1, keepdims=True) / features
    gu = grad + inv_norm * (q - mean_q - uhat * mean_qu)
    gc = gu.astype(BF16)
    direct = dot_cols(gc, unite_ref[0:features, :])
    wide = dot_cols(gc, unite_ref[features : 2 * features, :]).astype(BF16)
    tall = dot_cols(gc, unite_ref[2 * features :, :]).astype(BF16)
    both = jnp.concatenate([wide, tall], axis=0)
    gb = direct + dot(mixing_back, both)
    cross = dot_cols(both, branch)
    return dict(
        grad_low=grad_low,
        gpre=gpre,
        bias=bias,
        gain=gain,
        gu=gu,
        gc=gc,
        gb=gb,
        cross=cross,
        offset=jnp.sum(gb, axis=0, keepdims=True),
        scale=jnp.sum(gb * ahat, axis=0, keepdims=True),
    )


def mixing_grads(cross, side):
    cells = side * WIDE
    out = lax.broadcasted_iota(jnp.int32, (cells, cells), 0)
    inp = lax.broadcasted_iota(jnp.int32, (cells, cells), 1)
    same_h = out // WIDE == inp // WIDE
    same_w = out % WIDE == inp % WIDE
    row = lax.broadcasted_iota(jnp.int32, (cells, WIDE), 0)
    col = lax.broadcasted_iota(jnp.int32, (cells, WIDE), 1)
    exact = functools.partial(
        lax.dot_general, precision=lax.Precision.HIGHEST, preferred_element_type=F32
    )

    def fold(values, keep, picks):
        picks = picks.astype(F32)
        half = exact(jnp.where(keep, values, 0.0), picks, (((1,), (0,)), ((), ())))
        return exact(picks, half, (((0,), (0,)), ((), ())))

    width = fold(cross[:cells], same_h, row % WIDE == col)
    height = fold(cross[cells:], same_w, row // WIDE == col)
    return width, height


def conv_back_image(gb, ahat, stream, gu, center_scale, offset_mean, scale_mean, taps, side):
    rows = gb.shape[0]
    valid = valid_rows(rows, side)
    ga = jnp.where(valid, center_scale * (gb - offset_mean - ahat * scale_mean), 0.0)
    shifted = three_shifts(stream)
    kernel_grads = []
    for i in range(3):
        for j in range(3):
            kernel_grads.append(
                jnp.sum(ga * shifted[j][WIDE * i : WIDE * i + rows], axis=0, keepdims=True)
            )
    turned = three_shifts(ga)
    summed = gu
    for i in range(3):
        for j in range(3):
            summed = (
                summed
                + turned[2 - j][WIDE * (2 - i) : WIDE * (2 - i) + rows]
                * taps[3 * i + j : 3 * i + j + 1]
            )
    return jnp.where(valid, summed, 0.0), jnp.concatenate(kernel_grads, axis=0)


def add_up(total, part):
    return part if total is None else total + part


def stage_forward(
    layer,
    gathered_ref,
    conv_ref,
    stream_ref,
    gain_ref,
    bias_ref,
    mixing_ref,
    unite_ref,
    norm_gain_ref,
    packed_ref,
    up_bias_ref,
    taps_ref,
    result_ref,
    next_conv_ref,
    next_moments_ref,
    stats_ref,
    branch_ref,
    along_w_ref,
    along_h_ref,
    uhat_ref,
    inv_norm_ref,
    normal_ref,
    slope_ref,
    hidden_ref,
    squares_ref,
    up_ref,
    down_ref,
    *,
    images,
    side,
):
    rows = side * WIDE
    unpack_mlp(packed_ref, up_ref, down_ref)
    center, inv_std = whole_moments(gathered_ref, images * side * side)
    stats_ref[0:1, :] = center
    stats_ref[1:2, :] = inv_std
    squares = None
    for n in range(images):
        at = slice(n * rows, (n + 1) * rows)
        kept = forward_image(
            conv_ref[at, :],
            stream_ref[at, :],
            center,
            inv_std,
            gain_ref[layer : layer + 1, :],
            bias_ref[layer : layer + 1, :],
            mixing_ref[layer],
            unite_ref,
            norm_gain_ref[layer : layer + 1, :],
            up_ref,
            up_bias_ref[layer : layer + 1, :],
            down_ref,
            side,
        )
        branch_ref[at, :] = kept["branch"]
        along_w_ref[at, :] = kept["along_w"]
        along_h_ref[at, :] = kept["along_h"]
        uhat_ref[at, :] = kept["uhat"]
        inv_norm_ref[at, :] = kept["inv_norm"]
        normal_ref[at, :] = kept["normal"]
        slope_ref[at, :] = kept["slope"].astype(slope_ref.dtype)
        hidden_ref[at, :] = kept["hidden"]
        result_ref[at, :] = kept["result"].astype(result_ref.dtype)
        squares = add_up(squares, kept["squares"])
        if next_conv_ref is not None:
            next_conv_ref[at, :] = convolve(kept["result"], taps_ref[layer + 1], side)
    squares_ref[...] = squares
    if next_conv_ref is not None:
        local_moments(next_conv_ref, next_moments_ref, images, side)


def stage_backward(
    layer,
    grad_of,
    center,
    inv_std,
    conv_ref,
    mixing_back_ref,
    unite_ref,
    norm_gain_ref,
    branch_ref,
    along_w_ref,
    along_h_ref,
    uhat_ref,
    inv_norm_ref,
    normal_ref,
    slope_ref,
    hidden_ref,
    up_ref,
    down_ref,
    gb_ref,
    gu_ref,
    sums_ref,
    unite_grad_ref,
    mlp_grad_ref,
    norm_grad_ref,
    bias_grad_ref,
    width_ref,
    height_ref,
    grad_low_ref,
    gpre_ref,
    gc_ref,
    *,
    images,
    side,
):
    rows = side * WIDE
    offset = scale = gain = bias = cross = None
    for n in range(images):
        at = slice(n * rows, (n + 1) * rows)
        found = backward_image(
            grad_of(n),
            (conv_ref[at, :] - center) * inv_std,
            branch_ref[at, :],
            uhat_ref[at, :],
            inv_norm_ref[at, :],
            slope_ref[at, :].astype(F32),
            mixing_back_ref[layer],
            unite_ref,
            norm_gain_ref[layer : layer + 1, :],
            up_ref,
            down_ref,
        )
        grad_low_ref[at, :] = found["grad_low"]
        gpre_ref[at, :] = found["gpre"]
        gc_ref[at, :] = found["gc"]
        gb_ref[at, :] = found["gb"]
        gu_ref[at, :] = found["gu"]
        offset = add_up(offset, found["offset"])
        scale = add_up(scale, found["scale"])
        gain = add_up(gain, found["gain"])
        bias = add_up(bias, found["bias"])
        cross = add_up(cross, found["cross"])
    sums_ref[0:1, :] = offset
    sums_ref[1:2, :] = scale
    norm_grad_ref[...] = gain
    bias_grad_ref[...] = bias
    width, height = mixing_grads(cross, side)
    width_ref[...] = width
    height_ref[...] = height
    features = gc_ref.shape[1]
    gc = gc_ref[...]
    for index, part in enumerate((branch_ref, along_w_ref, along_h_ref)):
        unite_grad_ref[index * features : (index + 1) * features, :] = dot_rows(
            part[...], gc
        ).astype(BF16)
    mlp_grad_ref[0] = dot_rows(normal_ref[...], gpre_ref[...]).astype(BF16)
    mlp_grad_ref[1] = dot_rows(grad_low_ref[...], hidden_ref[...]).astype(BF16)


def middle_kernel(*refs, images, side, layer):
    (gathered, conv, stream, gain, bias, mixing, unite, norm_gain, packed, up_bias, taps) = refs[:11]
    outs = refs[11:25]
    up, down = refs[25:]
    stage_forward(
        layer,
        gathered, conv, stream, gain, bias, mixing, unite, norm_gain, packed, up_bias, taps,
        *outs, up, down, images=images, side=side,
    )


def last_kernel(*refs, images, side, layer):
    (
        place, gathered, conv, stream, gain, bias, mixing, unite, norm_gain, packed, up_bias, taps,
        mixing_back, cotangent,
    ) = refs[:14]
    (
        result, stats, squares, gb, gu, sums, unite_grad, mlp_grad, norm_grad, bias_grad, width, height,
    ) = refs[14:26]
    (
        branch, along_w, along_h, uhat, inv_norm, normal, slope, hidden, up, down, grad_low, gpre, gc, own,
    ) = refs[26:]
    stage_forward(
        layer,
        gathered, conv, stream, gain, bias, mixing, unite, norm_gain, packed, up_bias, taps,
        result, None, None, stats, branch, along_w, along_h, uhat, inv_norm, normal, slope, hidden,
        squares, up, down, images=images, side=side,
    )
    by_image(cotangent, own)

    def grad_of(n):
        return own[place[0] * images + n]

    stage_backward(
        layer, grad_of, stats[0:1, :], stats[1:2, :], conv, mixing_back, unite, norm_gain,
        branch, along_w, along_h, uhat, inv_norm, normal, slope, hidden, up, down,
        gb, gu, sums, unite_grad, mlp_grad, norm_grad, bias_grad, width, height, grad_low, gpre, gc,
        images=images, side=side,
    )


def conv_back(
    layer, gathered_ref, gb_ref, gu_ref, conv_ref, stream_ref, stats_ref, gain_ref, taps_ref, totals_ref,
    kernel_ref, *, images, side,
):
    rows = side * WIDE
    cells = images * side * side * gathered_ref.shape[0]
    offset = jnp.sum(gathered_ref[:, 0, :], axis=0, keepdims=True)
    scale = jnp.sum(gathered_ref[:, 1, :], axis=0, keepdims=True)
    totals_ref[0:1, :] = offset
    totals_ref[1:2, :] = scale
    center, inv_std = stats_ref[0:1, :], stats_ref[1:2, :]
    factor = gain_ref[layer : layer + 1, :] * inv_std
    grads, kernel = [], None
    for n in range(images):
        at = slice(n * rows, (n + 1) * rows)
        grad, part = conv_back_image(
            gb_ref[at, :],
            (conv_ref[at, :] - center) * inv_std,
            stream_ref[at, :],
            gu_ref[at, :],
            factor,
            offset / cells,
            scale / cells,
            taps_ref[layer],
            side,
        )
        grads.append(grad)
        kernel = add_up(kernel, part)
    kernel_ref[...] = kernel
    return grads


def between_kernel(*refs, images, side, layer):
    (
        gathered, gb_up, gu_up, conv_up, stream_up, stats_up, gain, taps,
        conv, stats, mixing_back, unite, norm_gain, packed,
        branch, along_w, along_h, uhat, inv_norm, normal, slope, hidden,
    ) = refs[:22]
    (
        totals, kernel, gb, gu, sums, unite_grad, mlp_grad, norm_grad, bias_grad, width, height,
    ) = refs[22:33]
    up, down, grad_low, gpre, gc = refs[33:]
    unpack_mlp(packed, up, down)
    grads = conv_back(
        layer + 1, gathered, gb_up, gu_up, conv_up, stream_up, stats_up, gain, taps, totals, kernel,
        images=images, side=side,
    )
    stage_backward(
        layer, lambda n: grads[n], stats[0:1, :], stats[1:2, :], conv, mixing_back, unite, norm_gain,
        branch, along_w, along_h, uhat, inv_norm, normal, slope, hidden, up, down,
        gb, gu, sums, unite_grad, mlp_grad, norm_grad, bias_grad, width, height, grad_low, gpre, gc,
        images=images, side=side,
    )


def end_kernel(*refs, images, side):
    (gathered, gb, gu, conv, stream, stats, gain, taps, totals, kernel, grad_out) = refs
    grads = conv_back(
        0, gathered, gb, gu, conv, stream, stats, gain, taps, totals, kernel, images=images, side=side
    )
    rows = side * WIDE
    for n in range(images):
        grad_out[n * rows : (n + 1) * rows, :] = grads[n].astype(grad_out.dtype)


def spread_kernel(*refs, images, side):
    half = len(refs) // 2
    for packed, out in zip(refs[:half], refs[half:]):
        for h in range(side):
            lines = packed[:, h * WIDE : (h + 1) * WIDE, :].astype(F32)
            out[h] = jnp.swapaxes(lines, 0, 1)[:side]


def call(body, outs, args, scratch=(), scalars=0):
    whole = pl.BlockSpec(memory_space=pltpu.VMEM)
    return pl.pallas_call(
        body,
        out_shape=[jax.ShapeDtypeStruct(shape, dtype) for shape, dtype in outs],
        in_specs=[pl.BlockSpec(memory_space=pltpu.SMEM)] * scalars + [whole] * (len(args) - scalars),
        out_specs=[whole] * len(outs),
        scratch_shapes=[pltpu.VMEM(shape, dtype) for shape, dtype in scratch],
        compiler_params=pltpu.CompilerParams(vmem_limit_bytes=VMEM_LIMIT),
    )(*args)


def per_device(
    inputs,
    conv_weight,
    batch_gain,
    batch_bias,
    mix_width,
    mix_height,
    unite_weight,
    layer_gain,
    up_weight,
    up_bias,
    down_weight,
    cotangent,
):
    held, side, _, features = inputs.shape
    dp, mp = lax.axis_size("dp"), lax.axis_size("mp")
    devices = dp * mp
    images = held // mp
    rows = images * side * WIDE
    units = up_bias.shape[1]
    both = ("dp", "mp")
    sizes = dict(images=images, side=side)
    place = lax.axis_index("mp").astype(jnp.int32).reshape(1)

    def share(values):
        return lax.all_to_all(
            jnp.broadcast_to(values[None], (devices,) + values.shape), both, 0, 0, tiled=False
        )

    pairs = jnp.stack([up_weight, down_weight], axis=1)
    pairs = lax.all_gather(pairs, "mp", axis=3, tiled=True)
    packed = [
        lax.all_gather(pairs[l].reshape(-1, units), "dp", axis=0, tiled=False) for l in range(2)
    ]
    unite = [lax.all_gather(unite_weight[l], "dp", axis=0, tiled=True) for l in range(2)]

    stream = jnp.transpose(inputs, (1, 2, 0, 3))
    cotangent = jnp.transpose(cotangent, (1, 2, 0, 3))
    cells = side * WIDE

    own, conv0, moments0, mixing, mixing_back = call(
        functools.partial(first_kernel, **sizes),
        [
            ((rows, features), F32),
            ((rows, features), F32),
            ((2, features), F32),
            ((2, 2 * cells, cells), BF16),
            ((2, cells, 2 * cells), BF16),
        ],
        [place, stream, conv_weight, mix_width, mix_height],
        [((held, cells, features), F32)],
        scalars=1,
    )
    kept_shapes = [
        ((rows, features), BF16),
        ((rows, features), BF16),
        ((rows, features), BF16),
        ((rows, features), F32),
        ((rows, 1), F32),
        ((rows, features), BF16),
        ((rows, units), BF16),
        ((rows, units), BF16),
    ]
    weight_scratch = [((features, units), BF16), ((features, units), BF16)]
    (stream1, conv1, moments1, stats0, branch, along_w, along_h, uhat, inv_norm, normal, slope, hidden, squares0) = call(
        functools.partial(middle_kernel_flat, layer=0, **sizes),
        [
            ((rows, features), F32),
            ((rows, features), F32),
            ((2, features), F32),
            ((2, features), F32),
        ]
        + kept_shapes
        + [((3, features), F32)],
        [
            share(moments0), conv0, own, batch_gain, batch_bias, mixing, unite[0], layer_gain, packed[0],
            up_bias, conv_weight,
        ],
        weight_scratch,
    )
    back_scratch = [
        ((rows, features), BF16),
        ((rows, units), BF16),
        ((rows, features), BF16),
    ]
    back_outs = [
        ((rows, features), F32),
        ((rows, features), F32),
        ((2, features), F32),
        ((3 * features, features), BF16),
        ((2, features, units), BF16),
        ((1, features), F32),
        ((1, units), F32),
        ((WIDE, WIDE), F32),
        ((WIDE, WIDE), F32),
    ]
    slope_f32 = [(shape, dtype) for shape, dtype in kept_shapes]
    slope_f32[6] = ((rows, units), F32)
    (result, stats1, squares1, gb1, gu1, sums1, unite_g1, mlp_g1, norm_g1, bias_g1, width_g1, height_g1) = call(
        functools.partial(last_kernel, layer=1, **sizes),
        [((rows, features), BF16), ((2, features), F32), ((3, features), F32)] + back_outs,
        [
            place, share(moments1), conv1, stream1, batch_gain, batch_bias, mixing, unite[1], layer_gain,
            packed[1], up_bias, conv_weight, mixing_back, cotangent,
        ],
        slope_f32 + weight_scratch + back_scratch + [((held, cells, features), F32)],
        scalars=1,
    )
    (totals1, kernel_g1, gb0, gu0, sums0, unite_g0, mlp_g0, norm_g0, bias_g0, width_g0, height_g0) = call(
        functools.partial(between_kernel, layer=0, **sizes),
        [((2, features), F32), ((9, features), F32)] + back_outs,
        [
            share(sums1), gb1, gu1, conv1, stream1, stats1, batch_gain, conv_weight,
            conv0, stats0, mixing_back, unite[0], layer_gain, packed[0],
            branch, along_w, along_h, uhat, inv_norm, normal, slope, hidden,
        ],
        weight_scratch + back_scratch,
    )
    totals0, kernel_g0, grad = call(
        functools.partial(end_kernel, **sizes),
        [((2, features), F32), ((9, features), F32), ((rows, features), BF16)],
        [share(sums0), gb0, gu0, conv0, own, stats0, batch_gain, conv_weight],
    )

    output, input_grad = call(
        functools.partial(spread_kernel, **sizes),
        [((side, side, held, features), F32)] * 2,
        [
            lax.all_gather(v, "mp").reshape(held, cells, features)
            for v in (result, grad)
        ],
    )

    def whole(maps):
        return jnp.transpose(maps, (2, 0, 1, 3))

    def scatter_unite(part):
        part = lax.psum_scatter(part, "dp", scatter_dimension=0, tiled=True)
        return lax.psum(part, "mp").astype(F32)

    def scatter_mlp(part):
        part = lax.psum_scatter(part, "dp", scatter_dimension=1, tiled=True)
        return lax.psum_scatter(part, "mp", scatter_dimension=2, tiled=True).astype(F32)

    unite_grad = jnp.stack([scatter_unite(g) for g in (unite_g0, unite_g1)])
    mlp_grads = [scatter_mlp(g) for g in (mlp_g0, mlp_g1)]
    up_grad = jnp.stack([g[0] for g in mlp_grads])
    down_grad = jnp.stack([g[1] for g in mlp_grads])

    small = [
        jnp.stack([kernel_g0, kernel_g1]),
        jnp.stack([norm_g0, norm_g1]),
        jnp.stack([bias_g0, bias_g1]),
        jnp.stack([width_g0[:side, :side], width_g1[:side, :side]]),
        jnp.stack([height_g0[:side, :side], height_g1[:side, :side]]),
        jnp.sum(jnp.stack([squares0, squares1]), axis=2),
    ]
    kernel_grad, gain_grad, bias_grad, width_grad, height_grad, squares = lax.psum(small, both)
    bias_grad = bias_grad.reshape(2, mp, units // mp)
    bias_grad = lax.dynamic_index_in_dim(bias_grad, lax.axis_index("mp"), 1, keepdims=False)
    entries = held * side * side * features * dp
    return (
        whole(output),
        whole(input_grad),
        kernel_grad,
        jnp.stack([totals0[1], totals1[1]]),
        jnp.stack([totals0[0], totals1[0]]),
        width_grad,
        height_grad,
        unite_grad,
        gain_grad.reshape(2, features),
        up_grad,
        bias_grad,
        down_grad,
        jnp.sqrt(squares / entries),
    )


def middle_kernel_flat(*refs, images, side, layer):
    (
        gathered, conv, stream, gain, bias, mixing, unite, norm_gain, packed, up_bias, taps,
        result, next_conv, next_moments, stats, branch, along_w, along_h, uhat, inv_norm, normal, slope,
        hidden, squares, up, down,
    ) = refs
    stage_forward(
        layer,
        gathered, conv, stream, gain, bias, mixing, unite, norm_gain, packed, up_bias, taps,
        result, next_conv, next_moments, stats, branch, along_w, along_h, uhat, inv_norm, normal, slope,
        hidden, squares, up, down, images=images, side=side,
    )


def solution(mesh):
    in_specs = (
        P("dp", None, None, None),
        P(),
        P(),
        P(),
        P(),
        P(),
        P(None, "dp", None),
        P(),
        P(None, "dp", "mp"),
        P(),
        P(None, "dp", "mp"),
        P("dp", None, None, None),
    )
    out_specs = (
        P("dp", None, None, None),
        P("dp", None, None, None),
        P(),
        P(),
        P(),
        P(),
        P(),
        P(None, "dp", None),
        P(),
        P(None, "dp", "mp"),
        P(None, "mp"),
        P(None, "dp", "mp"),
        P(),
    )
    return jax.shard_map(
        per_device, mesh=mesh, in_specs=in_specs, out_specs=out_specs, check_vma=False
    )
```

```python
import functools
from types import SimpleNamespace

import jax
import jax.numpy as jnp
from jax import lax
from jax.experimental import pallas as pl
from jax.experimental.pallas import tpu as pltpu
from jax.sharding import PartitionSpec as P

EPSILON = 1e-05
WIDE = 16
VMEM_LIMIT = 58 * 1024 * 1024
COST_BYTES = 3.0e6
COST_FLOPS = 1.0e10
F32 = jnp.float32
BF16 = jnp.bfloat16


def dot(left, right):
    return lax.dot_general(left, right, (((1,), (0,)), ((), ())), preferred_element_type=F32)


def dot_cols(left, right):
    return lax.dot_general(left, right, (((1,), (1,)), ((), ())), preferred_element_type=F32)


def dot_rows(left, right):
    return lax.dot_general(left, right, (((0,), (0,)), ((), ())), preferred_element_type=F32)


def valid_rows(rows, side):
    return lax.broadcasted_iota(jnp.int32, (rows, 1), 0) % WIDE < side


def three_shifts(image):
    rows, features = image.shape
    empty = jnp.zeros((WIDE, features), image.dtype)
    padded = jnp.concatenate([empty, image, empty], axis=0)
    total = rows + 2 * WIDE
    return pltpu.roll(padded, 1, 0), padded, pltpu.roll(padded, total - 1, 0)


def convolve(image, taps, side):
    rows = image.shape[0]
    shifted = three_shifts(image)
    summed = None
    for i in range(3):
        for j in range(3):
            term = shifted[j][WIDE * i : WIDE * i + rows] * taps[3 * i + j : 3 * i + j + 1]
            summed = term if summed is None else summed + term
    return jnp.where(valid_rows(rows, side), summed, 0.0)


def to_all(message_ref, row, values):
    devices = message_ref.shape[0]
    message_ref[:, row, 0 : values.shape[1]] = jnp.broadcast_to(values, (devices, values.shape[1]))


def local_moments(conv_ref, moments_ref, images, side):
    rows = side * WIDE
    count = images * side * side
    total = None
    for n in range(images):
        part = jnp.sum(conv_ref[n * rows : (n + 1) * rows, :], axis=0, keepdims=True)
        total = part if total is None else total + part
    mean = total / count
    squares = None
    for n in range(images):
        deviate = jnp.where(
            valid_rows(rows, side), conv_ref[n * rows : (n + 1) * rows, :] - mean, 0.0
        )
        part = jnp.sum(deviate * deviate, axis=0, keepdims=True)
        squares = part if squares is None else squares + part
    to_all(moments_ref, 0, mean)
    to_all(moments_ref, 1, squares)


def whole_moments(gathered_ref, count):
    devices = gathered_ref.shape[0]
    means = gathered_ref[:, 0, :]
    squares = gathered_ref[:, 1, :]
    center = jnp.sum(means, axis=0, keepdims=True) / devices
    apart = means - center
    spread = (
        jnp.sum(squares, axis=0, keepdims=True)
        + jnp.sum(apart * apart, axis=0, keepdims=True) * count
    ) / (count * devices)
    return center, lax.rsqrt(spread + EPSILON)


def mixing_matrices(mix_w, mix_h, side):
    cells = side * WIDE
    row = lax.broadcasted_iota(jnp.int32, (cells, side), 0)
    col = lax.broadcasted_iota(jnp.int32, (cells, side), 1)
    at_w = (row % WIDE == col).astype(BF16)
    at_h = (row // WIDE == col).astype(BF16)
    out = lax.broadcasted_iota(jnp.int32, (cells, cells), 0)
    inp = lax.broadcasted_iota(jnp.int32, (cells, cells), 1)
    same_h = out // WIDE == inp // WIDE
    same_w = (out % WIDE == inp % WIDE) & (out % WIDE < side)

    def spread(picks, mix, keep, flip):
        left = (dot_cols if flip else dot)(picks, mix).astype(BF16)
        return jnp.where(keep, dot_cols(left, picks), 0.0).astype(BF16)

    forward = jnp.concatenate(
        [spread(at_w, mix_w, same_h, False), spread(at_h, mix_h, same_w, False)], axis=0
    )
    backward = jnp.concatenate(
        [spread(at_w, mix_w, same_h, True), spread(at_h, mix_h, same_w, True)], axis=1
    )
    return forward, backward


def by_image(maps_ref, all_ref):
    side, _, held, features = maps_ref.shape
    empty = jnp.zeros((WIDE - side, held, features), F32)
    for h in range(side):
        lines = jnp.concatenate([maps_ref[h], empty], axis=0)
        all_ref[:, h * WIDE : (h + 1) * WIDE, :] = jnp.swapaxes(lines, 0, 1)


def unpack_weights(tmp, unite_ref, up_ref, down_ref):
    packed_ref = tmp.packed
    shards, height, _ = packed_ref.shape
    part = height // 3
    features = unite_ref.shape[1]
    ups, downs, unites = [], [], []
    for s in range(shards):
        piece = packed_ref[s].astype(F32)
        ups.append(piece[:part])
        downs.append(piece[part : 2 * part])
        for q in range(3):
            unites.append(piece[2 * part :, q * features : (q + 1) * features])
    up_ref[...] = jnp.concatenate(ups, axis=0).astype(BF16)
    down_ref[...] = jnp.concatenate(downs, axis=0).astype(BF16)
    unite_ref[...] = jnp.concatenate(unites, axis=0).astype(BF16)


def pack_grads(unite, up, down, pieces_of, dp):
    features = up.shape[0]
    part = features // dp
    for s in range(dp):
        columns = [
            unite[(3 * s + q) * part : (3 * s + q + 1) * part] for q in range(3)
        ]
        filler = jnp.zeros((part, up.shape[1] - 3 * features), F32)
        piece = jnp.concatenate(
            [
                up[s * part : (s + 1) * part],
                down[s * part : (s + 1) * part],
                jnp.concatenate(columns + [filler], axis=1),
            ],
            axis=0,
        )
        pieces_of(s, piece.astype(BF16))


def pack_image_rows(values):
    half = values.shape[0] // 2
    return jnp.concatenate([values[:half], values[half:]], axis=1)


def hidden_bias(up_bias_ref, layer, place_ref):
    groups = up_bias_ref.shape[1]
    blocks = [up_bias_ref[layer, pl.ds(place_ref[0] ^ j, 1), :] for j in range(groups)]
    return jnp.concatenate(blocks, axis=1)


def forward_image(
    conv,
    stream,
    center,
    inv_std,
    bn_gain,
    bn_bias,
    mixing,
    unite_ref,
    norm_gain,
    up_ref,
    up_bias,
    down_ref,
    side,
):
    rows, features = conv.shape
    valid = valid_rows(rows, side)
    ahat = (conv - center) * inv_std
    branch = jnp.where(valid, ahat * bn_gain + bn_bias, 0.0).astype(BF16)
    along = dot(mixing, branch).astype(BF16)
    along_w, along_h = along[:rows], along[rows:]
    united = (
        dot(branch, unite_ref[0:features, :])
        + dot(along_w, unite_ref[features : 2 * features, :])
        + dot(along_h, unite_ref[2 * features :, :])
    )
    resid = stream + united
    mid = jnp.sum(resid, axis=-1, keepdims=True) / features
    deviate = resid - mid
    spread = jnp.sum(deviate * deviate, axis=-1, keepdims=True) / features
    inv_norm = lax.rsqrt(spread + EPSILON)
    uhat = deviate * inv_norm
    normal = (uhat * norm_gain).astype(BF16)
    pre = dot(normal, up_ref[...]) + up_bias
    below = 0.5 + 0.5 * lax.erf(pre * (0.5**0.5))
    slope = below + pre * (jnp.exp(-0.5 * pre * pre) * 0.3989422804014327)
    hidden = (pre * below).astype(BF16)
    mlp = jnp.where(valid, dot_cols(hidden, down_ref[...]), 0.0)
    result = resid + mlp
    squares = jnp.concatenate(
        [jnp.sum(v * v, axis=0, keepdims=True) for v in (united, mlp, result)], axis=0
    )
    return SimpleNamespace(
        ahat=ahat,
        branch=branch,
        along_w=along_w,
        along_h=along_h,
        uhat=uhat,
        inv_norm=inv_norm,
        normal=normal,
        slope=slope,
        hidden=hidden,
        result=result,
        squares=squares,
    )


def backward_image(
    grad, ahat, branch, uhat, inv_norm, slope, mixing_back, unite_ref, norm_gain, up_ref, down_ref
):
    rows, features = grad.shape
    grad_low = grad.astype(BF16)
    gh = dot(grad_low, down_ref[...])
    gpre = (gh * slope).astype(BF16)
    bias = jnp.sum(gpre.astype(F32), axis=0, keepdims=True)
    gn = dot_cols(gpre, up_ref[...])
    gain = jnp.sum(gn * uhat, axis=0, keepdims=True)
    q = gn * norm_gain
    mean_q = jnp.sum(q, axis=-1, keepdims=True) / features
    mean_qu = jnp.sum(q * uhat, axis=-1, keepdims=True) / features
    gu = grad + inv_norm * (q - mean_q - uhat * mean_qu)
    gc = gu.astype(BF16)
    direct = dot_cols(gc, unite_ref[0:features, :])
    wide = dot_cols(gc, unite_ref[features : 2 * features, :]).astype(BF16)
    tall = dot_cols(gc, unite_ref[2 * features :, :]).astype(BF16)
    both = jnp.concatenate([wide, tall], axis=0)
    gb = direct + dot(mixing_back, both)
    cross = dot_cols(both, branch)
    return SimpleNamespace(
        grad_low=grad_low,
        gpre=gpre,
        bias=bias,
        gain=gain,
        gu=gu,
        gc=gc,
        gb=gb,
        cross=cross,
        offset=jnp.sum(gb, axis=0, keepdims=True),
        scale=jnp.sum(gb * ahat, axis=0, keepdims=True),
    )


def mixing_grads(cross, side):
    cells = side * WIDE
    out = lax.broadcasted_iota(jnp.int32, (cells, cells), 0)
    inp = lax.broadcasted_iota(jnp.int32, (cells, cells), 1)
    same_h = out // WIDE == inp // WIDE
    same_w = out % WIDE == inp % WIDE
    row = lax.broadcasted_iota(jnp.int32, (cells, WIDE), 0)
    col = lax.broadcasted_iota(jnp.int32, (cells, WIDE), 1)
    exact = functools.partial(
        lax.dot_general, precision=lax.Precision.HIGHEST, preferred_element_type=F32
    )

    def fold(values, keep, picks):
        picks = picks.astype(F32)
        half = exact(jnp.where(keep, values, 0.0), picks, (((1,), (0,)), ((), ())))
        return exact(picks, half, (((0,), (0,)), ((), ())))

    width = fold(cross[:cells], same_h, row % WIDE == col)
    height = fold(cross[cells:], same_w, row // WIDE == col)
    return width, height


def tap_sums(values, stream):
    rows = values.shape[0]
    shifted = three_shifts(stream)
    return jnp.concatenate(
        [
            jnp.sum(values * shifted[j][WIDE * i : WIDE * i + rows], axis=0, keepdims=True)
            for i in range(3)
            for j in range(3)
        ],
        axis=0,
    )


def conv_back_image(gb, ahat, gu, factor, offset_mean, scale_mean, taps, side):
    rows = gb.shape[0]
    valid = valid_rows(rows, side)
    ga = jnp.where(valid, factor * (gb - offset_mean - ahat * scale_mean), 0.0)
    turned = three_shifts(ga)
    summed = gu
    for i in range(3):
        for j in range(3):
            summed = (
                summed
                + turned[2 - j][WIDE * (2 - i) : WIDE * (2 - i) + rows]
                * taps[3 * i + j : 3 * i + j + 1]
            )
    return jnp.where(valid, summed, 0.0), ga


def add_up(total, part):
    return part if total is None else total + part


SMALL_ROWS, SMALL_WIDE = 60, 384
NORM_ROW, SQUARES_ROW, BIAS_ROW, TAPS_ROW = (27, 48), (28, 49), (31, 52), 39
KEPT = ("branch", "along_w", "along_h", "uhat", "inv_norm", "normal", "slope", "hidden")


def stage_forward(layer, place, moments, conv, stream, par, weights, kept, on_result, *, images, side):
    rows = side * WIDE
    center, inv_std = whole_moments(moments, images * side * side)
    up_bias = hidden_bias(par.up_bias, layer, place)
    squares = None
    for n in range(images):
        at = slice(n * rows, (n + 1) * rows)
        found = forward_image(
            conv[at, :],
            stream[at, :],
            center,
            inv_std,
            par.batch_gain[layer : layer + 1, :],
            par.batch_bias[layer : layer + 1, :],
            par.mixing[layer],
            weights[0],
            par.layer_gain[layer : layer + 1, :],
            weights[1],
            up_bias,
            weights[2],
            side,
        )
        for name in KEPT:
            to = getattr(kept, name)
            to[at, :] = getattr(found, name).astype(to.dtype)
        squares = add_up(squares, found.squares)
        on_result(n, found.result)
    return center, inv_std, squares


def stage_backward(
    layer, place, grad_of, center, inv_std, conv, par, weights, kept, outs, small, rows_ref, pieces_of,
    dp, *, images, side,
):
    rows = side * WIDE
    gb, gu = outs.gb, outs.gu
    features = gb.shape[1]
    grad_low, gpre, gc = rows_ref
    offset = scale = gain = bias = cross = None
    for n in range(images):
        at = slice(n * rows, (n + 1) * rows)
        found = backward_image(
            grad_of(n),
            (conv[at, :] - center) * inv_std,
            kept.branch[at, :],
            kept.uhat[at, :],
            kept.inv_norm[at, :],
            kept.slope[at, :].astype(F32),
            par.mixing_back[layer],
            weights[0],
            par.layer_gain[layer : layer + 1, :],
            weights[1],
            weights[2],
        )
        grad_low[at, :] = found.grad_low
        gpre[at, :] = found.gpre
        gc[at, :] = found.gc
        gb[at, :] = found.gb
        gu[at, :] = found.gu
        offset = add_up(offset, found.offset)
        scale = add_up(scale, found.scale)
        gain = add_up(gain, found.gain)
        bias = add_up(bias, found.bias)
        cross = add_up(cross, found.cross)
    small[NORM_ROW[layer] : NORM_ROW[layer] + 1, 0:features] = gain
    groups = par.up_bias.shape[1]
    width = bias.shape[1] // groups
    for j in range(groups):
        small[pl.ds(BIAS_ROW[layer] + (place[0] ^ j), 1), 0:width] = bias[:, j * width : (j + 1) * width]
    wide, tall = mixing_grads(cross, side)
    mixes = slice(layer * WIDE, (layer + 1) * WIDE)
    small[mixes, features : features + WIDE] = wide
    small[mixes, features + WIDE : features + 2 * WIDE] = tall
    unite_grad = jnp.concatenate(
        [dot_rows(ref[...], gc[...]) for ref in (kept.branch, kept.along_w, kept.along_h)], axis=0
    )
    up_grad = dot_rows(kept.normal[...], gpre[...])
    down_grad = dot_rows(grad_low[...], kept.hidden[...])
    pack_grads(unite_grad, up_grad, down_grad, pieces_of, dp)
    return offset, scale


def first_body(ins, outs, tmp, *, images, side):
    place, taps = ins.place, ins.taps
    own, conv, moments = outs.own, outs.conv, outs.moments
    every = tmp.every
    rows = side * WIDE
    by_image(ins.stream, every)
    for n in range(images):
        own[n * rows : (n + 1) * rows, :] = every[place[0] * images + n]
    for n in range(images):
        at = slice(n * rows, (n + 1) * rows)
        conv[at, :] = convolve(own[at, :], taps[:, 0, :], side)
    local_moments(conv, moments, images, side)


def other_body(ins, outs, tmp, *, images, side):
    rows = side * WIDE
    by_image(ins.cotangent, tmp.every)
    for n in range(images):
        outs.cotangent[n * rows : (n + 1) * rows, :] = tmp.every[ins.place[0] * images + n]
    mixes = ins.mix_w[...].astype(F32), ins.mix_h[...].astype(F32)
    for layer in range(ins.mix_w.shape[1]):
        outs.mixing[layer], outs.mixing_back[layer] = mixing_matrices(
            *(mix[:, layer, :].astype(BF16) for mix in mixes), side
        )


def middle_body(ins, outs, tmp, *, images, side):
    rows = side * WIDE
    weights = outs.unite, outs.up, outs.down
    unpack_weights(tmp, *weights)

    def on_result(n, result):
        at = slice(n * rows, (n + 1) * rows)
        outs.stream1[at, :] = result
        outs.conv1[at, :] = convolve(result, ins.taps[:, 1, :], side)

    center, inv_std, squares = stage_forward(
        0, ins.place, ins.moments, ins.conv, ins.stream, ins, weights, outs, on_result,
        images=images, side=side,
    )
    outs.stats[0:1, :] = center
    outs.stats[1:2, :] = inv_std
    outs.squares[...] = squares
    local_moments(outs.conv1, outs.moments1, images, side)


def last_body(ins, outs, tmp, *, images, side, dp):
    weights = tmp.unite, tmp.up, tmp.down
    unpack_weights(tmp, *weights)
    results = []
    center, inv_std, squares = stage_forward(
        1, ins.place, ins.moments, ins.conv, ins.stream, ins, weights, tmp,
        lambda n, result: results.append(result.astype(BF16)), images=images, side=side,
    )
    outs.result[...] = pack_image_rows(jnp.concatenate(results, axis=0))
    outs.stats[0:1, :] = center
    outs.stats[1:2, :] = inv_std
    outs.small[...] = jnp.zeros_like(outs.small)
    pieces_of = sort_pieces(ins.place[1], outs)
    offset, scale = stage_backward(
        1, ins.place, lambda n: ins.cotangent[n * side * WIDE : (n + 1) * side * WIDE, :], center, inv_std,
        ins.conv, ins, weights, tmp, outs, outs.small,
        (tmp.grad_low, tmp.gpre, tmp.gc), pieces_of, dp, images=images, side=side,
    )
    features = squares.shape[1]
    outs.small[SQUARES_ROW[1] : SQUARES_ROW[1] + 3, 0:features] = squares
    to_all(outs.sums, 0, offset)
    to_all(outs.sums, 1, scale)


def conv_back(layer, sums, gb, gu, conv, stats, par, totals, *, images, side):
    rows = side * WIDE
    features = gb.shape[1]
    cells = images * side * side * sums.shape[0]
    offset = jnp.sum(sums[:, 0, 0:features], axis=0, keepdims=True)
    scale = jnp.sum(sums[:, 1, 0:features], axis=0, keepdims=True)
    totals[0:1, :] = offset
    totals[1:2, :] = scale
    center, inv_std = stats[0:1, :], stats[1:2, :]
    factor = par.batch_gain[layer : layer + 1, :] * inv_std
    found = []
    for n in range(images):
        at = slice(n * rows, (n + 1) * rows)
        found.append(
            conv_back_image(
                gb[at, :],
                (conv[at, :] - center) * inv_std,
                gu[at, :],
                factor,
                offset / cells,
                scale / cells,
                par.taps[:, layer, :],
                side,
            )
        )
    return found


def taps_body(ins, outs, tmp, *, images, side):
    rows = side * WIDE
    center, inv_std = ins.stats[0:1, :], ins.stats[1:2, :]
    plain = scaled = None
    for n in range(images):
        at = slice(n * rows, (n + 1) * rows)
        stream = ins.stream[at, :]
        valid = valid_rows(rows, side)
        ones = jnp.where(valid, jnp.ones_like(stream), 0.0)
        ahat = jnp.where(valid, (ins.conv[at, :] - center) * inv_std, 0.0)
        plain = add_up(plain, tap_sums(ones, stream))
        scaled = add_up(scaled, tap_sums(ahat, stream))
    outs.plain[...] = plain
    outs.scaled[...] = scaled


def sort_pieces(mine, outs):
    def put(s, piece):
        to = mine ^ s
        even = (to & 1) == 0

        @pl.when(even)
        def _():
            outs.keep[to >> 1] = piece

        @pl.when(jnp.logical_not(even))
        def _():
            outs.give[to >> 1] = piece

    return put


def between_body(ins, outs, tmp, *, images, side, dp):
    weights = ins.unite, ins.up, ins.down
    rows = side * WIDE
    features = ins.gb1.shape[1]
    small, sums = tmp.small, outs.sums
    small[...] = ins.small[...]
    grads, kernel = [], None
    found = conv_back(
        1, ins.sums1, ins.gb1, ins.gu1, ins.conv1, ins.stats1, ins, outs.totals1, images=images, side=side
    )
    for n, (grad, ga) in enumerate(found):
        grads.append(grad)
        kernel = add_up(kernel, tap_sums(ga, ins.stream1[n * rows : (n + 1) * rows, :]))
    small[TAPS_ROW : TAPS_ROW + 9, 0:features] = kernel
    stats = ins.stats0
    offset, scale = stage_backward(
        0, ins.place, lambda n: grads[n], stats[0:1, :], stats[1:2, :], ins.conv0, ins, weights, ins,
        outs, small, (tmp.grad_low, tmp.gpre, tmp.gc), sort_pieces(ins.place[1], outs), dp,
        images=images, side=side,
    )
    kernel = None
    for n in range(images):
        at = slice(n * rows, (n + 1) * rows)
        kernel = add_up(kernel, tap_sums(outs.gb[at, :], ins.stream0[at, :]))
    for k, values in enumerate((kernel, ins.plain[...], ins.scaled[...])):
        small[9 * k : 9 * k + 9, 0:features] = values
    small[SQUARES_ROW[0] : SQUARES_ROW[0] + 3, 0:features] = ins.squares0[...]
    to_all(sums, 0, offset)
    to_all(sums, 1, scale)
    devices, height, _ = sums.shape
    for g in range(height - 2):
        held = min(devices, SMALL_ROWS - g * devices)
        sums[0:held, 2 + g, :] = small[g * devices : g * devices + held, :]
        if held < devices:
            sums[held:, 2 + g, :] = jnp.zeros((devices - held, SMALL_WIDE), F32)


def end_body(ins, outs, tmp, *, images, side):
    sums, totals = ins.sums0, tmp.totals
    found = conv_back(
        0, sums, ins.gb, ins.gu, ins.conv0, ins.stats0, ins, totals, images=images, side=side
    )
    outs.grad[...] = pack_image_rows(jnp.concatenate([grad for grad, _ in found], axis=0)).astype(BF16)
    for row, total in enumerate((outs.offset_grad, outs.scale_grad)):
        total[0:1, :] = totals[row : row + 1, :]
        total[1:2, :] = ins.totals1[row : row + 1, :]


def gather_body(ins, outs, tmp):
    for g in range(outs.message.shape[1]):
        to_all(outs.message, g, jnp.sum(ins.sums0[:, 2 + g, :], axis=0, keepdims=True))


def spread_body(ins, outs, tmp, *, images, side):
    rows = side * WIDE
    place = ins.place[0]
    every, out = tmp.every, outs.out
    features = every.shape[2]
    for j, part in enumerate(ins.parts):
        packed = part[...].astype(F32)
        values = jnp.concatenate([packed[:, :features], packed[:, features:]], axis=0)
        for n in range(images):
            every[(place ^ j) * images + n] = values[n * rows : (n + 1) * rows]
    for h in range(side):
        out[h] = jnp.swapaxes(every[:, h * WIDE : (h + 1) * WIDE, :], 0, 1)[:side]


def core_body(ins, outs, tmp):
    for k in range(ins.keep.shape[0]):
        outs.parts[k][...] = (ins.keep[k].astype(F32) + ins.got[k].astype(F32)).astype(BF16)


def chips_body(ins, outs, tmp):
    total = ins.parts[0][...].astype(F32)
    for part in ins.parts[1:]:
        total = total + part[...].astype(F32)
    part = total.shape[0] // 3
    groups = len(outs.give)
    width = total.shape[1] // groups
    features = outs.give[0].shape[1] - 2 * width
    for j in range(groups):
        block = jnp.concatenate(
            [
                total[:part, j * width : (j + 1) * width],
                total[part : 2 * part, j * width : (j + 1) * width],
                total[2 * part :, :features],
            ],
            axis=1,
        )
        outs.give[j][...] = block.astype(BF16)


def weights_body(ins, outs, tmp):
    layers = outs.up_grad.shape[0]
    for layer in range(layers):
        terms = [ref[...].astype(F32) for ref in ins.got[layer]]
        while len(terms) > 1:
            terms = [terms[j] + terms[j + 1] for j in range(0, len(terms), 2)]
        total = terms[0]
        width = outs.up_grad.shape[2]
        features = outs.unite_grad.shape[1]
        outs.up_grad[layer] = total[:, :width]
        outs.down_grad[layer] = total[:, width : 2 * width]
        rest = total[:, 2 * width :]
        rows = jnp.concatenate([rest[:, q * features : (q + 1) * features] for q in range(3)], axis=0)
        outs.unite_grad[layer] = rows.T


def small_body(ins, outs, tmp, *, side, cells, entries):
    got = ins.got
    features = outs.gain_grad.shape[1]
    devices, height, _ = got.shape
    values = tmp.values
    for g in range(height):
        values[g * devices : (g + 1) * devices, :] = got[:, g, :]
    factor = ins.batch_gain[0:1, :] * ins.stats0[1:2, :]
    first = factor * (
        values[0:9, 0:features]
        - ins.offset[0:1, :] / cells * values[9:18, 0:features]
        - ins.scale[0:1, :] / cells * values[18:27, 0:features]
    )
    for k in range(9):
        outs.kernel_grad[k, 0:1, :] = first[k : k + 1]
        outs.kernel_grad[k, 1:2, :] = values[TAPS_ROW + k : TAPS_ROW + k + 1, 0:features]
    width = outs.bias_grad.shape[1]
    for layer in range(2):
        outs.gain_grad[layer : layer + 1, :] = values[NORM_ROW[layer] : NORM_ROW[layer] + 1, 0:features]
        outs.bias_grad[layer : layer + 1, :] = values[pl.ds(BIAS_ROW[layer] + ins.place[0], 1), 0:width]
        rows = slice(layer * WIDE, layer * WIDE + side)
        outs.width_grad[:, layer, :] = values[rows, features : features + side]
        outs.height_grad[:, layer, :] = values[rows, features + WIDE : features + WIDE + side]
        squares = values[SQUARES_ROW[layer] : SQUARES_ROW[layer] + 3, 0:features]
        outs.stream_rms[:, layer : layer + 1] = jnp.sqrt(
            jnp.sum(squares, axis=1, keepdims=True) / entries
        )


def call(body, ins, outs, scratch=None, shards=(), micros=0, **static):
    operands, in_tree = jax.tree.flatten(ins)
    shapes, out_tree = jax.tree.flatten(
        {name: jax.tree.map(lambda shape: jax.ShapeDtypeStruct(*shape), outs[name], is_leaf=is_shape) for name in outs}
    )
    scratch = dict(scratch or {})
    if shards:
        scratch["packed"] = (len(shards),) + shards[0].shape, shards[0].dtype
    tmp_names = list(scratch)

    def kernel(*refs):
        refs, sems = (refs[:-1], refs[-1]) if shards else (refs, None)
        cut = len(operands), len(operands) + len(shards), len(operands) + len(shards) + len(shapes)
        given = SimpleNamespace(**jax.tree.unflatten(in_tree, refs[: cut[0]]))
        results = SimpleNamespace(**jax.tree.unflatten(out_tree, refs[cut[1] : cut[2]]))
        tmp = SimpleNamespace(**dict(zip(tmp_names, refs[cut[2] :])))
        copies = [
            pltpu.make_async_copy(ref, tmp.packed.at[given.place[1] ^ k], sems.at[k])
            for k, ref in enumerate(refs[cut[0] : cut[1]])
        ]
        for copy in copies:
            copy.start()
        for copy in copies:
            copy.wait()
        body(given, results, tmp, **static)

    whole = pl.BlockSpec(memory_space=pltpu.VMEM)
    spaces = jax.tree.leaves(
        {
            name: jax.tree.map(
                lambda _: pl.BlockSpec(memory_space=pltpu.SMEM) if name == "place" else whole, ins[name]
            )
            for name in ins
        }
    )
    found = pl.pallas_call(
        kernel,
        out_shape=shapes,
        in_specs=spaces + [pl.BlockSpec(memory_space=pltpu.HBM)] * len(shards),
        out_specs=[whole] * len(shapes),
        scratch_shapes=[pltpu.VMEM(*scratch[name]) for name in tmp_names]
        + ([pltpu.SemaphoreType.DMA((len(shards),))] if shards else []),
        compiler_params=pltpu.CompilerParams(vmem_limit_bytes=VMEM_LIMIT),
        cost_estimate=pl.CostEstimate(
            flops=int(micros * COST_FLOPS), transcendentals=0, bytes_accessed=int(micros * COST_BYTES)
        ),
    )(*operands, *shards)
    return SimpleNamespace(**jax.tree.unflatten(out_tree, found))


def is_shape(value):
    return isinstance(value, tuple)


def swap(values, axis, mask):
    return lax.ppermute(values, axis, [(i, i ^ mask) for i in range(lax.axis_size(axis))])


def after(values, *others):
    return lax.optimization_barrier((values, others))[0]


def per_device(
    inputs,
    conv_weight,
    batch_gain,
    batch_bias,
    mix_width,
    mix_height,
    unite_weight,
    layer_gain,
    up_weight,
    up_bias,
    down_weight,
    cotangent,
):
    held, side, _, features = inputs.shape
    layers = conv_weight.shape[0]
    dp, mp = lax.axis_size("dp"), lax.axis_size("mp")
    devices = dp * mp
    images = held // mp
    cells = side * WIDE
    rows = images * cells
    units = up_bias.shape[1]
    part = features // dp
    both = ("dp", "mp")
    sizes = dict(images=images, side=side)
    place = jnp.stack([lax.axis_index("mp"), lax.axis_index("dp")]).astype(jnp.int32)

    def group_parts(values):
        if not isinstance(values, (list, tuple)):
            values = [values] * mp
        return [swap(value, "mp", j) if j else value for j, value in enumerate(values)]

    def share(blocks):
        return lax.all_to_all(blocks, both, 0, 0, tiled=False)

    maps = jnp.transpose(inputs, (1, 2, 0, 3))
    cotangent_maps = jnp.transpose(cotangent, (1, 2, 0, 3))
    taps = jnp.transpose(conv_weight, (1, 0, 2))
    mix_w, mix_h = (jnp.transpose(mix, (1, 0, 2)) for mix in (mix_width, mix_height))
    shared = (devices, 2, features)
    found = call(
        first_body,
        dict(place=place, stream=maps, taps=taps),
        dict(own=((rows, features), F32), conv=((rows, features), F32), moments=(shared, F32)),
        dict(every=((held, cells, features), F32)),
        micros=4,
        **sizes,
    )
    other = call(
        other_body,
        dict(place=place, cotangent=cotangent_maps, mix_w=mix_w, mix_h=mix_h),
        dict(
            cotangent=((rows, features), F32),
            mixing=((layers, 2 * cells, cells), BF16),
            mixing_back=((layers, cells, 2 * cells), BF16),
        ),
        dict(every=((held, cells, features), F32)),
        micros=3,
        **sizes,
    )

    pairs = jnp.concatenate([up_weight, down_weight], axis=1)
    thirds = unite_weight.reshape(layers, 3, part, features)
    thirds = jnp.concatenate([thirds[:, q] for q in range(3)], axis=2)
    thirds = jnp.pad(thirds, ((0, 0), (0, 0), (0, units - 3 * features)))
    wides, packed = [], []
    for layer in range(layers):
        wide, step = pairs[layer], 1
        if layer:
            wide = after(wide, wides[0][0])
        wides.append([])
        while step < mp:
            wide = jnp.concatenate([wide, swap(wide, "mp", step)], axis=1)
            wides[layer].append(wide)
            wide = after(wide, wides[0][-1] if layer else found.moments)
            step *= 2
    moments0 = share(after(found.moments, wides[0][0]))

    def over_dp(layer, wait_chips, wait_core):
        piece = after(jnp.concatenate([wides[layer][-1], thirds[layer]], axis=0), *wait_chips)
        shards = [piece] + [swap(piece, "dp", 2 * k) for k in range(1, dp // 2)]
        mates = [swap(after(shard, *wait_core), "dp", 1) for shard in shards]
        return [shard for pair in zip(shards, mates) for shard in pair]

    packed = [over_dp(0, (), (moments0, other.mixing))]

    own, conv0 = found.own, found.conv
    par = dict(
        place=place,
        taps=taps,
        batch_gain=batch_gain,
        batch_bias=batch_bias,
        layer_gain=layer_gain,
        up_bias=up_bias.reshape(layers, mp, units // mp),
    )
    kept = dict(
        branch=((rows, features), BF16),
        along_w=((rows, features), BF16),
        along_h=((rows, features), BF16),
        uhat=((rows, features), F32),
        inv_norm=((rows, 1), F32),
        normal=((rows, features), BF16),
        slope=((rows, units), BF16),
        hidden=((rows, units), BF16),
    )
    weight_tmp = dict(
        unite=((3 * features, features), BF16),
        up=((features, units), BF16),
        down=((features, units), BF16),
    )
    back_tmp = dict(
        grad_low=((rows, features), BF16), gpre=((rows, units), BF16), gc=((rows, features), BF16)
    )
    back_outs = dict(gb=((rows, features), F32), gu=((rows, features), F32))
    stats = ((2, features), F32)
    piece = ((3 * part, units), BF16)
    pieces = {name: ((dp // 2, 3 * part, units), BF16) for name in ("keep", "give")}

    def over_core(values, *before):
        return call(
            core_body,
            dict(keep=values.keep, got=swap(after(values.give, *before), "dp", 1)),
            dict(parts=[piece] * (dp // 2)),
            micros=0,
        ).parts

    def from_chips(parts):
        return [swap(values, "dp", 2 * k) if k else values for k, values in enumerate(parts)]

    def over_chips(parts):
        block = ((part, 2 * (units // mp) + 3 * features), BF16)
        return call(chips_body, dict(parts=parts), dict(give=[block] * mp), micros=0).give

    mid = call(
        middle_body,
        dict(
            par,
            moments=moments0,
            conv=conv0,
            stream=own,
            mixing=other.mixing,
        ),
        dict(
            kept,
            stream1=((rows, features), F32),
            conv1=((rows, features), F32),
            moments1=(shared, F32),
            stats=stats,
            squares=((3, features), F32),
            **weight_tmp,
        ),
        None,
        packed[0],
        micros=6,
        **sizes,
    )
    packed.append(over_dp(1, packed[0][::2], (mid.moments1,)))
    under = call(
        taps_body,
        dict(stream=own, conv=conv0, stats=mid.stats),
        dict(plain=((9, features), F32), scaled=((9, features), F32)),
        micros=2,
        **sizes,
    )
    last = call(
        last_body,
        dict(
            par,
            moments=after(share(mid.moments1), under.plain),
            conv=mid.conv1,
            stream=mid.stream1,
            mixing=other.mixing,
            mixing_back=other.mixing_back,
            cotangent=other.cotangent,
        ),
        dict(
            back_outs,
            result=((rows // 2, 2 * features), BF16),
            stats=stats,
            small=((SMALL_ROWS, SMALL_WIDE), F32),
            sums=(shared, F32),
            **pieces,
        ),
        dict(
            dict(kept, slope=((rows, units), F32)),
            **weight_tmp,
            **back_tmp,
        ),
        packed[1],
        micros=10,
        dp=dp,
        **sizes,
    )
    summed1 = over_core(last)
    groups = -(-SMALL_ROWS // devices)
    between = call(
        between_body,
        {
            **par,
            **{name: getattr(mid, name) for name in (*kept, *weight_tmp)},
            **dict(
                sums1=after(share(last.sums), summed1),
                gb1=last.gb,
                gu1=last.gu,
                conv1=mid.conv1,
                stream1=mid.stream1,
                stats1=last.stats,
                small=last.small,
                stream0=own,
                plain=under.plain,
                scaled=under.scaled,
                conv0=conv0,
                stats0=mid.stats,
                squares0=mid.squares,
                mixing_back=other.mixing_back,
            ),
        },
        dict(
            back_outs,
            totals1=stats,
            sums=((devices, 2 + groups, SMALL_WIDE), F32),
            **pieces,
        ),
        dict(
            back_tmp,
            small=((SMALL_ROWS, SMALL_WIDE), F32),
        ),
        micros=10,
        dp=dp,
        **sizes,
    )
    result_parts = group_parts(after(last.result, summed1))
    result_parts = after(result_parts[: mp - 1], between.sums) + result_parts[mp - 1 :]
    parts1 = after(from_chips(summed1), between.sums)
    sums0 = share(after(between.sums, parts1, result_parts[: mp - 1]))
    cut1 = over_chips(parts1)
    summed0 = over_core(between, sums0)
    sums0 = after(sums0, cut1)
    shares1 = group_parts(cut1)
    end = call(
        end_body,
        dict(
            sums0=sums0,
            gb=between.gb,
            gu=between.gu,
            conv0=conv0,
            stats0=mid.stats,
            totals1=between.totals1,
            batch_gain=batch_gain,
            taps=taps,
        ),
        dict(
            grad=((rows // 2, 2 * features), BF16),
            offset_grad=stats,
            scale_grad=stats,
        ),
        dict(totals=stats),
        micros=3,
        **sizes,
    )

    cut0 = over_chips(from_chips(after(summed0, end.grad)))
    grads = call(
        weights_body,
        dict(got=[group_parts(cut0), shares1]),
        dict(
            up_grad=((layers, part, units // mp), F32),
            down_grad=((layers, part, units // mp), F32),
            unite_grad=((layers, features, 3 * part), F32),
        ),
    )

    def whole(parts):
        out = call(
            spread_body,
            dict(place=place, parts=parts),
            dict(out=((side, side, held, features), F32)),
            dict(every=((held, cells, features), F32)),
            **sizes,
        ).out
        return jnp.transpose(out, (2, 0, 1, 3))

    chunk = call(
        gather_body, dict(sums0=sums0), dict(message=((devices, groups, SMALL_WIDE), F32)), micros=0
    )
    outputs = whole(after(result_parts, end.grad)), whole(after(group_parts(after(end.grad, result_parts, shares1)), cut0, shares1))
    small = call(
        small_body,
        dict(
            place=place,
            got=share(chunk.message),
            batch_gain=batch_gain,
            stats0=mid.stats,
            offset=end.offset_grad,
            scale=end.scale_grad,
        ),
        dict(
            kernel_grad=((9, layers, features), F32),
            gain_grad=((layers, features), F32),
            bias_grad=((layers, units // mp), F32),
            width_grad=((side, layers, side), F32),
            height_grad=((side, layers, side), F32),
            stream_rms=((3, layers), F32),
        ),
        dict(values=((groups * devices, SMALL_WIDE), F32)),
        side=side,
        cells=images * side * side * devices,
        entries=held * side * side * features * dp,
    )
    return (
        *outputs,
        jnp.transpose(small.kernel_grad, (1, 0, 2)),
        end.scale_grad,
        end.offset_grad,
        jnp.transpose(small.width_grad, (1, 0, 2)),
        jnp.transpose(small.height_grad, (1, 0, 2)),
        jnp.transpose(grads.unite_grad, (0, 2, 1)),
        small.gain_grad,
        grads.up_grad,
        small.bias_grad,
        grads.down_grad,
        small.stream_rms.T,
    )


def solution(mesh):
    in_specs = (
        P("dp", None, None, None),
        P(),
        P(),
        P(),
        P(),
        P(),
        P(None, "dp", None),
        P(),
        P(None, "dp", "mp"),
        P(),
        P(None, "dp", "mp"),
        P("dp", None, None, None),
    )
    out_specs = (
        P("dp", None, None, None),
        P("dp", None, None, None),
        P(),
        P(),
        P(),
        P(),
        P(),
        P(None, "dp", None),
        P(),
        P(None, "dp", "mp"),
        P(None, "mp"),
        P(None, "dp", "mp"),
        P(),
    )
    return jax.shard_map(
        per_device, mesh=mesh, in_specs=in_specs, out_specs=out_specs, check_vma=False
    )
```

```python
import functools
from types import SimpleNamespace

import jax
import jax.numpy as jnp
from jax import lax
from jax.experimental import pallas as pl
from jax.experimental.pallas import tpu as pltpu
from jax.sharding import PartitionSpec as P

EPSILON = 1e-05
WIDE = 16
VMEM_LIMIT = 58 * 1024 * 1024
COST_BYTES = 3.0e6
COST_FLOPS = 1.0e10
F32 = jnp.float32
BF16 = jnp.bfloat16


def dot(left, right):
    return lax.dot_general(left, right, (((1,), (0,)), ((), ())), preferred_element_type=F32)


def dot_cols(left, right):
    return lax.dot_general(left, right, (((1,), (1,)), ((), ())), preferred_element_type=F32)


def dot_rows(left, right):
    return lax.dot_general(left, right, (((0,), (0,)), ((), ())), preferred_element_type=F32)


def valid_rows(rows, side):
    return lax.broadcasted_iota(jnp.int32, (rows, 1), 0) % WIDE < side


def three_shifts(image):
    rows, features = image.shape
    empty = jnp.zeros((WIDE, features), image.dtype)
    padded = jnp.concatenate([empty, image, empty], axis=0)
    total = rows + 2 * WIDE
    return pltpu.roll(padded, 1, 0), padded, pltpu.roll(padded, total - 1, 0)


def convolve(image, taps, side):
    rows = image.shape[0]
    shifted = three_shifts(image)
    summed = None
    for i in range(3):
        for j in range(3):
            term = shifted[j][WIDE * i : WIDE * i + rows] * taps[3 * i + j : 3 * i + j + 1]
            summed = term if summed is None else summed + term
    return jnp.where(valid_rows(rows, side), summed, 0.0)


def to_all(message_ref, row, values):
    devices = message_ref.shape[0]
    message_ref[:, row, 0 : values.shape[1]] = jnp.broadcast_to(values, (devices, values.shape[1]))


def local_moments(conv_ref, moments_ref, images, side):
    rows = side * WIDE
    count = images * side * side
    total = None
    for n in range(images):
        part = jnp.sum(conv_ref[n * rows : (n + 1) * rows, :], axis=0, keepdims=True)
        total = part if total is None else total + part
    mean = total / count
    squares = None
    for n in range(images):
        deviate = jnp.where(
            valid_rows(rows, side), conv_ref[n * rows : (n + 1) * rows, :] - mean, 0.0
        )
        part = jnp.sum(deviate * deviate, axis=0, keepdims=True)
        squares = part if squares is None else squares + part
    to_all(moments_ref, 0, mean)
    to_all(moments_ref, 1, squares)


def whole_moments(gathered_ref, count):
    devices = gathered_ref.shape[0]
    means = gathered_ref[:, 0, :]
    squares = gathered_ref[:, 1, :]
    center = jnp.sum(means, axis=0, keepdims=True) / devices
    apart = means - center
    spread = (
        jnp.sum(squares, axis=0, keepdims=True)
        + jnp.sum(apart * apart, axis=0, keepdims=True) * count
    ) / (count * devices)
    return center, lax.rsqrt(spread + EPSILON)


def mixing_matrices(mix_w, mix_h, side):
    cells = side * WIDE
    row = lax.broadcasted_iota(jnp.int32, (cells, side), 0)
    col = lax.broadcasted_iota(jnp.int32, (cells, side), 1)
    at_w = (row % WIDE == col).astype(BF16)
    at_h = (row // WIDE == col).astype(BF16)
    out = lax.broadcasted_iota(jnp.int32, (cells, cells), 0)
    inp = lax.broadcasted_iota(jnp.int32, (cells, cells), 1)
    same_h = out // WIDE == inp // WIDE
    same_w = (out % WIDE == inp % WIDE) & (out % WIDE < side)

    def spread(picks, mix, keep, flip):
        left = (dot_cols if flip else dot)(picks, mix).astype(BF16)
        return jnp.where(keep, dot_cols(left, picks), 0.0).astype(BF16)

    forward = jnp.concatenate(
        [spread(at_w, mix_w, same_h, False), spread(at_h, mix_h, same_w, False)], axis=0
    )
    backward = jnp.concatenate(
        [spread(at_w, mix_w, same_h, True), spread(at_h, mix_h, same_w, True)], axis=1
    )
    return forward, backward


def by_image(maps_ref, all_ref):
    side, _, held, features = maps_ref.shape
    empty = jnp.zeros((WIDE - side, held, features), F32)
    for h in range(side):
        lines = jnp.concatenate([maps_ref[h], empty], axis=0)
        all_ref[:, h * WIDE : (h + 1) * WIDE, :] = jnp.swapaxes(lines, 0, 1)


def unpack_weights(tmp, unite_ref, up_ref, down_ref):
    packed_ref = tmp.packed
    shards, height, _ = packed_ref.shape
    part = height // 3
    features = unite_ref.shape[1]
    ups, downs, unites = [], [], []
    for s in range(shards):
        piece = packed_ref[s].astype(F32)
        ups.append(piece[:part])
        downs.append(piece[part : 2 * part])
        for q in range(3):
            unites.append(piece[2 * part :, q * features : (q + 1) * features])
    up_ref[...] = jnp.concatenate(ups, axis=0).astype(BF16)
    down_ref[...] = jnp.concatenate(downs, axis=0).astype(BF16)
    unite_ref[...] = jnp.concatenate(unites, axis=0).astype(BF16)


def pack_grads(unite, up, down, pieces_of, dp):
    features = up.shape[0]
    part = features // dp
    for s in range(dp):
        columns = [
            unite[(3 * s + q) * part : (3 * s + q + 1) * part] for q in range(3)
        ]
        filler = jnp.zeros((part, up.shape[1] - 3 * features), F32)
        piece = jnp.concatenate(
            [
                up[s * part : (s + 1) * part],
                down[s * part : (s + 1) * part],
                jnp.concatenate(columns + [filler], axis=1),
            ],
            axis=0,
        )
        pieces_of(s, piece.astype(BF16))


def pack_image_rows(values, side):
    lines = [values[r : r + side] for r in range(0, values.shape[0], WIDE)]
    half = len(lines) // 2
    return jnp.concatenate(
        [jnp.concatenate(lines[:half], axis=0), jnp.concatenate(lines[half:], axis=0)], axis=1
    )


def hidden_bias(up_bias_ref, layer, place_ref):
    groups = up_bias_ref.shape[1]
    blocks = [up_bias_ref[layer, pl.ds(place_ref[0] ^ j, 1), :] for j in range(groups)]
    return jnp.concatenate(blocks, axis=1)


def forward_image(
    conv,
    stream,
    center,
    inv_std,
    bn_gain,
    bn_bias,
    mixing,
    unite_ref,
    norm_gain,
    up_ref,
    up_bias,
    down_ref,
    side,
):
    rows, features = conv.shape
    valid = valid_rows(rows, side)
    ahat = (conv - center) * inv_std
    branch = jnp.where(valid, ahat * bn_gain + bn_bias, 0.0).astype(BF16)
    along = dot(mixing, branch).astype(BF16)
    along_w, along_h = along[:rows], along[rows:]
    united = (
        dot(branch, unite_ref[0:features, :])
        + dot(along_w, unite_ref[features : 2 * features, :])
        + dot(along_h, unite_ref[2 * features :, :])
    )
    resid = stream + united
    mid = jnp.sum(resid, axis=-1, keepdims=True) / features
    deviate = resid - mid
    spread = jnp.sum(deviate * deviate, axis=-1, keepdims=True) / features
    inv_norm = lax.rsqrt(spread + EPSILON)
    uhat = deviate * inv_norm
    normal = (uhat * norm_gain).astype(BF16)
    pre = dot(normal, up_ref[...]) + up_bias
    below = 0.5 + 0.5 * lax.erf(pre * (0.5**0.5))
    slope = below + pre * (jnp.exp(-0.5 * pre * pre) * 0.3989422804014327)
    hidden = (pre * below).astype(BF16)
    mlp = jnp.where(valid, dot_cols(hidden, down_ref[...]), 0.0)
    result = resid + mlp
    squares = jnp.concatenate(
        [jnp.sum(v * v, axis=0, keepdims=True) for v in (united, mlp, result)], axis=0
    )
    return SimpleNamespace(
        ahat=ahat,
        branch=branch,
        along_w=along_w,
        along_h=along_h,
        uhat=uhat,
        inv_norm=inv_norm,
        normal=normal,
        slope=slope,
        hidden=hidden,
        result=result,
        squares=squares,
    )


def backward_image(
    grad, ahat, branch, uhat, inv_norm, slope, mixing_back, unite_ref, norm_gain, up_ref, down_ref
):
    rows, features = grad.shape
    grad_low = grad.astype(BF16)
    gh = dot(grad_low, down_ref[...])
    gpre = (gh * slope).astype(BF16)
    bias = jnp.sum(gpre.astype(F32), axis=0, keepdims=True)
    gn = dot_cols(gpre, up_ref[...])
    gain = jnp.sum(gn * uhat, axis=0, keepdims=True)
    q = gn * norm_gain
    mean_q = jnp.sum(q, axis=-1, keepdims=True) / features
    mean_qu = jnp.sum(q * uhat, axis=-1, keepdims=True) / features
    gu = grad + inv_norm * (q - mean_q - uhat * mean_qu)
    gc = gu.astype(BF16)
    direct = dot_cols(gc, unite_ref[0:features, :])
    wide = dot_cols(gc, unite_ref[features : 2 * features, :]).astype(BF16)
    tall = dot_cols(gc, unite_ref[2 * features :, :]).astype(BF16)
    both = jnp.concatenate([wide, tall], axis=0)
    gb = direct + dot(mixing_back, both)
    cross = dot_cols(both, branch)
    return SimpleNamespace(
        grad_low=grad_low,
        gpre=gpre,
        bias=bias,
        gain=gain,
        gu=gu,
        gc=gc,
        gb=gb,
        cross=cross,
        offset=jnp.sum(gb, axis=0, keepdims=True),
        scale=jnp.sum(gb * ahat, axis=0, keepdims=True),
    )


def mixing_grads(cross, side):
    cells = side * WIDE
    out = lax.broadcasted_iota(jnp.int32, (cells, cells), 0)
    inp = lax.broadcasted_iota(jnp.int32, (cells, cells), 1)
    same_h = out // WIDE == inp // WIDE
    same_w = out % WIDE == inp % WIDE
    row = lax.broadcasted_iota(jnp.int32, (cells, WIDE), 0)
    col = lax.broadcasted_iota(jnp.int32, (cells, WIDE), 1)
    exact = functools.partial(
        lax.dot_general, precision=lax.Precision.HIGHEST, preferred_element_type=F32
    )

    def fold(values, keep, picks):
        picks = picks.astype(F32)
        half = exact(jnp.where(keep, values, 0.0), picks, (((1,), (0,)), ((), ())))
        return exact(picks, half, (((0,), (0,)), ((), ())))

    width = fold(cross[:cells], same_h, row % WIDE == col)
    height = fold(cross[cells:], same_w, row // WIDE == col)
    return width, height


def tap_sums(values, stream):
    rows = values.shape[0]
    shifted = three_shifts(stream)
    return jnp.concatenate(
        [
            jnp.sum(values * shifted[j][WIDE * i : WIDE * i + rows], axis=0, keepdims=True)
            for i in range(3)
            for j in range(3)
        ],
        axis=0,
    )


def conv_back_image(gb, ahat, gu, factor, offset_mean, scale_mean, taps, side):
    rows = gb.shape[0]
    valid = valid_rows(rows, side)
    ga = jnp.where(valid, factor * (gb - offset_mean - ahat * scale_mean), 0.0)
    turned = three_shifts(ga)
    summed = gu
    for i in range(3):
        for j in range(3):
            summed = (
                summed
                + turned[2 - j][WIDE * (2 - i) : WIDE * (2 - i) + rows]
                * taps[3 * i + j : 3 * i + j + 1]
            )
    return jnp.where(valid, summed, 0.0), ga


def add_up(total, part):
    return part if total is None else total + part


SMALL_ROWS, SMALL_WIDE = 60, 384
NORM_ROW, SQUARES_ROW, BIAS_ROW, TAPS_ROW = (27, 48), (28, 49), (31, 52), 39
KEPT = ("branch", "along_w", "along_h", "uhat", "inv_norm", "normal", "slope", "hidden")


def stage_forward(layer, place, moments, conv, stream, par, weights, kept, on_result, *, images, side):
    rows = side * WIDE
    center, inv_std = whole_moments(moments, images * side * side)
    up_bias = hidden_bias(par.up_bias, layer, place)
    squares = None
    for n in range(images):
        at = slice(n * rows, (n + 1) * rows)
        found = forward_image(
            conv[at, :],
            stream[at, :],
            center,
            inv_std,
            par.batch_gain[layer : layer + 1, :],
            par.batch_bias[layer : layer + 1, :],
            par.mixing[layer],
            weights[0],
            par.layer_gain[layer : layer + 1, :],
            weights[1],
            up_bias,
            weights[2],
            side,
        )
        for name in KEPT:
            to = getattr(kept, name)
            to[at, :] = getattr(found, name).astype(to.dtype)
        squares = add_up(squares, found.squares)
        on_result(n, found.result)
    return center, inv_std, squares


def stage_backward(
    layer, place, grad_of, center, inv_std, conv, par, weights, kept, gb, gu, small, rows_ref, pieces_of,
    dp, *, images, side,
):
    rows = side * WIDE
    features = gb.shape[1]
    grad_low, gpre, gc = rows_ref
    offset = scale = gain = bias = cross = None
    for n in range(images):
        at = slice(n * rows, (n + 1) * rows)
        found = backward_image(
            grad_of(n),
            (conv[at, :] - center) * inv_std,
            kept.branch[at, :],
            kept.uhat[at, :],
            kept.inv_norm[at, :],
            kept.slope[at, :].astype(F32),
            par.mixing_back[layer],
            weights[0],
            par.layer_gain[layer : layer + 1, :],
            weights[1],
            weights[2],
        )
        grad_low[at, :] = found.grad_low
        gpre[at, :] = found.gpre
        gc[at, :] = found.gc
        gb[at, :] = found.gb
        gu[at, :] = found.gu
        offset = add_up(offset, found.offset)
        scale = add_up(scale, found.scale)
        gain = add_up(gain, found.gain)
        bias = add_up(bias, found.bias)
        cross = add_up(cross, found.cross)
    small[NORM_ROW[layer] : NORM_ROW[layer] + 1, 0:features] = gain
    groups = par.up_bias.shape[1]
    width = bias.shape[1] // groups
    for j in range(groups):
        small[pl.ds(BIAS_ROW[layer] + (place[0] ^ j), 1), 0:width] = bias[:, j * width : (j + 1) * width]
    wide, tall = mixing_grads(cross, side)
    mixes = slice(layer * WIDE, (layer + 1) * WIDE)
    small[mixes, features : features + WIDE] = wide
    small[mixes, features + WIDE : features + 2 * WIDE] = tall
    unite_grad = jnp.concatenate(
        [dot_rows(ref[...], gc[...]) for ref in (kept.branch, kept.along_w, kept.along_h)], axis=0
    )
    up_grad = dot_rows(kept.normal[...], gpre[...])
    down_grad = dot_rows(grad_low[...], kept.hidden[...])
    pack_grads(unite_grad, up_grad, down_grad, pieces_of, dp)
    return offset, scale


def first_body(ins, outs, tmp, *, images, side):
    place, taps = ins.place, ins.taps
    own, conv, moments = outs.own, outs.conv, outs.moments
    every = tmp.every
    rows = side * WIDE
    by_image(ins.stream, every)
    for n in range(images):
        own[n * rows : (n + 1) * rows, :] = every[place[0] * images + n]
    for n in range(images):
        at = slice(n * rows, (n + 1) * rows)
        conv[at, :] = convolve(own[at, :], taps[:, 0, :], side)
    local_moments(conv, moments, images, side)


def other_body(ins, outs, tmp, *, images, side):
    rows = side * WIDE
    by_image(ins.cotangent, tmp.every)
    for n in range(images):
        outs.cotangent[n * rows : (n + 1) * rows, :] = tmp.every[ins.place[0] * images + n]
    mixes = ins.mix_w[...].astype(F32), ins.mix_h[...].astype(F32)
    for layer in range(ins.mix_w.shape[1]):
        outs.mixing[layer], outs.mixing_back[layer] = mixing_matrices(
            *(mix[:, layer, :].astype(BF16) for mix in mixes), side
        )


def middle_body(ins, outs, tmp, *, images, side):
    rows = side * WIDE
    weights = outs.unite, outs.up, outs.down
    unpack_weights(tmp, *weights)

    def on_result(n, result):
        at = slice(n * rows, (n + 1) * rows)
        outs.stream1[at, :] = result
        outs.conv1[at, :] = convolve(result, ins.taps[:, 1, :], side)

    center, inv_std, squares = stage_forward(
        0, ins.place, ins.moments, ins.conv, ins.stream, ins, weights, outs, on_result,
        images=images, side=side,
    )
    outs.stats[0:1, :] = center
    outs.stats[1:2, :] = inv_std
    outs.squares[...] = squares
    local_moments(outs.conv1, outs.moments1, images, side)


def last_body(ins, outs, tmp, *, images, side, dp):
    weights = tmp.unite, tmp.up, tmp.down
    unpack_weights(tmp, *weights)
    results = []
    center, inv_std, squares = stage_forward(
        1, ins.place, ins.moments, ins.conv, ins.stream, ins, weights, tmp,
        lambda n, result: results.append(result), images=images, side=side,
    )
    outs.result[...] = pack_image_rows(jnp.concatenate(results, axis=0), side).astype(BF16)
    outs.stats[0:1, :] = center
    outs.stats[1:2, :] = inv_std
    outs.small[...] = jnp.zeros_like(outs.small)
    pieces_of = sort_pieces(ins.place[1], outs)
    offset, scale = stage_backward(
        1, ins.place, lambda n: ins.cotangent[n * side * WIDE : (n + 1) * side * WIDE, :], center, inv_std,
        ins.conv, ins, weights, tmp, outs.gb, outs.gu, outs.small,
        (tmp.grad_low, tmp.gpre, tmp.gc), pieces_of, dp, images=images, side=side,
    )
    features = squares.shape[1]
    outs.small[SQUARES_ROW[1] : SQUARES_ROW[1] + 3, 0:features] = squares
    to_all(outs.sums, 0, offset)
    to_all(outs.sums, 1, scale)


def conv_back(layer, sums, gb, gu, conv, stats, par, totals, *, images, side):
    rows = side * WIDE
    features = gb.shape[1]
    cells = images * side * side * sums.shape[0]
    offset = jnp.sum(sums[:, 0, 0:features], axis=0, keepdims=True)
    scale = jnp.sum(sums[:, 1, 0:features], axis=0, keepdims=True)
    totals[0:1, :] = offset
    totals[1:2, :] = scale
    center, inv_std = stats[0:1, :], stats[1:2, :]
    factor = par.batch_gain[layer : layer + 1, :] * inv_std
    found = []
    for n in range(images):
        at = slice(n * rows, (n + 1) * rows)
        found.append(
            conv_back_image(
                gb[at, :],
                (conv[at, :] - center) * inv_std,
                gu[at, :],
                factor,
                offset / cells,
                scale / cells,
                par.taps[:, layer, :],
                side,
            )
        )
    return found


def taps_body(ins, outs, tmp, *, images, side):
    rows = side * WIDE
    center, inv_std = ins.stats[0:1, :], ins.stats[1:2, :]
    plain = scaled = None
    for n in range(images):
        at = slice(n * rows, (n + 1) * rows)
        stream = ins.stream[at, :]
        valid = valid_rows(rows, side)
        ones = jnp.where(valid, jnp.ones_like(stream), 0.0)
        ahat = jnp.where(valid, (ins.conv[at, :] - center) * inv_std, 0.0)
        plain = add_up(plain, tap_sums(ones, stream))
        scaled = add_up(scaled, tap_sums(ahat, stream))
    outs.plain[...] = plain
    outs.scaled[...] = scaled


def sort_pieces(mine, outs):
    def put(s, piece):
        same = ((mine ^ s) & 1) == 0

        @pl.when(same)
        def _():
            outs.keep[s >> 1] = piece

        @pl.when(jnp.logical_not(same))
        def _():
            outs.give[s >> 1] = piece

    return put


def between_body(ins, outs, tmp, *, images, side, dp):
    weights = ins.unite, ins.up, ins.down
    rows = side * WIDE
    features = ins.gb1.shape[1]
    small, sums = tmp.small, outs.sums
    small[...] = ins.small[...]
    grads, kernel = [], None
    found = conv_back(
        1, ins.sums1, ins.gb1, ins.gu1, ins.conv1, ins.stats1, ins, outs.totals1, images=images, side=side
    )
    for n, (grad, ga) in enumerate(found):
        grads.append(grad)
        kernel = add_up(kernel, tap_sums(ga, ins.stream1[n * rows : (n + 1) * rows, :]))
    small[TAPS_ROW : TAPS_ROW + 9, 0:features] = kernel
    stats = ins.stats0
    offset, scale = stage_backward(
        0, ins.place, lambda n: grads[n], stats[0:1, :], stats[1:2, :], ins.conv0, ins, weights, ins,
        tmp.gb, tmp.gu, small, (tmp.grad_low, tmp.gpre, tmp.gc), sort_pieces(ins.place[1], outs), dp,
        images=images, side=side,
    )
    kernel = None
    for n in range(images):
        at = slice(n * rows, (n + 1) * rows)
        kernel = add_up(kernel, tap_sums(tmp.gb[at, :], ins.stream0[at, :]))
    for k, values in enumerate((kernel, ins.plain[...], ins.scaled[...])):
        small[9 * k : 9 * k + 9, 0:features] = values
    small[SQUARES_ROW[0] : SQUARES_ROW[0] + 3, 0:features] = ins.squares0[...]
    cells = images * side * side
    center, inv_std = stats[0:1, :], stats[1:2, :]
    grads = []
    for n in range(images):
        at = slice(n * rows, (n + 1) * rows)
        ahat = (ins.conv0[at, :] - center) * inv_std
        factor = ins.batch_gain[0:1, :] * inv_std
        grad, _ = conv_back_image(
            tmp.gb[at, :], ahat, tmp.gu[at, :], factor, offset / cells, scale / cells, ins.taps[:, 0, :], side
        )
        grads.append(grad)
    outs.grad[...] = pack_image_rows(jnp.concatenate(grads, axis=0), side).astype(BF16)
    to_all(sums, 0, offset)
    to_all(sums, 1, scale)
    devices, height, _ = sums.shape
    for g in range(height - 2):
        held = min(devices, SMALL_ROWS - g * devices)
        sums[0:held, 2 + g, :] = small[g * devices : g * devices + held, :]
        if held < devices:
            sums[held:, 2 + g, :] = jnp.zeros((devices - held, SMALL_WIDE), F32)


def final_body(ins, outs, tmp, *, images, side):
    held, rows, features = tmp.every.shape
    sums = ins.sums0
    cells = images * side * side
    devices = sums.shape[0]
    group = held // images
    offset = jnp.sum(sums[:, 0, 0:features], axis=0, keepdims=True)
    scale = jnp.sum(sums[:, 1, 0:features], axis=0, keepdims=True)
    for row, total in enumerate((offset, scale)):
        to = (outs.offset_grad, outs.scale_grad)[row]
        to[0:1, :] = total
        to[1:2, :] = ins.totals1[row : row + 1, :]
    center, inv_std = ins.stats0[0:1, :], ins.stats0[1:2, :]
    factor = ins.batch_gain[0:1, :] * inv_std
    first = ins.place[1] * group

    def apart(row, total):
        own = [sums[first + p, row : row + 1, 0:features] for p in range(group)]
        own = jnp.concatenate([value for value in own for _ in range(images)], axis=0)
        return factor * (total / (cells * devices) - own / cells)

    shift, slant = apart(0, offset), apart(1, scale)
    put_images(ins.place[0], ins.parts, tmp.every, images, side)
    padded, fields = tmp.padded, tmp.fields
    for ref in (padded, fields):
        edge = jnp.zeros((1,) + ref.shape[1:], F32)
        ref[0:1] = edge
        ref[side + 1 : side + 2] = edge
        edge = jnp.zeros((side, 1) + ref.shape[2:], F32)
        ref[1 : side + 1, 0:1] = edge
        ref[1 : side + 1, side + 1 : side + 2] = edge
    padded[1 : side + 1, 1 : side + 1] = ins.stream[...]
    taps = ins.taps[:, 0, :]
    for h in range(side):
        conv = None
        for i in range(3):
            for j in range(3):
                term = padded[h + i, j : j + side] * taps[3 * i + j : 3 * i + j + 1]
                conv = add_up(conv, term)
        fields[h + 1, 1 : side + 1] = shift + (conv - center) * inv_std * slant
    for h in range(side):
        lines = jnp.swapaxes(tmp.every[:, h * WIDE : (h + 1) * WIDE, :], 0, 1)[:side]
        for i in range(3):
            for j in range(3):
                lines = lines - fields[h + 2 - i, 2 - j : 2 - j + side] * taps[3 * i + j : 3 * i + j + 1]
        outs.out[h] = lines


def put_images(place, parts, every, images, side):
    features = every.shape[2]
    for j, part in enumerate(parts):
        packed = part[...].astype(F32)
        lines = packed.shape[0] // side
        for half in range(2):
            values = packed[:, half * features : (half + 1) * features]
            for k in range(lines):
                n, h = divmod(half * lines + k, side)
                every[(place ^ j) * images + n, h * WIDE : h * WIDE + side, :] = values[
                    k * side : (k + 1) * side
                ]


def gather_body(ins, outs, tmp):
    for g in range(outs.message.shape[1]):
        to_all(outs.message, g, jnp.sum(ins.sums0[:, 2 + g, :], axis=0, keepdims=True))


def spread_body(ins, outs, tmp, *, images, side):
    put_images(ins.place[0], ins.parts, tmp.every, images, side)
    for h in range(side):
        outs.out[h] = jnp.swapaxes(tmp.every[:, h * WIDE : (h + 1) * WIDE, :], 0, 1)[:side]


def core_body(ins, outs, tmp):
    apart = isinstance(outs.parts, list)
    for k in range(ins.keep.shape[0]):
        at = (ins.place[1] >> 1) ^ k if apart else k
        to = outs.parts[k] if apart else outs.parts.at[k]
        to[...] = (ins.keep[at].astype(F32) + ins.got[at].astype(F32)).astype(BF16)


def chips_body(ins, outs, tmp):
    groups = len(outs.give)
    for layer, parts in enumerate(ins.parts):
        parts = parts if isinstance(parts, list) else [parts.at[k] for k in range(parts.shape[0])]
        total = parts[0][...].astype(F32)
        for other in parts[1:]:
            total = total + other[...].astype(F32)
        part = total.shape[0] // 3
        width = total.shape[1] // groups
        features = outs.give[0].shape[2] - 2 * width
        for j in range(groups):
            block = jnp.concatenate(
                [
                    total[:part, j * width : (j + 1) * width],
                    total[part : 2 * part, j * width : (j + 1) * width],
                    total[2 * part :, :features],
                ],
                axis=1,
            )
            outs.give[j][layer] = block.astype(BF16)


def weights_body(ins, outs, tmp):
    layers = outs.up_grad.shape[0]
    for layer in range(layers):
        terms = [ref[layer].astype(F32) for ref in ins.got]
        while len(terms) > 1:
            terms = [terms[j] + terms[j + 1] for j in range(0, len(terms), 2)]
        total = terms[0]
        width = outs.up_grad.shape[2]
        features = outs.unite_grad.shape[1]
        outs.up_grad[layer] = total[:, :width]
        outs.down_grad[layer] = total[:, width : 2 * width]
        rest = total[:, 2 * width :]
        rows = jnp.concatenate([rest[:, q * features : (q + 1) * features] for q in range(3)], axis=0)
        outs.unite_grad[layer] = rows.T


def small_body(ins, outs, tmp, *, side, cells, entries):
    got = ins.got
    features = outs.gain_grad.shape[1]
    devices, height, _ = got.shape
    values = tmp.values
    for g in range(height):
        values[g * devices : (g + 1) * devices, :] = got[:, g, :]
    factor = ins.batch_gain[0:1, :] * ins.stats0[1:2, :]
    first = factor * (
        values[0:9, 0:features]
        - ins.offset[0:1, :] / cells * values[9:18, 0:features]
        - ins.scale[0:1, :] / cells * values[18:27, 0:features]
    )
    for k in range(9):
        outs.kernel_grad[k, 0:1, :] = first[k : k + 1]
        outs.kernel_grad[k, 1:2, :] = values[TAPS_ROW + k : TAPS_ROW + k + 1, 0:features]
    width = outs.bias_grad.shape[1]
    for layer in range(2):
        outs.gain_grad[layer : layer + 1, :] = values[NORM_ROW[layer] : NORM_ROW[layer] + 1, 0:features]
        outs.bias_grad[layer : layer + 1, :] = values[pl.ds(BIAS_ROW[layer] + ins.place[0], 1), 0:width]
        rows = slice(layer * WIDE, layer * WIDE + side)
        outs.width_grad[:, layer, :] = values[rows, features : features + side]
        outs.height_grad[:, layer, :] = values[rows, features + WIDE : features + WIDE + side]
        squares = values[SQUARES_ROW[layer] : SQUARES_ROW[layer] + 3, 0:features]
        outs.stream_rms[:, layer : layer + 1] = jnp.sqrt(
            jnp.sum(squares, axis=1, keepdims=True) / entries
        )


def call(body, ins, outs, scratch=None, shards=(), micros=0, **static):
    operands, in_tree = jax.tree.flatten(ins)
    shapes, out_tree = jax.tree.flatten(
        {name: jax.tree.map(lambda shape: jax.ShapeDtypeStruct(*shape), outs[name], is_leaf=is_shape) for name in outs}
    )
    scratch = dict(scratch or {})
    if shards:
        scratch["packed"] = (len(shards),) + shards[0].shape, shards[0].dtype
    tmp_names = list(scratch)

    def kernel(*refs):
        refs, sems = (refs[:-1], refs[-1]) if shards else (refs, None)
        cut = len(operands), len(operands) + len(shards), len(operands) + len(shards) + len(shapes)
        given = SimpleNamespace(**jax.tree.unflatten(in_tree, refs[: cut[0]]))
        results = SimpleNamespace(**jax.tree.unflatten(out_tree, refs[cut[1] : cut[2]]))
        tmp = SimpleNamespace(**dict(zip(tmp_names, refs[cut[2] :])))
        copies = [
            pltpu.make_async_copy(ref, tmp.packed.at[given.place[1] ^ k], sems.at[k])
            for k, ref in enumerate(refs[cut[0] : cut[1]])
        ]
        for copy in copies:
            copy.start()
        for copy in copies:
            copy.wait()
        body(given, results, tmp, **static)

    whole = pl.BlockSpec(memory_space=pltpu.VMEM)
    spaces = jax.tree.leaves(
        {
            name: jax.tree.map(
                lambda _: pl.BlockSpec(memory_space=pltpu.SMEM) if name == "place" else whole, ins[name]
            )
            for name in ins
        }
    )
    found = pl.pallas_call(
        kernel,
        out_shape=shapes,
        in_specs=spaces + [pl.BlockSpec(memory_space=pltpu.HBM)] * len(shards),
        out_specs=[whole] * len(shapes),
        scratch_shapes=[pltpu.VMEM(*scratch[name]) for name in tmp_names]
        + ([pltpu.SemaphoreType.DMA((len(shards),))] if shards else []),
        compiler_params=pltpu.CompilerParams(vmem_limit_bytes=VMEM_LIMIT),
        cost_estimate=pl.CostEstimate(
            flops=int(micros * COST_FLOPS), transcendentals=0, bytes_accessed=int(micros * COST_BYTES)
        ),
    )(*operands, *shards)
    return SimpleNamespace(**jax.tree.unflatten(out_tree, found))


def is_shape(value):
    return isinstance(value, tuple)


def swap(values, axis, mask):
    return lax.ppermute(values, axis, [(i, i ^ mask) for i in range(lax.axis_size(axis))])


def after(values, *others):
    return lax.optimization_barrier((values, others))[0]


def per_device(
    inputs,
    conv_weight,
    batch_gain,
    batch_bias,
    mix_width,
    mix_height,
    unite_weight,
    layer_gain,
    up_weight,
    up_bias,
    down_weight,
    cotangent,
):
    held, side, _, features = inputs.shape
    layers = conv_weight.shape[0]
    dp, mp = lax.axis_size("dp"), lax.axis_size("mp")
    devices = dp * mp
    images = held // mp
    cells = side * WIDE
    rows = images * cells
    units = up_bias.shape[1]
    part = features // dp
    both = ("dp", "mp")
    sizes = dict(images=images, side=side)
    place = jnp.stack([lax.axis_index("mp"), lax.axis_index("dp")]).astype(jnp.int32)

    def group_parts(values):
        if not isinstance(values, (list, tuple)):
            values = [values] * mp
        return [swap(value, "mp", j) if j else value for j, value in enumerate(values)]

    def share(blocks):
        return lax.all_to_all(blocks, both, 0, 0, tiled=False)

    maps = jnp.transpose(inputs, (1, 2, 0, 3))
    cotangent_maps = jnp.transpose(cotangent, (1, 2, 0, 3))
    taps = jnp.transpose(conv_weight, (1, 0, 2))
    mix_w, mix_h = (jnp.transpose(mix, (1, 0, 2)) for mix in (mix_width, mix_height))
    shared = (devices, 2, features)
    found = call(
        first_body,
        dict(place=place, stream=maps, taps=taps),
        dict(own=((rows, features), F32), conv=((rows, features), F32), moments=(shared, F32)),
        dict(every=((held, cells, features), F32)),
        micros=4,
        **sizes,
    )
    other = call(
        other_body,
        dict(place=place, cotangent=cotangent_maps, mix_w=mix_w, mix_h=mix_h),
        dict(
            cotangent=((rows, features), F32),
            mixing=((layers, 2 * cells, cells), BF16),
            mixing_back=((layers, cells, 2 * cells), BF16),
        ),
        dict(every=((held, cells, features), F32)),
        micros=3,
        **sizes,
    )

    pairs = jnp.concatenate([up_weight, down_weight], axis=1)
    thirds = unite_weight.reshape(layers, 3, part, features)
    thirds = jnp.concatenate([thirds[:, q] for q in range(3)], axis=2)
    thirds = jnp.pad(thirds, ((0, 0), (0, 0), (0, units - 3 * features)))
    wides, packed = [], []
    for layer in range(layers):
        wide, step = pairs[layer], 1
        if layer:
            wide = after(wide, wides[0][0])
        wides.append([])
        while step < mp:
            wide = jnp.concatenate([wide, swap(wide, "mp", step)], axis=1)
            wides[layer].append(wide)
            wide = after(wide, wides[0][-1] if layer else found.moments)
            step *= 2
    moments0 = share(after(found.moments, wides[0][0]))

    def over_dp(layer, wait_chips, wait_core):
        piece = after(jnp.concatenate([wides[layer][-1], thirds[layer]], axis=0), *wait_chips)
        shards = [piece] + [swap(piece, "dp", 2 * k) for k in range(1, dp // 2)]
        mates = [swap(after(shard, *wait_core), "dp", 1) for shard in shards]
        return [shard for pair in zip(shards, mates) for shard in pair]

    packed = [over_dp(0, (), (moments0, other.mixing))]

    own, conv0 = found.own, found.conv
    par = dict(
        place=place,
        taps=taps,
        batch_gain=batch_gain,
        batch_bias=batch_bias,
        layer_gain=layer_gain,
        up_bias=up_bias.reshape(layers, mp, units // mp),
    )
    kept = dict(
        branch=((rows, features), BF16),
        along_w=((rows, features), BF16),
        along_h=((rows, features), BF16),
        uhat=((rows, features), F32),
        inv_norm=((rows, 1), F32),
        normal=((rows, features), BF16),
        slope=((rows, units), BF16),
        hidden=((rows, units), BF16),
    )
    weight_tmp = dict(
        unite=((3 * features, features), BF16),
        up=((features, units), BF16),
        down=((features, units), BF16),
    )
    back_tmp = dict(
        grad_low=((rows, features), BF16), gpre=((rows, units), BF16), gc=((rows, features), BF16)
    )
    back_outs = dict(gb=((rows, features), F32), gu=((rows, features), F32))
    stats = ((2, features), F32)
    pieces = [((dp // 2, 3 * part, units), BF16)] * 2
    piece = ((3 * part, units), BF16)

    def over_core(values, apart=False):
        return call(
            core_body,
            dict(place=place, keep=values.keep, got=swap(values.give, "dp", 1)),
            dict(parts=[piece] * (dp // 2) if apart else pieces[0]),
            micros=0,
        ).parts

    def from_chips(parts):
        if isinstance(parts, list):
            return [swap(values, "dp", 2 * k) if k else values for k, values in enumerate(parts)]
        groups = [[2 * q + c for q in range(dp // 2)] for c in range(2)]
        return lax.all_to_all(parts, "dp", 0, 0, axis_index_groups=groups, tiled=False)

    mid = call(
        middle_body,
        dict(
            par,
            moments=moments0,
            conv=conv0,
            stream=own,
            mixing=other.mixing,
        ),
        dict(
            kept,
            stream1=((rows, features), F32),
            conv1=((rows, features), F32),
            moments1=(shared, F32),
            stats=stats,
            squares=((3, features), F32),
            **weight_tmp,
        ),
        None,
        packed[0],
        micros=6,
        **sizes,
    )
    packed.append(over_dp(1, packed[0][::2], (mid.moments1,)))
    under = call(
        taps_body,
        dict(stream=own, conv=conv0, stats=mid.stats),
        dict(plain=((9, features), F32), scaled=((9, features), F32)),
        micros=2,
        **sizes,
    )
    last = call(
        last_body,
        dict(
            par,
            moments=after(share(mid.moments1), under.plain),
            conv=mid.conv1,
            stream=mid.stream1,
            mixing=other.mixing,
            mixing_back=other.mixing_back,
            cotangent=other.cotangent,
        ),
        dict(
            back_outs,
            result=((images * side * side // 2, 2 * features), BF16),
            stats=stats,
            small=((SMALL_ROWS, SMALL_WIDE), F32),
            sums=(shared, F32),
            keep=pieces[0],
            give=pieces[1],
        ),
        dict(
            dict(kept, slope=((rows, units), F32)),
            **weight_tmp,
            **back_tmp,
        ),
        packed[1],
        micros=10,
        dp=dp,
        **sizes,
    )
    summed1 = over_core(last)
    groups = -(-SMALL_ROWS // devices)
    between = call(
        between_body,
        {
            **par,
            **{name: getattr(mid, name) for name in (*kept, *weight_tmp)},
            **dict(
                sums1=after(share(last.sums), summed1),
                gb1=last.gb,
                gu1=last.gu,
                conv1=mid.conv1,
                stream1=mid.stream1,
                stats1=last.stats,
                small=last.small,
                stream0=own,
                plain=under.plain,
                scaled=under.scaled,
                conv0=conv0,
                stats0=mid.stats,
                squares0=mid.squares,
                mixing_back=other.mixing_back,
            ),
        },
        dict(
            grad=((images * side * side // 2, 2 * features), BF16),
            totals1=stats,
            sums=((devices, 2 + groups, SMALL_WIDE), F32),
            keep=pieces[0],
            give=pieces[1],
        ),
        dict(
            back_tmp,
            **back_outs,
            small=((SMALL_ROWS, SMALL_WIDE), F32),
        ),
        micros=10,
        dp=dp,
        **sizes,
    )
    result = after(last.result, summed1)
    result_parts = group_parts(result)
    parts1 = from_chips(summed1)
    grad, sums0, give, parts1, result_parts = lax.optimization_barrier(
        (between.grad, between.sums, between.give, parts1, result_parts)
    )
    sums0 = share(sums0)
    chunk = call(
        gather_body, dict(sums0=sums0), dict(message=((devices, groups, SMALL_WIDE), F32)), micros=0
    )
    shared_small = share(chunk.message)
    summed0 = over_core(SimpleNamespace(keep=between.keep, give=give), True)
    grad_parts = group_parts(after(grad, summed0))
    cut = call(
        chips_body,
        dict(parts=[from_chips(summed0), parts1]),
        dict(give=[((layers, part, 2 * (units // mp) + 3 * features), BF16)] * mp),
        micros=0,
    ).give
    grads = call(
        weights_body,
        dict(got=group_parts(after(cut, grad_parts, shared_small))),
        dict(
            up_grad=((layers, part, units // mp), F32),
            down_grad=((layers, part, units // mp), F32),
            unite_grad=((layers, features, 3 * part), F32),
        ),
    )
    whole_maps = ((side, side, held, features), F32)
    output = call(
        spread_body,
        dict(place=place, parts=result_parts),
        dict(out=whole_maps),
        dict(every=((held, cells, features), F32)),
        **sizes,
    ).out
    padded = ((side + 2, side + 2, held, features), F32)
    end = call(
        final_body,
        dict(
            place=place,
            parts=grad_parts,
            stream=maps,
            sums0=sums0,
            totals1=between.totals1,
            stats0=mid.stats,
            batch_gain=batch_gain,
            taps=taps,
        ),
        dict(out=whole_maps, offset_grad=stats, scale_grad=stats),
        dict(every=((held, cells, features), F32), padded=padded, fields=padded),
        **sizes,
    )
    outputs = [jnp.transpose(out, (2, 0, 1, 3)) for out in (output, end.out)]
    small = call(
        small_body,
        dict(
            place=place,
            got=shared_small,
            batch_gain=batch_gain,
            stats0=mid.stats,
            offset=end.offset_grad,
            scale=end.scale_grad,
        ),
        dict(
            kernel_grad=((9, layers, features), F32),
            gain_grad=((layers, features), F32),
            bias_grad=((layers, units // mp), F32),
            width_grad=((side, layers, side), F32),
            height_grad=((side, layers, side), F32),
            stream_rms=((3, layers), F32),
        ),
        dict(values=((groups * devices, SMALL_WIDE), F32)),
        side=side,
        cells=images * side * side * devices,
        entries=held * side * side * features * dp,
    )
    return (
        *outputs,
        jnp.transpose(small.kernel_grad, (1, 0, 2)),
        end.scale_grad,
        end.offset_grad,
        jnp.transpose(small.width_grad, (1, 0, 2)),
        jnp.transpose(small.height_grad, (1, 0, 2)),
        jnp.transpose(grads.unite_grad, (0, 2, 1)),
        small.gain_grad,
        grads.up_grad,
        small.bias_grad,
        grads.down_grad,
        small.stream_rms.T,
    )


def solution(mesh):
    in_specs = (
        P("dp", None, None, None),
        P(),
        P(),
        P(),
        P(),
        P(),
        P(None, "dp", None),
        P(),
        P(None, "dp", "mp"),
        P(),
        P(None, "dp", "mp"),
        P("dp", None, None, None),
    )
    out_specs = (
        P("dp", None, None, None),
        P("dp", None, None, None),
        P(),
        P(),
        P(),
        P(),
        P(),
        P(None, "dp", None),
        P(),
        P(None, "dp", "mp"),
        P(None, "mp"),
        P(None, "dp", "mp"),
        P(),
    )
    return jax.shard_map(
        per_device, mesh=mesh, in_specs=in_specs, out_specs=out_specs, check_vma=False
    )
```

```python
import functools
from types import SimpleNamespace

import jax
import jax.numpy as jnp
from jax import lax
from jax.experimental import pallas as pl
from jax.experimental.pallas import tpu as pltpu
from jax.sharding import PartitionSpec as P

EPSILON = 1e-05
WIDE = 16
VMEM_LIMIT = 58 * 1024 * 1024
SMALL_LIMIT = 14 * 1024 * 1024
COST_BYTES = 3.0e6
COST_FLOPS = 1.0e10
F32 = jnp.float32
BF16 = jnp.bfloat16


def dot(left, right):
    return lax.dot_general(left, right, (((1,), (0,)), ((), ())), preferred_element_type=F32)


def dot_cols(left, right):
    return lax.dot_general(left, right, (((1,), (1,)), ((), ())), preferred_element_type=F32)


def dot_rows(left, right):
    return lax.dot_general(left, right, (((0,), (0,)), ((), ())), preferred_element_type=F32)


def valid_rows(rows, side):
    return lax.broadcasted_iota(jnp.int32, (rows, 1), 0) % WIDE < side


def three_shifts(image):
    rows, features = image.shape
    empty = jnp.zeros((WIDE, features), image.dtype)
    padded = jnp.concatenate([empty, image, empty], axis=0)
    total = rows + 2 * WIDE
    return pltpu.roll(padded, 1, 0), padded, pltpu.roll(padded, total - 1, 0)


def convolve(image, taps, side):
    rows = image.shape[0]
    shifted = three_shifts(image)
    summed = None
    for i in range(3):
        for j in range(3):
            term = shifted[j][WIDE * i : WIDE * i + rows] * taps[3 * i + j : 3 * i + j + 1]
            summed = term if summed is None else summed + term
    return jnp.where(valid_rows(rows, side), summed, 0.0)


def to_all(message_ref, row, values):
    devices = message_ref.shape[0]
    message_ref[:, row, 0 : values.shape[1]] = jnp.broadcast_to(values, (devices, values.shape[1]))


def local_moments(conv_ref, moments_ref, images, side):
    rows = side * WIDE
    count = images * side * side
    total = None
    for n in range(images):
        part = jnp.sum(conv_ref[n * rows : (n + 1) * rows, :], axis=0, keepdims=True)
        total = part if total is None else total + part
    mean = total / count
    squares = None
    for n in range(images):
        deviate = jnp.where(
            valid_rows(rows, side), conv_ref[n * rows : (n + 1) * rows, :] - mean, 0.0
        )
        part = jnp.sum(deviate * deviate, axis=0, keepdims=True)
        squares = part if squares is None else squares + part
    to_all(moments_ref, 0, mean)
    to_all(moments_ref, 1, squares)


def whole_moments(gathered_ref, count):
    devices = gathered_ref.shape[0]
    means = gathered_ref[:, 0, :]
    squares = gathered_ref[:, 1, :]
    center = jnp.sum(means, axis=0, keepdims=True) / devices
    apart = means - center
    spread = (
        jnp.sum(squares, axis=0, keepdims=True)
        + jnp.sum(apart * apart, axis=0, keepdims=True) * count
    ) / (count * devices)
    return center, lax.rsqrt(spread + EPSILON)


def mixing_matrices(mix_w, mix_h, side):
    cells = side * WIDE
    row = lax.broadcasted_iota(jnp.int32, (cells, side), 0)
    col = lax.broadcasted_iota(jnp.int32, (cells, side), 1)
    at_w = (row % WIDE == col).astype(BF16)
    at_h = (row // WIDE == col).astype(BF16)
    out = lax.broadcasted_iota(jnp.int32, (cells, cells), 0)
    inp = lax.broadcasted_iota(jnp.int32, (cells, cells), 1)
    same_h = out // WIDE == inp // WIDE
    same_w = (out % WIDE == inp % WIDE) & (out % WIDE < side)

    def spread(picks, mix, keep, flip):
        left = (dot_cols if flip else dot)(picks, mix).astype(BF16)
        return jnp.where(keep, dot_cols(left, picks), 0.0).astype(BF16)

    forward = jnp.concatenate(
        [spread(at_w, mix_w, same_h, False), spread(at_h, mix_h, same_w, False)], axis=0
    )
    backward = jnp.concatenate(
        [spread(at_w, mix_w, same_h, True), spread(at_h, mix_h, same_w, True)], axis=1
    )
    return forward, backward


def by_image(maps_ref, all_ref):
    side, _, held, features = maps_ref.shape
    empty = jnp.zeros((WIDE - side, held, features), F32)
    for h in range(side):
        lines = jnp.concatenate([maps_ref[h], empty], axis=0)
        all_ref[:, h * WIDE : (h + 1) * WIDE, :] = jnp.swapaxes(lines, 0, 1)


def unpack_weights(tmp, unite_ref, up_ref, down_ref):
    packed_ref = tmp.packed
    shards, height, _ = packed_ref.shape
    part = height // 3
    features = unite_ref.shape[1]
    ups, downs, unites = [], [], []
    for s in range(shards):
        piece = packed_ref[s].astype(F32)
        ups.append(piece[:part])
        downs.append(piece[part : 2 * part])
        for q in range(3):
            unites.append(piece[2 * part :, q * features : (q + 1) * features])
    up_ref[...] = jnp.concatenate(ups, axis=0).astype(BF16)
    down_ref[...] = jnp.concatenate(downs, axis=0).astype(BF16)
    unite_ref[...] = jnp.concatenate(unites, axis=0).astype(BF16)


def pack_grads(unite, up, down, pieces_of, dp):
    features = up.shape[0]
    part = features // dp
    for s in range(dp):
        columns = [
            unite[(3 * s + q) * part : (3 * s + q + 1) * part] for q in range(3)
        ]
        filler = jnp.zeros((part, up.shape[1] - 3 * features), F32)
        piece = jnp.concatenate(
            [
                up[s * part : (s + 1) * part],
                down[s * part : (s + 1) * part],
                jnp.concatenate(columns + [filler], axis=1),
            ],
            axis=0,
        )
        pieces_of(s, piece.astype(BF16))


def pack_image_rows(values, side):
    lines = [values[r : r + side] for r in range(0, values.shape[0], WIDE)]
    half = len(lines) // 2
    return jnp.concatenate(
        [jnp.concatenate(lines[:half], axis=0), jnp.concatenate(lines[half:], axis=0)], axis=1
    )


def hidden_bias(up_bias_ref, layer, place_ref):
    groups = up_bias_ref.shape[1]
    blocks = [up_bias_ref[layer, pl.ds(place_ref[0] ^ j, 1), :] for j in range(groups)]
    return jnp.concatenate(blocks, axis=1)


def mix_image(conv, center, inv_std, bn_gain, bn_bias, mixing, side):
    rows = conv.shape[0]
    ahat = (conv - center) * inv_std
    branch = jnp.where(valid_rows(rows, side), ahat * bn_gain + bn_bias, 0.0).astype(BF16)
    along = dot(mixing, branch).astype(BF16)
    return branch, along[:rows], along[rows:]


def mlp_image(stream, branch, along_w, along_h, unite_ref, norm_gain, up_ref, up_bias, down_ref, side):
    rows, features = stream.shape
    united = (
        dot(branch, unite_ref[0:features, :])
        + dot(along_w, unite_ref[features : 2 * features, :])
        + dot(along_h, unite_ref[2 * features :, :])
    )
    resid = stream + united
    mid = jnp.sum(resid, axis=-1, keepdims=True) / features
    deviate = resid - mid
    spread = jnp.sum(deviate * deviate, axis=-1, keepdims=True) / features
    inv_norm = lax.rsqrt(spread + EPSILON)
    uhat = deviate * inv_norm
    normal = (uhat * norm_gain).astype(BF16)
    pre = dot(normal, up_ref[...]) + up_bias
    below = 0.5 + 0.5 * lax.erf(pre * (0.5**0.5))
    slope = below + pre * (jnp.exp(-0.5 * pre * pre) * 0.3989422804014327)
    hidden = (pre * below).astype(BF16)
    mlp = jnp.where(valid_rows(rows, side), dot_cols(hidden, down_ref[...]), 0.0)
    result = resid + mlp
    squares = jnp.concatenate(
        [jnp.sum(v * v, axis=0, keepdims=True) for v in (united, mlp, result)], axis=0
    )
    return SimpleNamespace(
        uhat=uhat,
        inv_norm=inv_norm,
        slope=slope,
        hidden=hidden,
        result=result,
        squares=squares,
    )


def backward_image(
    grad, ahat, branch, uhat, inv_norm, slope, mixing_back, unite_ref, norm_gain, up_ref, down_ref
):
    rows, features = grad.shape
    grad_low = grad.astype(BF16)
    gh = dot(grad_low, down_ref[...])
    gpre = (gh * slope).astype(BF16)
    bias = jnp.sum(gpre.astype(F32), axis=0, keepdims=True)
    gn = dot_cols(gpre, up_ref[...])
    gain = jnp.sum(gn * uhat, axis=0, keepdims=True)
    q = gn * norm_gain
    mean_q = jnp.sum(q, axis=-1, keepdims=True) / features
    mean_qu = jnp.sum(q * uhat, axis=-1, keepdims=True) / features
    gu = grad + inv_norm * (q - mean_q - uhat * mean_qu)
    gc = gu.astype(BF16)
    direct = dot_cols(gc, unite_ref[0:features, :])
    wide = dot_cols(gc, unite_ref[features : 2 * features, :]).astype(BF16)
    tall = dot_cols(gc, unite_ref[2 * features :, :]).astype(BF16)
    both = jnp.concatenate([wide, tall], axis=0)
    gb = direct + dot(mixing_back, both)
    cross = dot_cols(both, branch)
    return SimpleNamespace(
        grad_low=grad_low,
        gpre=gpre,
        bias=bias,
        gain=gain,
        gu=gu,
        gc=gc,
        gb=gb,
        cross=cross,
        offset=jnp.sum(gb, axis=0, keepdims=True),
        scale=jnp.sum(gb * ahat, axis=0, keepdims=True),
    )


def mixing_grads(cross, side):
    cells = side * WIDE
    width = None
    for h in range(side):
        at = slice(h * WIDE, (h + 1) * WIDE)
        width = add_up(width, cross[at, at])
    out = lax.broadcasted_iota(jnp.int32, (cells, cells), 0)
    inp = lax.broadcasted_iota(jnp.int32, (cells, cells), 1)
    kept = jnp.where(out % WIDE == inp % WIDE, cross[cells:], 0.0)
    lines = jnp.concatenate(
        [jnp.sum(kept[v * WIDE : (v + 1) * WIDE], axis=0, keepdims=True) for v in range(side)]
        + [jnp.zeros((WIDE - side, cells), F32)],
        axis=0,
    )
    row = lax.broadcasted_iota(jnp.int32, (cells, WIDE), 0)
    col = lax.broadcasted_iota(jnp.int32, (cells, WIDE), 1)
    height = lax.dot_general(
        lines,
        (row // WIDE == col).astype(F32),
        (((1,), (0,)), ((), ())),
        precision=lax.Precision.HIGHEST,
        preferred_element_type=F32,
    )
    return width, height


def tap_sums(values, stream):
    rows = values.shape[0]
    shifted = three_shifts(stream)
    return jnp.concatenate(
        [
            jnp.sum(values * shifted[j][WIDE * i : WIDE * i + rows], axis=0, keepdims=True)
            for i in range(3)
            for j in range(3)
        ],
        axis=0,
    )


def conv_back_image(gb, ahat, gu, factor, offset_mean, scale_mean, taps, side):
    rows = gb.shape[0]
    valid = valid_rows(rows, side)
    ga = jnp.where(valid, factor * (gb - offset_mean - ahat * scale_mean), 0.0)
    turned = three_shifts(ga)
    summed = gu
    for i in range(3):
        for j in range(3):
            summed = (
                summed
                + turned[2 - j][WIDE * (2 - i) : WIDE * (2 - i) + rows]
                * taps[3 * i + j : 3 * i + j + 1]
            )
    return jnp.where(valid, summed, 0.0), ga


def add_up(total, part):
    return part if total is None else total + part


SMALL_ROWS, SMALL_WIDE = 60, 384
NORM_ROW, SQUARES_ROW, BIAS_ROW, TAPS_ROW = (27, 48), (28, 49), (31, 52), 39
KEPT = ("uhat", "inv_norm", "slope", "hidden")


def stage_forward(layer, ins, weights, weights_of, kept, on_result, *, images, side):
    rows = side * WIDE
    at = [slice(n * rows, (n + 1) * rows) for n in range(images)]
    center, inv_std = whole_moments(ins.moments, images * side * side)
    for n in range(images):
        kept.branch[at[n], :], kept.along_w[at[n], :], kept.along_h[at[n], :] = mix_image(
            ins.conv[at[n], :],
            center,
            inv_std,
            ins.batch_gain[layer : layer + 1, :],
            ins.batch_bias[layer : layer + 1, :],
            ins.mixing[...],
            side,
        )
    weights_of()
    up_bias = hidden_bias(ins.up_bias, layer, ins.place)
    squares = None
    for n in range(images):
        found = mlp_image(
            ins.stream[at[n], :],
            kept.branch[at[n], :],
            kept.along_w[at[n], :],
            kept.along_h[at[n], :],
            weights[0],
            ins.layer_gain[layer : layer + 1, :],
            weights[1],
            up_bias,
            weights[2],
            side,
        )
        for name in KEPT:
            to = getattr(kept, name)
            to[at[n], :] = getattr(found, name).astype(to.dtype)
        squares = add_up(squares, found.squares)
        on_result(n, found.result)
    return center, inv_std, squares


def stage_backward(
    layer, place, grad_of, center, inv_std, conv, par, weights, kept, gb, gu, small, rows_ref, pieces_of,
    dp, *, images, side,
):
    rows = side * WIDE
    features = gb.shape[1]
    grad_low, gpre, gc = rows_ref
    offset = scale = gain = bias = cross = None
    for n in range(images):
        at = slice(n * rows, (n + 1) * rows)
        found = backward_image(
            grad_of(n),
            (conv[at, :] - center) * inv_std,
            kept.branch[at, :],
            kept.uhat[at, :],
            kept.inv_norm[at, :],
            kept.slope[at, :].astype(F32),
            par.mixing_back[...],
            weights[0],
            par.layer_gain[layer : layer + 1, :],
            weights[1],
            weights[2],
        )
        grad_low[at, :] = found.grad_low
        gpre[at, :] = found.gpre
        gc[at, :] = found.gc
        gb[at, :] = found.gb.astype(gb.dtype)
        gu[at, :] = found.gu.astype(gu.dtype)
        offset = add_up(offset, found.offset)
        scale = add_up(scale, found.scale)
        gain = add_up(gain, found.gain)
        bias = add_up(bias, found.bias)
        cross = add_up(cross, found.cross)
    small[NORM_ROW[layer] : NORM_ROW[layer] + 1, 0:features] = gain
    groups = par.up_bias.shape[1]
    width = bias.shape[1] // groups
    for j in range(groups):
        small[pl.ds(BIAS_ROW[layer] + (place[0] ^ j), 1), 0:width] = bias[:, j * width : (j + 1) * width]
    wide, tall = mixing_grads(cross, side)
    mixes = slice(layer * WIDE, (layer + 1) * WIDE)
    small[mixes, features : features + WIDE] = wide
    small[mixes, features + WIDE : features + 2 * WIDE] = tall
    unite_grad = jnp.concatenate(
        [dot_rows(ref[...], gc[...]) for ref in (kept.branch, kept.along_w, kept.along_h)], axis=0
    )
    normal = (kept.uhat[...] * par.layer_gain[layer : layer + 1, :]).astype(BF16)
    up_grad = dot_rows(normal, gpre[...])
    down_grad = dot_rows(grad_low[...], kept.hidden[...])
    pack_grads(unite_grad, up_grad, down_grad, pieces_of, dp)
    return offset, scale


def first_body(ins, outs, tmp, *, images, side):
    place, taps = ins.place, ins.taps
    own, conv, moments = outs.own, outs.conv, outs.moments
    every = tmp.every
    rows = side * WIDE
    by_image(ins.stream, every)
    for n in range(images):
        own[n * rows : (n + 1) * rows, :] = every[place[0] * images + n]
    for n in range(images):
        at = slice(n * rows, (n + 1) * rows)
        conv[at, :] = convolve(own[at, :], taps[:, 0, :], side)
    local_moments(conv, moments, images, side)


def other_body(ins, outs, tmp, *, images, side):
    rows = side * WIDE
    by_image(ins.cotangent, tmp.every)
    for n in range(images):
        outs.cotangent[n * rows : (n + 1) * rows, :] = tmp.every[ins.place[0] * images + n]
    _, groups, width = outs.up_bias.shape
    for j in range(groups):
        outs.up_bias[:, j, :] = ins.up_bias[:, j * width : (j + 1) * width]
    mixes = ins.mix_w[...].astype(F32), ins.mix_h[...].astype(F32)
    for layer in range(ins.mix_w.shape[1]):
        outs.mixing[layer][...], outs.mixing_back[layer][...] = mixing_matrices(
            *(mix[:, layer, :].astype(BF16) for mix in mixes), side
        )


def middle_body(ins, outs, tmp, *, images, side):
    rows = side * WIDE
    weights = tmp.unite, tmp.up, tmp.down
    results = []

    def weights_of():
        unpack_weights(tmp, *weights)

    center, inv_std, squares = stage_forward(
        0, ins, weights, weights_of, outs, lambda n, result: results.append(result), images=images, side=side
    )
    outs.stats[0:1, :] = center
    outs.stats[1:2, :] = inv_std
    outs.squares[...] = squares
    for n, result in enumerate(results):
        at = slice(n * rows, (n + 1) * rows)
        outs.stream1[at, :] = result
        outs.conv1[at, :] = convolve(result, ins.taps[:, 1, :], side)
    local_moments(outs.conv1, outs.moments1, images, side)


def last_body(ins, outs, tmp, *, images, side, dp):
    weights = tmp.unite, tmp.up, tmp.down
    results = []

    def weights_of():
        unpack_weights(tmp, *weights)

    center, inv_std, squares = stage_forward(
        1, ins, weights, weights_of, tmp, lambda n, result: results.append(result), images=images, side=side
    )
    outs.result[...] = pack_image_rows(jnp.concatenate(results, axis=0), side).astype(BF16)
    outs.stats[0:1, :] = center
    outs.stats[1:2, :] = inv_std
    outs.small[...] = jnp.zeros_like(outs.small)
    pieces_of = sort_pieces(ins.place[1], outs)
    offset, scale = stage_backward(
        1, ins.place, lambda n: ins.cotangent[n * side * WIDE : (n + 1) * side * WIDE, :], center, inv_std,
        ins.conv, ins, weights, tmp, outs.gb, outs.gu, outs.small,
        (tmp.grad_low, tmp.gpre, tmp.gc), pieces_of, dp, images=images, side=side,
    )
    features = squares.shape[1]
    outs.small[SQUARES_ROW[1] : SQUARES_ROW[1] + 3, 0:features] = squares
    to_all(outs.sums, 0, offset)
    to_all(outs.sums, 1, scale)


def conv_back(layer, sums, gb, gu, conv, stats, par, totals, *, images, side):
    rows = side * WIDE
    features = gb.shape[1]
    cells = images * side * side * sums.shape[0]
    offset = jnp.sum(sums[:, 0, 0:features], axis=0, keepdims=True)
    scale = jnp.sum(sums[:, 1, 0:features], axis=0, keepdims=True)
    totals[0:1, :] = offset
    totals[1:2, :] = scale
    center, inv_std = stats[0:1, :], stats[1:2, :]
    factor = par.batch_gain[layer : layer + 1, :] * inv_std
    found = []
    for n in range(images):
        at = slice(n * rows, (n + 1) * rows)
        found.append(
            conv_back_image(
                gb[at, :].astype(F32),
                (conv[at, :] - center) * inv_std,
                gu[at, :].astype(F32),
                factor,
                offset / cells,
                scale / cells,
                par.taps[:, layer, :],
                side,
            )
        )
    return found


def taps_body(ins, outs, tmp, *, images, side):
    rows = side * WIDE
    center, inv_std = ins.stats[0:1, :], ins.stats[1:2, :]
    plain = scaled = None
    for n in range(images):
        at = slice(n * rows, (n + 1) * rows)
        stream = ins.stream[at, :]
        valid = valid_rows(rows, side)
        ones = jnp.where(valid, jnp.ones_like(stream), 0.0)
        ahat = jnp.where(valid, (ins.conv[at, :] - center) * inv_std, 0.0)
        plain = add_up(plain, tap_sums(ones, stream))
        scaled = add_up(scaled, tap_sums(ahat, stream))
    outs.plain[...] = plain
    outs.scaled[...] = scaled


def sort_pieces(mine, outs):
    def put(s, piece):
        same = ((mine ^ s) & 1) == 0

        @pl.when(same)
        def _():
            outs.keep[s >> 1] = piece

        @pl.when(jnp.logical_not(same))
        def _():
            outs.give[s >> 1] = piece

    return put


def between_body(ins, outs, tmp, *, images, side, dp):
    weights = tmp.unite, tmp.up, tmp.down
    unpack_weights(tmp, *weights)
    rows = side * WIDE
    features = ins.gb1.shape[1]
    small, sums = tmp.small, outs.sums
    small[...] = ins.small[...]
    grads, kernel = [], None
    found = conv_back(
        1, ins.sums1, ins.gb1, ins.gu1, ins.conv1, ins.stats1, ins, outs.totals1, images=images, side=side
    )
    for n, (grad, ga) in enumerate(found):
        grads.append(grad)
        kernel = add_up(kernel, tap_sums(ga, ins.stream1[n * rows : (n + 1) * rows, :]))
    small[TAPS_ROW : TAPS_ROW + 9, 0:features] = kernel
    stats = ins.stats0
    offset, scale = stage_backward(
        0, ins.place, lambda n: grads[n], stats[0:1, :], stats[1:2, :], ins.conv0, ins, weights, ins,
        tmp.gb, tmp.gu, small, (tmp.grad_low, tmp.gpre, tmp.gc), sort_pieces(ins.place[1], outs), dp,
        images=images, side=side,
    )
    kernel = None
    for n in range(images):
        at = slice(n * rows, (n + 1) * rows)
        kernel = add_up(kernel, tap_sums(tmp.gb[at, :], ins.stream0[at, :]))
    for k, values in enumerate((kernel, ins.plain[...], ins.scaled[...])):
        small[9 * k : 9 * k + 9, 0:features] = values
    small[SQUARES_ROW[0] : SQUARES_ROW[0] + 3, 0:features] = ins.squares0[...]
    cells = images * side * side
    center, inv_std = stats[0:1, :], stats[1:2, :]
    grads = []
    for n in range(images):
        at = slice(n * rows, (n + 1) * rows)
        ahat = (ins.conv0[at, :] - center) * inv_std
        factor = ins.batch_gain[0:1, :] * inv_std
        grad, _ = conv_back_image(
            tmp.gb[at, :], ahat, tmp.gu[at, :], factor, offset / cells, scale / cells, ins.taps[:, 0, :], side
        )
        grads.append(grad)
    outs.grad[...] = pack_image_rows(jnp.concatenate(grads, axis=0), side).astype(BF16)
    to_all(sums, 0, offset)
    to_all(sums, 1, scale)
    devices, height, _ = sums.shape
    for g in range(height - 2):
        held = min(devices, SMALL_ROWS - g * devices)
        sums[0:held, 2 + g, :] = small[g * devices : g * devices + held, :]
        if held < devices:
            sums[held:, 2 + g, :] = jnp.zeros((devices - held, SMALL_WIDE), F32)


def final_body(ins, outs, tmp, *, images, side):
    held, rows, features = tmp.every.shape
    sums = ins.sums0
    cells = images * side * side
    devices = sums.shape[0]
    group = held // images
    offset = jnp.sum(sums[:, 0, 0:features], axis=0, keepdims=True)
    scale = jnp.sum(sums[:, 1, 0:features], axis=0, keepdims=True)
    for row, total in enumerate((offset, scale)):
        to = (outs.offset_grad, outs.scale_grad)[row]
        to[0:1, :] = total
        to[1:2, :] = ins.totals1[row : row + 1, :]
    center, inv_std = ins.stats0[0:1, :], ins.stats0[1:2, :]
    factor = ins.batch_gain[0:1, :] * inv_std
    first = ins.place[1] * group

    def apart(row, total):
        own = [sums[first + p, row : row + 1, 0:features] for p in range(group)]
        own = jnp.concatenate([value for value in own for _ in range(images)], axis=0)
        return factor * (total / (cells * devices) - own / cells)

    shift, slant = apart(0, offset), apart(1, scale)
    put_images(ins.place[0], ins.parts, tmp.every, images, side)
    padded, fields = tmp.padded, tmp.fields
    for ref in (padded, fields):
        edge = jnp.zeros((1,) + ref.shape[1:], F32)
        ref[0:1] = edge
        ref[side + 1 : side + 2] = edge
        edge = jnp.zeros((side, 1) + ref.shape[2:], F32)
        ref[1 : side + 1, 0:1] = edge
        ref[1 : side + 1, side + 1 : side + 2] = edge
    padded[1 : side + 1, 1 : side + 1] = ins.stream[...]
    taps = ins.taps[:, 0, :]
    for h in range(side):
        conv = None
        for i in range(3):
            for j in range(3):
                term = padded[h + i, j : j + side] * taps[3 * i + j : 3 * i + j + 1]
                conv = add_up(conv, term)
        fields[h + 1, 1 : side + 1] = shift + (conv - center) * inv_std * slant
    for h in range(side):
        lines = jnp.swapaxes(tmp.every[:, h * WIDE : (h + 1) * WIDE, :], 0, 1)[:side]
        for i in range(3):
            for j in range(3):
                lines = lines - fields[h + 2 - i, 2 - j : 2 - j + side] * taps[3 * i + j : 3 * i + j + 1]
        outs.out[h] = lines


def put_images(place, parts, every, images, side):
    features = every.shape[2]
    for j, part in enumerate(parts):
        packed = part[...].astype(F32)
        lines = packed.shape[0] // side
        for half in range(2):
            values = packed[:, half * features : (half + 1) * features]
            for k in range(lines):
                n, h = divmod(half * lines + k, side)
                every[(place ^ j) * images + n, h * WIDE : h * WIDE + side, :] = values[
                    k * side : (k + 1) * side
                ]


def gather_body(ins, outs, tmp):
    for g in range(outs.message.shape[1]):
        to_all(outs.message, g, jnp.sum(ins.sums0[:, 2 + g, :], axis=0, keepdims=True))


def spread_body(ins, outs, tmp, *, images, side):
    put_images(ins.place[0], ins.parts, tmp.every, images, side)
    for h in range(side):
        outs.out[h] = jnp.swapaxes(tmp.every[:, h * WIDE : (h + 1) * WIDE, :], 0, 1)[:side]


def core_body(ins, outs, tmp):
    apart = isinstance(outs.parts, list)
    for k in range(ins.keep.shape[0]):
        at = (ins.place[1] >> 1) ^ k if apart else k
        to = outs.parts[k] if apart else outs.parts.at[k]
        to[...] = (ins.keep[at].astype(F32) + ins.got[at].astype(F32)).astype(BF16)


def chips_body(ins, outs, tmp):
    groups = len(outs.give)
    for layer, parts in enumerate(ins.parts):
        parts = parts if isinstance(parts, list) else [parts.at[k] for k in range(parts.shape[0])]
        total = parts[0][...].astype(F32)
        for other in parts[1:]:
            total = total + other[...].astype(F32)
        part = total.shape[0] // 3
        width = total.shape[1] // groups
        features = outs.give[0].shape[2] - 2 * width
        for j in range(groups):
            block = jnp.concatenate(
                [
                    total[:part, j * width : (j + 1) * width],
                    total[part : 2 * part, j * width : (j + 1) * width],
                    total[2 * part :, :features],
                ],
                axis=1,
            )
            outs.give[j][layer] = block.astype(BF16)


def weights_body(ins, outs, tmp):
    layers = outs.up_grad.shape[0]
    for layer in range(layers):
        terms = [ref[layer].astype(F32) for ref in ins.got]
        while len(terms) > 1:
            terms = [terms[j] + terms[j + 1] for j in range(0, len(terms), 2)]
        total = terms[0]
        width = outs.up_grad.shape[2]
        features = outs.unite_grad.shape[1]
        outs.up_grad[layer] = total[:, :width]
        outs.down_grad[layer] = total[:, width : 2 * width]
        rest = total[:, 2 * width :]
        rows = jnp.concatenate([rest[:, q * features : (q + 1) * features] for q in range(3)], axis=0)
        outs.unite_grad[layer] = rows.T


def small_body(ins, outs, tmp, *, side, cells, entries):
    got = ins.got
    features = outs.gain_grad.shape[1]
    devices, height, _ = got.shape
    values = tmp.values
    for g in range(height):
        values[g * devices : (g + 1) * devices, :] = got[:, g, :]
    factor = ins.batch_gain[0:1, :] * ins.stats0[1:2, :]
    first = factor * (
        values[0:9, 0:features]
        - ins.offset[0:1, :] / cells * values[9:18, 0:features]
        - ins.scale[0:1, :] / cells * values[18:27, 0:features]
    )
    for k in range(9):
        outs.kernel_grad[k, 0:1, :] = first[k : k + 1]
        outs.kernel_grad[k, 1:2, :] = values[TAPS_ROW + k : TAPS_ROW + k + 1, 0:features]
    width = outs.bias_grad.shape[1]
    for layer in range(2):
        outs.gain_grad[layer : layer + 1, :] = values[NORM_ROW[layer] : NORM_ROW[layer] + 1, 0:features]
        outs.bias_grad[layer : layer + 1, :] = values[pl.ds(BIAS_ROW[layer] + ins.place[0], 1), 0:width]
        rows = slice(layer * WIDE, layer * WIDE + side)
        outs.width_grad[:, layer, :] = values[rows, features : features + side]
        outs.height_grad[:, layer, :] = values[rows, features + WIDE : features + WIDE + side]
        squares = values[SQUARES_ROW[layer] : SQUARES_ROW[layer] + 3, 0:features]
        outs.stream_rms[:, layer : layer + 1] = jnp.sqrt(
            jnp.sum(squares, axis=1, keepdims=True) / entries
        )


def call(body, ins, outs, scratch=None, shards=(), micros=0, vmem=VMEM_LIMIT, **static):
    ins = dict(ins, shards=list(shards))
    operands, in_tree = jax.tree.flatten(ins)
    shapes, out_tree = jax.tree.flatten(
        {name: jax.tree.map(lambda shape: jax.ShapeDtypeStruct(*shape), outs[name], is_leaf=is_shape) for name in outs}
    )
    scratch = dict(scratch or {})
    if shards:
        scratch["packed"] = (len(shards),) + shards[0].shape, shards[0].dtype
    tmp_names = list(scratch)

    def kernel(*refs):
        cut = len(operands), len(operands) + len(shapes)
        given = SimpleNamespace(**jax.tree.unflatten(in_tree, refs[: cut[0]]))
        results = SimpleNamespace(**jax.tree.unflatten(out_tree, refs[cut[0] : cut[1]]))
        tmp = SimpleNamespace(**dict(zip(tmp_names, refs[cut[1] :])))
        for k, shard in enumerate(given.shards):
            tmp.packed[given.place[1] ^ k] = shard[...]
        body(given, results, tmp, **static)

    def space(name):
        return pl.BlockSpec(memory_space=pltpu.SMEM if name == "place" else pltpu.VMEM)

    found = pl.pallas_call(
        kernel,
        out_shape=shapes,
        in_specs=jax.tree.leaves({name: jax.tree.map(lambda _: space(name), ins[name]) for name in ins}),
        out_specs=[space("")] * len(shapes),
        scratch_shapes=[pltpu.VMEM(*scratch[name]) for name in tmp_names],
        compiler_params=pltpu.CompilerParams(vmem_limit_bytes=vmem),
        cost_estimate=pl.CostEstimate(
            flops=int(micros * COST_FLOPS), transcendentals=0, bytes_accessed=int(micros * COST_BYTES)
        ),
    )(*operands)
    return SimpleNamespace(**jax.tree.unflatten(out_tree, found))


def is_shape(value):
    return isinstance(value, tuple)


def swap(values, axis, mask):
    return lax.ppermute(values, axis, [(i, i ^ mask) for i in range(lax.axis_size(axis))])


def after(values, *others):
    return lax.optimization_barrier((values, others))[0]


def per_device(
    inputs,
    conv_weight,
    batch_gain,
    batch_bias,
    mix_width,
    mix_height,
    unite_weight,
    layer_gain,
    up_weight,
    up_bias,
    down_weight,
    cotangent,
):
    held, side, _, features = inputs.shape
    layers = conv_weight.shape[0]
    dp, mp = lax.axis_size("dp"), lax.axis_size("mp")
    devices = dp * mp
    images = held // mp
    cells = side * WIDE
    rows = images * cells
    units = up_bias.shape[1]
    part = features // dp
    both = ("dp", "mp")
    sizes = dict(images=images, side=side)
    place = jnp.stack([lax.axis_index("mp"), lax.axis_index("dp")]).astype(jnp.int32)

    def group_parts(values):
        if not isinstance(values, (list, tuple)):
            values = [values] * mp
        return [swap(value, "mp", j) if j else value for j, value in enumerate(values)]

    def share(blocks):
        return lax.all_to_all(blocks, both, 0, 0, tiled=False)

    maps = jnp.transpose(inputs, (1, 2, 0, 3))
    cotangent_maps = jnp.transpose(cotangent, (1, 2, 0, 3))
    taps = jnp.transpose(conv_weight, (1, 0, 2))
    mix_w, mix_h = (jnp.transpose(mix, (1, 0, 2)) for mix in (mix_width, mix_height))
    shared = (devices, 2, features)
    thirds = unite_weight.reshape(layers, 3, part, features)
    thirds = jnp.concatenate([thirds[:, q] for q in range(3)], axis=2)
    thirds = jnp.pad(thirds, ((0, 0), (0, 0), (0, units - 3 * features)))

    def widen(wide, step):
        return jnp.concatenate([wide, swap(wide, "mp", step)], axis=1)

    def over_dp(layer, wide, wait_chips, wait_core):
        piece = after(jnp.concatenate([wide, thirds[layer]], axis=0), *wait_chips)
        shards = [piece] + [swap(piece, "dp", 2 * k) for k in range(1, dp // 2)]
        mates = [swap(after(shard, *wait_core), "dp", 1) for shard in shards]
        return [shard for pair in zip(shards, mates) for shard in pair]

    wide = jnp.concatenate([up_weight[0], down_weight[0]], axis=0)
    wide = near = widen(wide, 1) if mp > 1 else wide
    step = 2
    while step < mp:
        wide = widen(wide, step)
        step *= 2
    found = call(
        first_body,
        dict(place=after(place, near), stream=maps, taps=taps),
        dict(own=((rows, features), F32), conv=((rows, features), F32), moments=(shared, F32)),
        dict(every=((held, cells, features), F32)),
        micros=4,
        **sizes,
    )
    moments0 = share(after(found.moments, wide))
    other = call(
        other_body,
        dict(place=place, cotangent=cotangent_maps, mix_w=mix_w, mix_h=mix_h, up_bias=up_bias),
        dict(
            cotangent=((rows, features), F32),
            up_bias=((layers, mp, units // mp), F32),
            mixing=[((2 * cells, cells), BF16)] * layers,
            mixing_back=[((cells, 2 * cells), BF16)] * layers,
        ),
        dict(every=((held, cells, features), F32)),
        micros=3,
        **sizes,
    )

    packed = [over_dp(0, wide, (found.moments,), (moments0, other.mixing[0]))]
    wide = after(jnp.concatenate([up_weight[1], down_weight[1]], axis=0), wide)
    step = 1
    while step < mp:
        wide = widen(wide, step)
        step *= 2
    wide1 = wide

    own, conv0 = found.own, found.conv
    par = dict(
        place=place,
        taps=taps,
        batch_gain=batch_gain,
        batch_bias=batch_bias,
        layer_gain=layer_gain,
        up_bias=other.up_bias,
    )
    kept = dict(
        branch=((rows, features), BF16),
        along_w=((rows, features), BF16),
        along_h=((rows, features), BF16),
        uhat=((rows, features), F32),
        inv_norm=((rows, 1), F32),
        slope=((rows, units), BF16),
        hidden=((rows, units), BF16),
    )
    weight_tmp = dict(
        unite=((3 * features, features), BF16),
        up=((features, units), BF16),
        down=((features, units), BF16),
    )
    back_tmp = dict(
        grad_low=((rows, features), BF16), gpre=((rows, units), BF16), gc=((rows, features), BF16)
    )
    back_outs = dict(gb=((rows, features), F32), gu=((rows, features), F32))
    stats = ((2, features), F32)
    pieces = [((dp // 2, 3 * part, units), BF16)] * 2
    piece = ((3 * part, units), BF16)

    def over_core(values, apart=False):
        return call(
            core_body,
            dict(place=place, keep=values.keep, got=swap(values.give, "dp", 1)),
            dict(parts=[piece] * (dp // 2) if apart else pieces[0]),
            vmem=SMALL_LIMIT,
        ).parts

    def from_chips(parts):
        if isinstance(parts, list):
            return [swap(values, "dp", 2 * k) if k else values for k, values in enumerate(parts)]
        groups = [[2 * q + c for q in range(dp // 2)] for c in range(2)]
        return lax.all_to_all(parts, "dp", 0, 0, axis_index_groups=groups, tiled=False)

    mid = call(
        middle_body,
        dict(
            par,
            moments=moments0,
            conv=conv0,
            stream=own,
            mixing=other.mixing[0],
        ),
        dict(
            kept,
            stream1=((rows, features), F32),
            conv1=((rows, features), F32),
            moments1=(shared, F32),
            stats=stats,
            squares=((3, features), F32),
        ),
        weight_tmp,
        packed[0],
        micros=6,
        **sizes,
    )
    packed.append(over_dp(1, wide1, packed[0][::2], (mid.moments1,)))
    under = call(
        taps_body,
        dict(stream=own, conv=conv0, stats=mid.stats),
        dict(plain=((9, features), F32), scaled=((9, features), F32)),
        micros=2,
        **sizes,
    )
    last = call(
        last_body,
        dict(
            par,
            moments=after(share(mid.moments1), under.plain),
            conv=mid.conv1,
            stream=mid.stream1,
            mixing=other.mixing[1],
            mixing_back=other.mixing_back[1],
            cotangent=other.cotangent,
        ),
        dict(
            gb=((rows, features), BF16),
            gu=((rows, features), BF16),
            result=((images * side * side // 2, 2 * features), BF16),
            stats=stats,
            small=((SMALL_ROWS, SMALL_WIDE), F32),
            sums=(shared, F32),
            keep=pieces[0],
            give=pieces[1],
        ),
        dict(
            dict(kept, slope=((rows, units), F32)),
            **weight_tmp,
            **back_tmp,
        ),
        packed[1],
        micros=10,
        dp=dp,
        **sizes,
    )
    summed1 = over_core(last)
    groups = -(-SMALL_ROWS // devices)
    between = call(
        between_body,
        {
            **par,
            **{name: getattr(mid, name) for name in kept},
            **dict(
                sums1=after(share(last.sums), summed1),
                gb1=last.gb,
                gu1=last.gu,
                conv1=mid.conv1,
                stream1=mid.stream1,
                stats1=last.stats,
                small=last.small,
                stream0=own,
                plain=under.plain,
                scaled=under.scaled,
                conv0=conv0,
                stats0=mid.stats,
                squares0=mid.squares,
                mixing_back=other.mixing_back[0],
            ),
        },
        dict(
            grad=((images * side * side // 2, 2 * features), BF16),
            totals1=stats,
            sums=((devices, 2 + groups, SMALL_WIDE), F32),
            keep=pieces[0],
            give=pieces[1],
        ),
        dict(
            back_tmp,
            **back_outs,
            **weight_tmp,
            small=((SMALL_ROWS, SMALL_WIDE), F32),
        ),
        packed[0],
        micros=10,
        dp=dp,
        **sizes,
    )
    result = after(last.result, summed1)
    result_parts = group_parts(result)
    parts1 = from_chips(summed1)
    grad, sums0, give, parts1, result_parts = lax.optimization_barrier(
        (between.grad, between.sums, between.give, parts1, result_parts)
    )
    sums0 = share(sums0)
    chunk = call(
        gather_body, dict(sums0=sums0), dict(message=((devices, groups, SMALL_WIDE), F32)), vmem=SMALL_LIMIT
    )
    shared_small = share(chunk.message)
    summed0 = over_core(SimpleNamespace(keep=between.keep, give=give), True)
    grad_parts = group_parts(after(grad, summed0))
    cut = call(
        chips_body,
        dict(parts=[from_chips(summed0), parts1]),
        dict(give=[((layers, part, 2 * (units // mp) + 3 * features), BF16)] * mp),
        vmem=SMALL_LIMIT,
    ).give
    grads = call(
        weights_body,
        dict(got=group_parts(after(cut, grad_parts, shared_small))),
        dict(
            up_grad=((layers, part, units // mp), F32),
            down_grad=((layers, part, units // mp), F32),
            unite_grad=((layers, features, 3 * part), F32),
        ),
        vmem=SMALL_LIMIT,
    )
    whole_maps = ((side, side, held, features), F32)
    output = call(
        spread_body,
        dict(place=place, parts=result_parts),
        dict(out=whole_maps),
        dict(every=((held, cells, features), F32)),
        **sizes,
    ).out
    padded = ((side + 2, side + 2, held, features), F32)
    end = call(
        final_body,
        dict(
            place=place,
            parts=grad_parts,
            stream=maps,
            sums0=sums0,
            totals1=between.totals1,
            stats0=mid.stats,
            batch_gain=batch_gain,
            taps=taps,
        ),
        dict(out=whole_maps, offset_grad=stats, scale_grad=stats),
        dict(every=((held, cells, features), F32), padded=padded, fields=padded),
        **sizes,
    )
    outputs = [jnp.transpose(out, (2, 0, 1, 3)) for out in (output, end.out)]
    small = call(
        small_body,
        dict(
            place=place,
            got=shared_small,
            batch_gain=batch_gain,
            stats0=mid.stats,
            offset=end.offset_grad,
            scale=end.scale_grad,
        ),
        dict(
            kernel_grad=((9, layers, features), F32),
            gain_grad=((layers, features), F32),
            bias_grad=((layers, units // mp), F32),
            width_grad=((side, layers, side), F32),
            height_grad=((side, layers, side), F32),
            stream_rms=((3, layers), F32),
        ),
        dict(values=((groups * devices, SMALL_WIDE), F32)),
        vmem=SMALL_LIMIT,
        side=side,
        cells=images * side * side * devices,
        entries=held * side * side * features * dp,
    )
    return (
        *outputs,
        jnp.transpose(small.kernel_grad, (1, 0, 2)),
        end.scale_grad,
        end.offset_grad,
        jnp.transpose(small.width_grad, (1, 0, 2)),
        jnp.transpose(small.height_grad, (1, 0, 2)),
        jnp.transpose(grads.unite_grad, (0, 2, 1)),
        small.gain_grad,
        grads.up_grad,
        small.bias_grad,
        grads.down_grad,
        small.stream_rms.T,
    )


def solution(mesh):
    in_specs = (
        P("dp", None, None, None),
        P(),
        P(),
        P(),
        P(),
        P(),
        P(None, "dp", None),
        P(),
        P(None, "dp", "mp"),
        P(),
        P(None, "dp", "mp"),
        P("dp", None, None, None),
    )
    out_specs = (
        P("dp", None, None, None),
        P("dp", None, None, None),
        P(),
        P(),
        P(),
        P(),
        P(),
        P(None, "dp", None),
        P(),
        P(None, "dp", "mp"),
        P(None, "mp"),
        P(None, "dp", "mp"),
        P(),
    )
    return jax.shard_map(
        per_device, mesh=mesh, in_specs=in_specs, out_specs=out_specs, check_vma=False
    )
```

```python
import functools
from types import SimpleNamespace

import jax
import jax.numpy as jnp
from jax import lax
from jax.experimental import pallas as pl
from jax.experimental.pallas import tpu as pltpu
from jax.sharding import PartitionSpec as P

EPSILON = 1e-05
WIDE = 16
VMEM_LIMIT = 58 * 1024 * 1024
SMALL_LIMIT = 14 * 1024 * 1024
COST_BYTES = 3.0e6
COST_FLOPS = 1.0e10
F32 = jnp.float32
BF16 = jnp.bfloat16


def dot(left, right):
    return lax.dot_general(left, right, (((1,), (0,)), ((), ())), preferred_element_type=F32)


def dot_cols(left, right):
    return lax.dot_general(left, right, (((1,), (1,)), ((), ())), preferred_element_type=F32)


def dot_rows(left, right):
    return lax.dot_general(left, right, (((0,), (0,)), ((), ())), preferred_element_type=F32)


def valid_rows(rows, side):
    return lax.broadcasted_iota(jnp.int32, (rows, 1), 0) % WIDE < side


def three_shifts(image):
    rows, features = image.shape
    empty = jnp.zeros((WIDE, features), image.dtype)
    padded = jnp.concatenate([empty, image, empty], axis=0)
    total = rows + 2 * WIDE
    return pltpu.roll(padded, 1, 0), padded, pltpu.roll(padded, total - 1, 0)


def convolve(image, taps, side):
    rows = image.shape[0]
    shifted = three_shifts(image)
    summed = None
    for i in range(3):
        for j in range(3):
            term = shifted[j][WIDE * i : WIDE * i + rows] * taps[3 * i + j : 3 * i + j + 1]
            summed = term if summed is None else summed + term
    return jnp.where(valid_rows(rows, side), summed, 0.0)


def to_all(message_ref, row, values):
    devices = message_ref.shape[0]
    message_ref[:, row, 0 : values.shape[1]] = jnp.broadcast_to(values, (devices, values.shape[1]))


def local_moments(conv_ref, moments_ref, images, side):
    rows = side * WIDE
    count = images * side * side
    total = None
    for n in range(images):
        part = jnp.sum(conv_ref[n * rows : (n + 1) * rows, :], axis=0, keepdims=True)
        total = part if total is None else total + part
    mean = total / count
    squares = None
    for n in range(images):
        deviate = jnp.where(
            valid_rows(rows, side), conv_ref[n * rows : (n + 1) * rows, :] - mean, 0.0
        )
        part = jnp.sum(deviate * deviate, axis=0, keepdims=True)
        squares = part if squares is None else squares + part
    to_all(moments_ref, 0, mean)
    to_all(moments_ref, 1, squares)


def whole_moments(gathered_ref, count):
    devices = gathered_ref.shape[0]
    means = gathered_ref[:, 0, :]
    squares = gathered_ref[:, 1, :]
    center = jnp.sum(means, axis=0, keepdims=True) / devices
    apart = means - center
    spread = (
        jnp.sum(squares, axis=0, keepdims=True)
        + jnp.sum(apart * apart, axis=0, keepdims=True) * count
    ) / (count * devices)
    return center, lax.rsqrt(spread + EPSILON)


def mixing_matrices(mix_w, mix_h, side):
    cells = side * WIDE
    row = lax.broadcasted_iota(jnp.int32, (cells, side), 0)
    col = lax.broadcasted_iota(jnp.int32, (cells, side), 1)
    at_w = (row % WIDE == col).astype(BF16)
    at_h = (row // WIDE == col).astype(BF16)
    out = lax.broadcasted_iota(jnp.int32, (cells, cells), 0)
    inp = lax.broadcasted_iota(jnp.int32, (cells, cells), 1)
    same_h = out // WIDE == inp // WIDE
    same_w = (out % WIDE == inp % WIDE) & (out % WIDE < side)

    def spread(picks, mix, keep, flip):
        left = (dot_cols if flip else dot)(picks, mix).astype(BF16)
        return jnp.where(keep, dot_cols(left, picks), 0.0).astype(BF16)

    forward = jnp.concatenate(
        [spread(at_w, mix_w, same_h, False), spread(at_h, mix_h, same_w, False)], axis=0
    )
    backward = jnp.concatenate(
        [spread(at_w, mix_w, same_h, True), spread(at_h, mix_h, same_w, True)], axis=1
    )
    return forward, backward


def by_image(maps_ref, all_ref):
    side, _, held, features = maps_ref.shape
    empty = jnp.zeros((WIDE - side, held, features), F32)
    for h in range(side):
        lines = jnp.concatenate([maps_ref[h], empty], axis=0)
        all_ref[:, h * WIDE : (h + 1) * WIDE, :] = jnp.swapaxes(lines, 0, 1)


def unpack_weights(tmp, unite_ref, up_ref, down_ref):
    packed_ref = tmp.packed
    shards, height, _ = packed_ref.shape
    part = height // 3
    features = unite_ref.shape[1]
    ups, downs, unites = [], [], []
    for s in range(shards):
        piece = packed_ref[s].astype(F32)
        ups.append(piece[:part])
        downs.append(piece[part : 2 * part])
        for q in range(3):
            unites.append(piece[2 * part :, q * features : (q + 1) * features])
    up_ref[...] = jnp.concatenate(ups, axis=0).astype(BF16)
    down_ref[...] = jnp.concatenate(downs, axis=0).astype(BF16)
    unite_ref[...] = jnp.concatenate(unites, axis=0).astype(BF16)


def pack_grads(unite, up, down, pieces_of, dp):
    features = up.shape[0]
    part = features // dp
    for s in range(dp):
        columns = [
            unite[(3 * s + q) * part : (3 * s + q + 1) * part] for q in range(3)
        ]
        filler = jnp.zeros((part, up.shape[1] - 3 * features), F32)
        piece = jnp.concatenate(
            [
                up[s * part : (s + 1) * part],
                down[s * part : (s + 1) * part],
                jnp.concatenate(columns + [filler], axis=1),
            ],
            axis=0,
        )
        pieces_of(s, piece.astype(BF16))


def pack_image_rows(values, side):
    lines = [values[r : r + side] for r in range(0, values.shape[0], WIDE)]
    half = len(lines) // 2
    return jnp.concatenate(
        [jnp.concatenate(lines[:half], axis=0), jnp.concatenate(lines[half:], axis=0)], axis=1
    )


def hidden_bias(up_bias_ref, layer, place_ref):
    groups = up_bias_ref.shape[1]
    blocks = [up_bias_ref[layer, pl.ds(place_ref[0] ^ j, 1), :] for j in range(groups)]
    return jnp.concatenate(blocks, axis=1)


def mix_image(conv, center, inv_std, bn_gain, bn_bias, mixing, side):
    rows = conv.shape[0]
    ahat = (conv - center) * inv_std
    branch = jnp.where(valid_rows(rows, side), ahat * bn_gain + bn_bias, 0.0).astype(BF16)
    along = dot(mixing, branch).astype(BF16)
    return branch, along[:rows], along[rows:]


def mlp_image(stream, joined, unite_ref, norm_gain, up_ref, up_bias, down_ref, side):
    rows, features = stream.shape
    united = dot(joined, unite_ref[...])
    resid = stream + united
    mid = jnp.sum(resid, axis=-1, keepdims=True) / features
    deviate = resid - mid
    spread = jnp.sum(deviate * deviate, axis=-1, keepdims=True) / features
    inv_norm = lax.rsqrt(spread + EPSILON)
    uhat = deviate * inv_norm
    normal = (uhat * norm_gain).astype(BF16)
    pre = dot(normal, up_ref[...]) + up_bias
    below = 0.5 + 0.5 * lax.erf(pre * (0.5**0.5))
    slope = below + pre * (jnp.exp(-0.5 * pre * pre) * 0.3989422804014327)
    hidden = (pre * below).astype(BF16)
    mlp = jnp.where(valid_rows(rows, side), dot_cols(hidden, down_ref[...]), 0.0)
    result = resid + mlp
    squares = jnp.concatenate(
        [jnp.sum(v * v, axis=0, keepdims=True) for v in (united, mlp, result)], axis=0
    )
    return SimpleNamespace(
        uhat=uhat,
        inv_norm=inv_norm,
        slope=slope,
        hidden=hidden,
        result=result,
        squares=squares,
    )


def backward_image(
    grad, ahat, branch, uhat, inv_norm, slope, mixing_back, unite_ref, norm_gain, up_ref, down_ref
):
    rows, features = grad.shape
    grad_low = grad.astype(BF16)
    gh = dot(grad_low, down_ref[...])
    gpre = (gh * slope).astype(BF16)
    bias = jnp.sum(gpre.astype(F32), axis=0, keepdims=True)
    gn = dot_cols(gpre, up_ref[...])
    gain = jnp.sum(gn * uhat, axis=0, keepdims=True)
    q = gn * norm_gain
    mean_q = jnp.sum(q, axis=-1, keepdims=True) / features
    mean_qu = jnp.sum(q * uhat, axis=-1, keepdims=True) / features
    gu = grad + inv_norm * (q - mean_q - uhat * mean_qu)
    gc = gu.astype(BF16)
    gj = dot_cols(gc, unite_ref[...])
    both = jnp.concatenate([gj[:, features : 2 * features], gj[:, 2 * features :]], axis=0).astype(BF16)
    gb = gj[:, :features] + dot(mixing_back, both)
    cross = dot_cols(both, branch)
    return SimpleNamespace(
        grad_low=grad_low,
        gpre=gpre,
        bias=bias,
        gain=gain,
        gu=gu,
        gc=gc,
        gb=gb,
        cross=cross,
        offset=jnp.sum(gb, axis=0, keepdims=True),
        scale=jnp.sum(gb * ahat, axis=0, keepdims=True),
    )


def mixing_grads(cross, side):
    cells = side * WIDE
    width = None
    for h in range(side):
        at = slice(h * WIDE, (h + 1) * WIDE)
        width = add_up(width, cross[at, at])
    out = lax.broadcasted_iota(jnp.int32, (cells, cells), 0)
    inp = lax.broadcasted_iota(jnp.int32, (cells, cells), 1)
    kept = jnp.where(out % WIDE == inp % WIDE, cross[cells:], 0.0)
    lines = jnp.concatenate(
        [jnp.sum(kept[v * WIDE : (v + 1) * WIDE], axis=0, keepdims=True) for v in range(side)]
        + [jnp.zeros((WIDE - side, cells), F32)],
        axis=0,
    )
    row = lax.broadcasted_iota(jnp.int32, (cells, WIDE), 0)
    col = lax.broadcasted_iota(jnp.int32, (cells, WIDE), 1)
    height = lax.dot_general(
        lines,
        (row // WIDE == col).astype(F32),
        (((1,), (0,)), ((), ())),
        precision=lax.Precision.HIGHEST,
        preferred_element_type=F32,
    )
    return width, height


def tap_sums(values, stream):
    rows = values.shape[0]
    shifted = three_shifts(stream)
    return jnp.concatenate(
        [
            jnp.sum(values * shifted[j][WIDE * i : WIDE * i + rows], axis=0, keepdims=True)
            for i in range(3)
            for j in range(3)
        ],
        axis=0,
    )


def conv_back_image(gb, ahat, gu, factor, offset_mean, scale_mean, taps, side):
    rows = gb.shape[0]
    valid = valid_rows(rows, side)
    ga = jnp.where(valid, factor * (gb - offset_mean - ahat * scale_mean), 0.0)
    turned = three_shifts(ga)
    summed = gu
    for i in range(3):
        for j in range(3):
            summed = (
                summed
                + turned[2 - j][WIDE * (2 - i) : WIDE * (2 - i) + rows]
                * taps[3 * i + j : 3 * i + j + 1]
            )
    return jnp.where(valid, summed, 0.0), ga


def add_up(total, part):
    return part if total is None else total + part


SMALL_ROWS, SMALL_WIDE = 60, 384
NORM_ROW, SQUARES_ROW, BIAS_ROW, TAPS_ROW = (27, 48), (28, 49), (31, 52), 39
KEPT = ("uhat", "inv_norm", "slope", "hidden")


def stage_forward(layer, ins, weights, weights_of, kept, on_result, *, images, side):
    rows = side * WIDE
    at = [slice(n * rows, (n + 1) * rows) for n in range(images)]
    center, inv_std = whole_moments(ins.moments, images * side * side)
    for n in range(images):
        branch, along_w, along_h = mix_image(
            ins.conv[at[n], :],
            center,
            inv_std,
            ins.batch_gain[layer : layer + 1, :],
            ins.batch_bias[layer : layer + 1, :],
            ins.mixing[...],
            side,
        )
        features = branch.shape[1]
        kept.joined[at[n], 0:features] = branch
        kept.joined[at[n], features : 2 * features] = along_w
        kept.joined[at[n], 2 * features : 3 * features] = along_h
    weights_of()
    up_bias = hidden_bias(ins.up_bias, layer, ins.place)
    squares = None
    for n in range(images):
        found = mlp_image(
            ins.stream[at[n], :],
            kept.joined[at[n], :],
            weights[0],
            ins.layer_gain[layer : layer + 1, :],
            weights[1],
            up_bias,
            weights[2],
            side,
        )
        for name in KEPT:
            to = getattr(kept, name)
            to[at[n], :] = getattr(found, name).astype(to.dtype)
        squares = add_up(squares, found.squares)
        on_result(n, found.result)
    return center, inv_std, squares


def stage_backward(
    layer, place, grad_of, center, inv_std, conv, par, weights, kept, gb, gu, small, rows_ref, pieces_of,
    dp, *, images, side,
):
    rows = side * WIDE
    features = gb.shape[1]
    grad_low, gpre, gc = rows_ref
    offset = scale = gain = bias = cross = None
    for n in range(images):
        at = slice(n * rows, (n + 1) * rows)
        found = backward_image(
            grad_of(n),
            (conv[at, :] - center) * inv_std,
            kept.joined[at, 0:features],
            kept.uhat[at, :],
            kept.inv_norm[at, :],
            kept.slope[at, :].astype(F32),
            par.mixing_back[...],
            weights[0],
            par.layer_gain[layer : layer + 1, :],
            weights[1],
            weights[2],
        )
        grad_low[at, :] = found.grad_low
        gpre[at, :] = found.gpre
        gc[at, :] = found.gc
        gb[at, :] = found.gb.astype(gb.dtype)
        gu[at, :] = found.gu.astype(gu.dtype)
        offset = add_up(offset, found.offset)
        scale = add_up(scale, found.scale)
        gain = add_up(gain, found.gain)
        bias = add_up(bias, found.bias)
        cross = add_up(cross, found.cross)
    small[NORM_ROW[layer] : NORM_ROW[layer] + 1, 0:features] = gain
    groups = par.up_bias.shape[1]
    width = bias.shape[1] // groups
    for j in range(groups):
        small[pl.ds(BIAS_ROW[layer] + (place[0] ^ j), 1), 0:width] = bias[:, j * width : (j + 1) * width]
    wide, tall = mixing_grads(cross, side)
    mixes = slice(layer * WIDE, (layer + 1) * WIDE)
    small[mixes, features : features + WIDE] = wide
    small[mixes, features + WIDE : features + 2 * WIDE] = tall
    unite_grad = dot_rows(kept.joined[...], gc[...])
    normal = (kept.uhat[...] * par.layer_gain[layer : layer + 1, :]).astype(BF16)
    up_grad = dot_rows(normal, gpre[...])
    down_grad = dot_rows(grad_low[...], kept.hidden[...])
    pack_grads(unite_grad, up_grad, down_grad, pieces_of, dp)
    return offset, scale


def first_body(ins, outs, tmp, *, images, side):
    place, taps = ins.place, ins.taps
    own, conv, moments = outs.own, outs.conv, outs.moments
    every = tmp.every
    rows = side * WIDE
    by_image(ins.stream, every)
    for n in range(images):
        own[n * rows : (n + 1) * rows, :] = every[place[0] * images + n]
    for n in range(images):
        at = slice(n * rows, (n + 1) * rows)
        conv[at, :] = convolve(own[at, :], taps[:, 0, :], side)
    local_moments(conv, moments, images, side)


def other_body(ins, outs, tmp, *, images, side):
    rows = side * WIDE
    by_image(ins.cotangent, tmp.every)
    for n in range(images):
        outs.cotangent[n * rows : (n + 1) * rows, :] = tmp.every[ins.place[0] * images + n]
    _, groups, width = outs.up_bias.shape
    for j in range(groups):
        outs.up_bias[:, j, :] = ins.up_bias[:, j * width : (j + 1) * width]
    mixes = ins.mix_w[...].astype(F32), ins.mix_h[...].astype(F32)
    for layer in range(ins.mix_w.shape[1]):
        outs.mixing[layer][...], outs.mixing_back[layer][...] = mixing_matrices(
            *(mix[:, layer, :].astype(BF16) for mix in mixes), side
        )


def middle_body(ins, outs, tmp, *, images, side):
    rows = side * WIDE
    weights = tmp.unite, tmp.up, tmp.down
    results = []

    def weights_of():
        unpack_weights(tmp, *weights)

    center, inv_std, squares = stage_forward(
        0, ins, weights, weights_of, outs, lambda n, result: results.append(result), images=images, side=side
    )
    outs.stats[0:1, :] = center
    outs.stats[1:2, :] = inv_std
    outs.squares[...] = squares
    for n, result in enumerate(results):
        at = slice(n * rows, (n + 1) * rows)
        outs.stream1[at, :] = result
        outs.conv1[at, :] = convolve(result, ins.taps[:, 1, :], side)
    local_moments(outs.conv1, outs.moments1, images, side)


def last_body(ins, outs, tmp, *, images, side, dp):
    weights = tmp.unite, tmp.up, tmp.down
    results = []

    def weights_of():
        unpack_weights(tmp, *weights)

    center, inv_std, squares = stage_forward(
        1, ins, weights, weights_of, tmp, lambda n, result: results.append(result), images=images, side=side
    )
    outs.result[...] = pack_image_rows(jnp.concatenate(results, axis=0), side).astype(BF16)
    outs.stats[0:1, :] = center
    outs.stats[1:2, :] = inv_std
    outs.small[...] = jnp.zeros_like(outs.small)
    pieces_of = sort_pieces(ins.place[1], outs)
    offset, scale = stage_backward(
        1, ins.place, lambda n: ins.cotangent[n * side * WIDE : (n + 1) * side * WIDE, :], center, inv_std,
        ins.conv, ins, weights, tmp, outs.gb, outs.gu, outs.small,
        (tmp.grad_low, tmp.gpre, tmp.gc), pieces_of, dp, images=images, side=side,
    )
    features = squares.shape[1]
    outs.small[SQUARES_ROW[1] : SQUARES_ROW[1] + 3, 0:features] = squares
    to_all(outs.sums, 0, offset)
    to_all(outs.sums, 1, scale)


def conv_back(layer, sums, gb, gu, conv, stats, par, totals, *, images, side):
    rows = side * WIDE
    features = gb.shape[1]
    cells = images * side * side * sums.shape[0]
    offset = jnp.sum(sums[:, 0, 0:features], axis=0, keepdims=True)
    scale = jnp.sum(sums[:, 1, 0:features], axis=0, keepdims=True)
    totals[0:1, :] = offset
    totals[1:2, :] = scale
    center, inv_std = stats[0:1, :], stats[1:2, :]
    factor = par.batch_gain[layer : layer + 1, :] * inv_std
    found = []
    for n in range(images):
        at = slice(n * rows, (n + 1) * rows)
        found.append(
            conv_back_image(
                gb[at, :].astype(F32),
                (conv[at, :] - center) * inv_std,
                gu[at, :].astype(F32),
                factor,
                offset / cells,
                scale / cells,
                par.taps[:, layer, :],
                side,
            )
        )
    return found


def taps_body(ins, outs, tmp, *, images, side):
    rows = side * WIDE
    center, inv_std = ins.stats[0:1, :], ins.stats[1:2, :]
    plain = scaled = None
    for n in range(images):
        at = slice(n * rows, (n + 1) * rows)
        stream = ins.stream[at, :]
        valid = valid_rows(rows, side)
        ones = jnp.where(valid, jnp.ones_like(stream), 0.0)
        ahat = jnp.where(valid, (ins.conv[at, :] - center) * inv_std, 0.0)
        plain = add_up(plain, tap_sums(ones, stream))
        scaled = add_up(scaled, tap_sums(ahat, stream))
    outs.plain[...] = plain
    outs.scaled[...] = scaled


def sort_pieces(mine, outs):
    def put(s, piece):
        same = ((mine ^ s) & 1) == 0

        @pl.when(same)
        def _():
            outs.keep[s >> 1] = piece

        @pl.when(jnp.logical_not(same))
        def _():
            outs.give[s >> 1] = piece

    return put


def between_body(ins, outs, tmp, *, images, side, dp):
    weights = tmp.unite, tmp.up, tmp.down
    unpack_weights(tmp, *weights)
    rows = side * WIDE
    features = ins.gb1.shape[1]
    small, sums = tmp.small, outs.sums
    small[...] = ins.small[...]
    grads, kernel = [], None
    found = conv_back(
        1, ins.sums1, ins.gb1, ins.gu1, ins.conv1, ins.stats1, ins, outs.totals1, images=images, side=side
    )
    for n, (grad, ga) in enumerate(found):
        grads.append(grad)
        kernel = add_up(kernel, tap_sums(ga, ins.stream1[n * rows : (n + 1) * rows, :]))
    small[TAPS_ROW : TAPS_ROW + 9, 0:features] = kernel
    stats = ins.stats0
    offset, scale = stage_backward(
        0, ins.place, lambda n: grads[n], stats[0:1, :], stats[1:2, :], ins.conv0, ins, weights, ins,
        tmp.gb, tmp.gu, small, (tmp.grad_low, tmp.gpre, tmp.gc), sort_pieces(ins.place[1], outs), dp,
        images=images, side=side,
    )
    kernel = None
    for n in range(images):
        at = slice(n * rows, (n + 1) * rows)
        kernel = add_up(kernel, tap_sums(tmp.gb[at, :], ins.stream0[at, :]))
    for k, values in enumerate((kernel, ins.plain[...], ins.scaled[...])):
        small[9 * k : 9 * k + 9, 0:features] = values
    small[SQUARES_ROW[0] : SQUARES_ROW[0] + 3, 0:features] = ins.squares0[...]
    cells = images * side * side
    center, inv_std = stats[0:1, :], stats[1:2, :]
    grads = []
    for n in range(images):
        at = slice(n * rows, (n + 1) * rows)
        ahat = (ins.conv0[at, :] - center) * inv_std
        factor = ins.batch_gain[0:1, :] * inv_std
        grad, _ = conv_back_image(
            tmp.gb[at, :], ahat, tmp.gu[at, :], factor, offset / cells, scale / cells, ins.taps[:, 0, :], side
        )
        grads.append(grad)
    outs.grad[...] = pack_image_rows(jnp.concatenate(grads, axis=0), side).astype(BF16)
    to_all(sums, 0, offset)
    to_all(sums, 1, scale)
    devices, height, _ = sums.shape
    for g in range(height - 2):
        held = min(devices, SMALL_ROWS - g * devices)
        sums[0:held, 2 + g, :] = small[g * devices : g * devices + held, :]
        if held < devices:
            sums[held:, 2 + g, :] = jnp.zeros((devices - held, SMALL_WIDE), F32)


def final_body(ins, outs, tmp, *, images, side):
    held, rows, features = tmp.every.shape
    sums = ins.sums0
    cells = images * side * side
    devices = sums.shape[0]
    group = held // images
    offset = jnp.sum(sums[:, 0, 0:features], axis=0, keepdims=True)
    scale = jnp.sum(sums[:, 1, 0:features], axis=0, keepdims=True)
    for row, total in enumerate((offset, scale)):
        to = (outs.offset_grad, outs.scale_grad)[row]
        to[0:1, :] = total
        to[1:2, :] = ins.totals1[row : row + 1, :]
    center, inv_std = ins.stats0[0:1, :], ins.stats0[1:2, :]
    factor = ins.batch_gain[0:1, :] * inv_std
    first = ins.place[1] * group

    def apart(row, total):
        own = [sums[first + p, row : row + 1, 0:features] for p in range(group)]
        own = jnp.concatenate([value for value in own for _ in range(images)], axis=0)
        return factor * (total / (cells * devices) - own / cells)

    shift, slant = apart(0, offset), apart(1, scale)
    put_images(ins.place[0], ins.parts, tmp.every, images, side)
    padded, fields = tmp.padded, tmp.fields
    for ref in (padded, fields):
        edge = jnp.zeros((1,) + ref.shape[1:], F32)
        ref[0:1] = edge
        ref[side + 1 : side + 2] = edge
        edge = jnp.zeros((side, 1) + ref.shape[2:], F32)
        ref[1 : side + 1, 0:1] = edge
        ref[1 : side + 1, side + 1 : side + 2] = edge
    padded[1 : side + 1, 1 : side + 1] = ins.stream[...]
    taps = ins.taps[:, 0, :]
    for h in range(side):
        conv = None
        for i in range(3):
            for j in range(3):
                term = padded[h + i, j : j + side] * taps[3 * i + j : 3 * i + j + 1]
                conv = add_up(conv, term)
        fields[h + 1, 1 : side + 1] = shift + (conv - center) * inv_std * slant
    for h in range(side):
        lines = jnp.swapaxes(tmp.every[:, h * WIDE : (h + 1) * WIDE, :], 0, 1)[:side]
        for i in range(3):
            for j in range(3):
                lines = lines - fields[h + 2 - i, 2 - j : 2 - j + side] * taps[3 * i + j : 3 * i + j + 1]
        outs.out[h] = lines


def put_images(place, parts, every, images, side):
    features = every.shape[2]
    for j, part in enumerate(parts):
        packed = part[...].astype(F32)
        lines = packed.shape[0] // side
        for half in range(2):
            values = packed[:, half * features : (half + 1) * features]
            for k in range(lines):
                n, h = divmod(half * lines + k, side)
                every[(place ^ j) * images + n, h * WIDE : h * WIDE + side, :] = values[
                    k * side : (k + 1) * side
                ]


def gather_body(ins, outs, tmp):
    for g in range(outs.message.shape[1]):
        to_all(outs.message, g, jnp.sum(ins.sums0[:, 2 + g, :], axis=0, keepdims=True))


def spread_body(ins, outs, tmp, *, images, side):
    put_images(ins.place[0], ins.parts, tmp.every, images, side)
    for h in range(side):
        outs.out[h] = jnp.swapaxes(tmp.every[:, h * WIDE : (h + 1) * WIDE, :], 0, 1)[:side]


def core_body(ins, outs, tmp):
    apart = isinstance(outs.parts, list)
    for k in range(ins.keep.shape[0]):
        at = (ins.place[1] >> 1) ^ k if apart else k
        to = outs.parts[k] if apart else outs.parts.at[k]
        to[...] = (ins.keep[at].astype(F32) + ins.got[at].astype(F32)).astype(BF16)


def chips_body(ins, outs, tmp):
    groups = len(outs.give)
    for layer, parts in enumerate(ins.parts):
        parts = parts if isinstance(parts, list) else [parts.at[k] for k in range(parts.shape[0])]
        total = parts[0][...].astype(F32)
        for other in parts[1:]:
            total = total + other[...].astype(F32)
        part = total.shape[0] // 3
        width = total.shape[1] // groups
        features = outs.give[0].shape[2] - 2 * width
        for j in range(groups):
            block = jnp.concatenate(
                [
                    total[:part, j * width : (j + 1) * width],
                    total[part : 2 * part, j * width : (j + 1) * width],
                    total[2 * part :, :features],
                ],
                axis=1,
            )
            outs.give[j][layer] = block.astype(BF16)


def weights_body(ins, outs, tmp):
    layers = outs.up_grad.shape[0]
    for layer in range(layers):
        terms = [ref[layer].astype(F32) for ref in ins.got]
        while len(terms) > 1:
            terms = [terms[j] + terms[j + 1] for j in range(0, len(terms), 2)]
        total = terms[0]
        width = outs.up_grad.shape[2]
        features = outs.unite_grad.shape[1]
        outs.up_grad[layer] = total[:, :width]
        outs.down_grad[layer] = total[:, width : 2 * width]
        rest = total[:, 2 * width :]
        rows = jnp.concatenate([rest[:, q * features : (q + 1) * features] for q in range(3)], axis=0)
        outs.unite_grad[layer] = rows.T


def small_body(ins, outs, tmp, *, side, cells, entries):
    got = ins.got
    features = outs.gain_grad.shape[1]
    devices, height, _ = got.shape
    values = tmp.values
    for g in range(height):
        values[g * devices : (g + 1) * devices, :] = got[:, g, :]
    factor = ins.batch_gain[0:1, :] * ins.stats0[1:2, :]
    first = factor * (
        values[0:9, 0:features]
        - ins.offset[0:1, :] / cells * values[9:18, 0:features]
        - ins.scale[0:1, :] / cells * values[18:27, 0:features]
    )
    for k in range(9):
        outs.kernel_grad[k, 0:1, :] = first[k : k + 1]
        outs.kernel_grad[k, 1:2, :] = values[TAPS_ROW + k : TAPS_ROW + k + 1, 0:features]
    width = outs.bias_grad.shape[1]
    for layer in range(2):
        outs.gain_grad[layer : layer + 1, :] = values[NORM_ROW[layer] : NORM_ROW[layer] + 1, 0:features]
        outs.bias_grad[layer : layer + 1, :] = values[pl.ds(BIAS_ROW[layer] + ins.place[0], 1), 0:width]
        rows = slice(layer * WIDE, layer * WIDE + side)
        outs.width_grad[:, layer, :] = values[rows, features : features + side]
        outs.height_grad[:, layer, :] = values[rows, features + WIDE : features + WIDE + side]
        squares = values[SQUARES_ROW[layer] : SQUARES_ROW[layer] + 3, 0:features]
        outs.stream_rms[:, layer : layer + 1] = jnp.sqrt(
            jnp.sum(squares, axis=1, keepdims=True) / entries
        )


def call(body, ins, outs, scratch=None, shards=(), micros=0, vmem=VMEM_LIMIT, **static):
    ins = dict(ins, shards=list(shards))
    operands, in_tree = jax.tree.flatten(ins)
    shapes, out_tree = jax.tree.flatten(
        {name: jax.tree.map(lambda shape: jax.ShapeDtypeStruct(*shape), outs[name], is_leaf=is_shape) for name in outs}
    )
    scratch = dict(scratch or {})
    if shards:
        scratch["packed"] = (len(shards),) + shards[0].shape, shards[0].dtype
    tmp_names = list(scratch)

    def kernel(*refs):
        cut = len(operands), len(operands) + len(shapes)
        given = SimpleNamespace(**jax.tree.unflatten(in_tree, refs[: cut[0]]))
        results = SimpleNamespace(**jax.tree.unflatten(out_tree, refs[cut[0] : cut[1]]))
        tmp = SimpleNamespace(**dict(zip(tmp_names, refs[cut[1] :])))
        for k, shard in enumerate(given.shards):
            tmp.packed[given.place[1] ^ k] = shard[...]
        body(given, results, tmp, **static)

    def space(name):
        return pl.BlockSpec(memory_space=pltpu.SMEM if name == "place" else pltpu.VMEM)

    found = pl.pallas_call(
        kernel,
        out_shape=shapes,
        in_specs=jax.tree.leaves({name: jax.tree.map(lambda _: space(name), ins[name]) for name in ins}),
        out_specs=[space("")] * len(shapes),
        scratch_shapes=[pltpu.VMEM(*scratch[name]) for name in tmp_names],
        compiler_params=pltpu.CompilerParams(vmem_limit_bytes=vmem),
        cost_estimate=pl.CostEstimate(
            flops=int(micros * COST_FLOPS), transcendentals=0, bytes_accessed=int(micros * COST_BYTES)
        ),
    )(*operands)
    return SimpleNamespace(**jax.tree.unflatten(out_tree, found))


def is_shape(value):
    return isinstance(value, tuple)


def swap(values, axis, mask):
    return lax.ppermute(values, axis, [(i, i ^ mask) for i in range(lax.axis_size(axis))])


def after(values, *others):
    return lax.optimization_barrier((values, others))[0]


def per_device(
    inputs,
    conv_weight,
    batch_gain,
    batch_bias,
    mix_width,
    mix_height,
    unite_weight,
    layer_gain,
    up_weight,
    up_bias,
    down_weight,
    cotangent,
):
    held, side, _, features = inputs.shape
    layers = conv_weight.shape[0]
    dp, mp = lax.axis_size("dp"), lax.axis_size("mp")
    devices = dp * mp
    images = held // mp
    cells = side * WIDE
    rows = images * cells
    units = up_bias.shape[1]
    part = features // dp
    both = ("dp", "mp")
    sizes = dict(images=images, side=side)
    place = jnp.stack([lax.axis_index("mp"), lax.axis_index("dp")]).astype(jnp.int32)

    def group_parts(values):
        if isinstance(values, (list, tuple)):
            return [swap(value, "mp", j) if j else value for j, value in enumerate(values)]
        parts = [values]
        for j in range(1, mp):
            step = j & -j
            parts.append(swap(parts[j ^ step], "mp", step))
        return parts

    def share(blocks):
        return lax.all_to_all(blocks, both, 0, 0, tiled=False)

    maps = jnp.transpose(inputs, (1, 2, 0, 3))
    cotangent_maps = jnp.transpose(cotangent, (1, 2, 0, 3))
    taps = jnp.transpose(conv_weight, (1, 0, 2))
    mix_w, mix_h = (jnp.transpose(mix, (1, 0, 2)) for mix in (mix_width, mix_height))
    shared = (devices, 2, features)
    thirds = unite_weight.reshape(layers, 3, part, features)
    thirds = jnp.concatenate([thirds[:, q] for q in range(3)], axis=2)
    thirds = jnp.pad(thirds, ((0, 0), (0, 0), (0, units - 3 * features)))

    def widen(wide, step):
        return jnp.concatenate([wide, swap(wide, "mp", step)], axis=1)

    def over_dp(layer, wide, wait_chips, wait_core):
        piece = after(jnp.concatenate([wide, thirds[layer]], axis=0), *wait_chips)
        shards = [piece] + [swap(piece, "dp", 2 * k) for k in range(1, dp // 2)]
        mates = [swap(after(shard, *wait_core), "dp", 1) for shard in shards]
        return [shard for pair in zip(shards, mates) for shard in pair]

    wide = jnp.concatenate([up_weight[0], down_weight[0]], axis=0)
    wide = near = widen(wide, 1) if mp > 1 else wide
    step = 2
    while step < mp:
        wide = widen(wide, step)
        step *= 2
    found = call(
        first_body,
        dict(place=after(place, near), stream=maps, taps=taps),
        dict(own=((rows, features), F32), conv=((rows, features), F32), moments=(shared, F32)),
        dict(every=((held, cells, features), F32)),
        micros=4,
        **sizes,
    )
    moments0 = share(after(found.moments, wide))
    other = call(
        other_body,
        dict(place=place, cotangent=cotangent_maps, mix_w=mix_w, mix_h=mix_h, up_bias=up_bias),
        dict(
            cotangent=((rows, features), F32),
            up_bias=((layers, mp, units // mp), F32),
            mixing=[((2 * cells, cells), BF16)] * layers,
            mixing_back=[((cells, 2 * cells), BF16)] * layers,
        ),
        dict(every=((held, cells, features), F32)),
        micros=3,
        **sizes,
    )

    packed = [over_dp(0, wide, (found.moments,), (moments0, other.mixing[0]))]
    wide = after(jnp.concatenate([up_weight[1], down_weight[1]], axis=0), wide)
    step = 1
    while step < mp:
        wide = widen(wide, step)
        step *= 2
    wide1 = wide

    own, conv0 = found.own, found.conv
    par = dict(
        place=place,
        taps=taps,
        batch_gain=batch_gain,
        batch_bias=batch_bias,
        layer_gain=layer_gain,
        up_bias=other.up_bias,
    )
    kept = dict(
        joined=((rows, 3 * features), BF16),
        uhat=((rows, features), F32),
        inv_norm=((rows, 1), F32),
        slope=((rows, units), BF16),
        hidden=((rows, units), BF16),
    )
    weight_tmp = dict(
        unite=((3 * features, features), BF16),
        up=((features, units), BF16),
        down=((features, units), BF16),
    )
    back_tmp = dict(
        grad_low=((rows, features), BF16), gpre=((rows, units), BF16), gc=((rows, features), BF16)
    )
    back_outs = dict(gb=((rows, features), F32), gu=((rows, features), F32))
    stats = ((2, features), F32)
    pieces = [((dp // 2, 3 * part, units), BF16)] * 2
    piece = ((3 * part, units), BF16)

    def over_core(values, apart=False):
        return call(
            core_body,
            dict(place=place, keep=values.keep, got=swap(values.give, "dp", 1)),
            dict(parts=[piece] * (dp // 2) if apart else pieces[0]),
            vmem=SMALL_LIMIT,
        ).parts

    def from_chips(parts):
        if isinstance(parts, list):
            return [swap(values, "dp", 2 * k) if k else values for k, values in enumerate(parts)]
        groups = [[2 * q + c for q in range(dp // 2)] for c in range(2)]
        return lax.all_to_all(parts, "dp", 0, 0, axis_index_groups=groups, tiled=False)

    mid = call(
        middle_body,
        dict(
            par,
            moments=moments0,
            conv=conv0,
            stream=own,
            mixing=other.mixing[0],
        ),
        dict(
            kept,
            stream1=((rows, features), F32),
            conv1=((rows, features), F32),
            moments1=(shared, F32),
            stats=stats,
            squares=((3, features), F32),
        ),
        weight_tmp,
        packed[0],
        micros=6,
        **sizes,
    )
    packed.append(over_dp(1, wide1, packed[0][::2], (mid.moments1,)))
    under = call(
        taps_body,
        dict(stream=own, conv=conv0, stats=mid.stats),
        dict(plain=((9, features), F32), scaled=((9, features), F32)),
        micros=2,
        **sizes,
    )
    last = call(
        last_body,
        dict(
            par,
            moments=after(share(mid.moments1), under.plain),
            conv=mid.conv1,
            stream=mid.stream1,
            mixing=other.mixing[1],
            mixing_back=other.mixing_back[1],
            cotangent=other.cotangent,
        ),
        dict(
            gb=((rows, features), BF16),
            gu=((rows, features), BF16),
            result=((images * side * side // 2, 2 * features), BF16),
            stats=stats,
            small=((SMALL_ROWS, SMALL_WIDE), F32),
            sums=(shared, F32),
            keep=pieces[0],
            give=pieces[1],
        ),
        dict(
            dict(kept, slope=((rows, units), F32)),
            **weight_tmp,
            **back_tmp,
        ),
        packed[1],
        micros=10,
        dp=dp,
        **sizes,
    )
    summed1 = over_core(last)
    groups = -(-SMALL_ROWS // devices)
    between = call(
        between_body,
        {
            **par,
            **{name: getattr(mid, name) for name in kept},
            **dict(
                sums1=after(share(last.sums), summed1),
                gb1=last.gb,
                gu1=last.gu,
                conv1=mid.conv1,
                stream1=mid.stream1,
                stats1=last.stats,
                small=last.small,
                stream0=own,
                plain=under.plain,
                scaled=under.scaled,
                conv0=conv0,
                stats0=mid.stats,
                squares0=mid.squares,
                mixing_back=other.mixing_back[0],
            ),
        },
        dict(
            grad=((images * side * side // 2, 2 * features), BF16),
            totals1=stats,
            sums=((devices, 2 + groups, SMALL_WIDE), F32),
            keep=pieces[0],
            give=pieces[1],
        ),
        dict(
            back_tmp,
            **back_outs,
            **weight_tmp,
            small=((SMALL_ROWS, SMALL_WIDE), F32),
        ),
        packed[0],
        micros=10,
        dp=dp,
        **sizes,
    )
    result_parts = [last.result] + [swap(last.result, "mp", 1 << k) for k in range((mp - 1).bit_length())]
    parts1 = from_chips(summed1)
    grad, sums0, give, parts1, near = lax.optimization_barrier(
        (between.grad, between.sums, between.give, parts1, result_parts[1:])
    )
    result_parts = [last.result]
    for j in range(1, mp):
        step = j & -j
        result_parts.append(near[j.bit_length() - 1] if j == step else swap(result_parts[j ^ step], "mp", step))
    sums0 = share(sums0)
    chunk = call(
        gather_body, dict(sums0=sums0), dict(message=((devices, groups, SMALL_WIDE), F32)), vmem=SMALL_LIMIT
    )
    shared_small = share(chunk.message)
    summed0 = over_core(SimpleNamespace(keep=between.keep, give=give), True)
    summed0 = after(summed0, result_parts)
    grad_parts = group_parts(after(grad, summed0))
    cut = call(
        chips_body,
        dict(parts=[from_chips(summed0), parts1]),
        dict(give=[((layers, part, 2 * (units // mp) + 3 * features), BF16)] * mp),
        vmem=SMALL_LIMIT,
    ).give
    grads = call(
        weights_body,
        dict(got=group_parts(after(cut, grad_parts, shared_small))),
        dict(
            up_grad=((layers, part, units // mp), F32),
            down_grad=((layers, part, units // mp), F32),
            unite_grad=((layers, features, 3 * part), F32),
        ),
        vmem=SMALL_LIMIT,
    )
    whole_maps = ((side, side, held, features), F32)
    output = call(
        spread_body,
        dict(place=place, parts=result_parts),
        dict(out=whole_maps),
        dict(every=((held, cells, features), F32)),
        **sizes,
    ).out
    padded = ((side + 2, side + 2, held, features), F32)
    end = call(
        final_body,
        dict(
            place=place,
            parts=grad_parts,
            stream=maps,
            sums0=sums0,
            totals1=between.totals1,
            stats0=mid.stats,
            batch_gain=batch_gain,
            taps=taps,
        ),
        dict(out=whole_maps, offset_grad=stats, scale_grad=stats),
        dict(every=((held, cells, features), F32), padded=padded, fields=padded),
        **sizes,
    )
    outputs = [jnp.transpose(out, (2, 0, 1, 3)) for out in (output, end.out)]
    small = call(
        small_body,
        dict(
            place=place,
            got=shared_small,
            batch_gain=batch_gain,
            stats0=mid.stats,
            offset=end.offset_grad,
            scale=end.scale_grad,
        ),
        dict(
            kernel_grad=((9, layers, features), F32),
            gain_grad=((layers, features), F32),
            bias_grad=((layers, units // mp), F32),
            width_grad=((side, layers, side), F32),
            height_grad=((side, layers, side), F32),
            stream_rms=((3, layers), F32),
        ),
        dict(values=((groups * devices, SMALL_WIDE), F32)),
        vmem=SMALL_LIMIT,
        side=side,
        cells=images * side * side * devices,
        entries=held * side * side * features * dp,
    )
    return (
        *outputs,
        jnp.transpose(small.kernel_grad, (1, 0, 2)),
        end.scale_grad,
        end.offset_grad,
        jnp.transpose(small.width_grad, (1, 0, 2)),
        jnp.transpose(small.height_grad, (1, 0, 2)),
        jnp.transpose(grads.unite_grad, (0, 2, 1)),
        small.gain_grad,
        grads.up_grad,
        small.bias_grad,
        grads.down_grad,
        small.stream_rms.T,
    )


def solution(mesh):
    in_specs = (
        P("dp", None, None, None),
        P(),
        P(),
        P(),
        P(),
        P(),
        P(None, "dp", None),
        P(),
        P(None, "dp", "mp"),
        P(),
        P(None, "dp", "mp"),
        P("dp", None, None, None),
    )
    out_specs = (
        P("dp", None, None, None),
        P("dp", None, None, None),
        P(),
        P(),
        P(),
        P(),
        P(),
        P(None, "dp", None),
        P(),
        P(None, "dp", "mp"),
        P(None, "mp"),
        P(None, "dp", "mp"),
        P(),
    )
    return jax.shard_map(
        per_device, mesh=mesh, in_specs=in_specs, out_specs=out_specs, check_vma=False
    )
```

```python
import functools
from types import SimpleNamespace

import jax
import jax.numpy as jnp
from jax import lax
from jax.experimental import pallas as pl
from jax.experimental.pallas import tpu as pltpu
from jax.sharding import PartitionSpec as P

EPSILON = 1e-05
WIDE = 16
VMEM_LIMIT = 58 * 1024 * 1024
SMALL_LIMIT = 14 * 1024 * 1024
COST_BYTES = 3.0e6
COST_FLOPS = 1.0e10
F32 = jnp.float32
BF16 = jnp.bfloat16


def dot(left, right):
    return lax.dot_general(left, right, (((1,), (0,)), ((), ())), preferred_element_type=F32)


def dot_cols(left, right):
    return lax.dot_general(left, right, (((1,), (1,)), ((), ())), preferred_element_type=F32)


def dot_rows(left, right):
    return lax.dot_general(left, right, (((0,), (0,)), ((), ())), preferred_element_type=F32)


def valid_rows(rows, side):
    return lax.broadcasted_iota(jnp.int32, (rows, 1), 0) % WIDE < side


def three_shifts(image):
    rows, features = image.shape
    empty = jnp.zeros((WIDE, features), image.dtype)
    padded = jnp.concatenate([empty, image, empty], axis=0)
    total = rows + 2 * WIDE
    return pltpu.roll(padded, 1, 0), padded, pltpu.roll(padded, total - 1, 0)


def convolve(image, taps, side):
    rows = image.shape[0]
    shifted = three_shifts(image)
    summed = None
    for i in range(3):
        for j in range(3):
            term = shifted[j][WIDE * i : WIDE * i + rows] * taps[3 * i + j : 3 * i + j + 1]
            summed = term if summed is None else summed + term
    return jnp.where(valid_rows(rows, side), summed, 0.0)


def to_all(message_ref, row, values):
    devices = message_ref.shape[0]
    message_ref[:, row, 0 : values.shape[1]] = jnp.broadcast_to(values, (devices, values.shape[1]))


def local_moments(conv_ref, moments_ref, images, side):
    rows = side * WIDE
    count = images * side * side
    total = None
    for n in range(images):
        part = jnp.sum(conv_ref[n * rows : (n + 1) * rows, :], axis=0, keepdims=True)
        total = part if total is None else total + part
    mean = total / count
    squares = None
    for n in range(images):
        deviate = jnp.where(
            valid_rows(rows, side), conv_ref[n * rows : (n + 1) * rows, :] - mean, 0.0
        )
        part = jnp.sum(deviate * deviate, axis=0, keepdims=True)
        squares = part if squares is None else squares + part
    to_all(moments_ref, 0, mean)
    to_all(moments_ref, 1, squares)


def whole_moments(gathered_ref, count):
    devices = gathered_ref.shape[0]
    means = gathered_ref[:, 0, :]
    squares = gathered_ref[:, 1, :]
    center = jnp.sum(means, axis=0, keepdims=True) / devices
    apart = means - center
    spread = (
        jnp.sum(squares, axis=0, keepdims=True)
        + jnp.sum(apart * apart, axis=0, keepdims=True) * count
    ) / (count * devices)
    return center, lax.rsqrt(spread + EPSILON)


def mixing_matrices(mix_w, mix_h, side):
    cells = side * WIDE
    row = lax.broadcasted_iota(jnp.int32, (cells, side), 0)
    col = lax.broadcasted_iota(jnp.int32, (cells, side), 1)
    at_w = (row % WIDE == col).astype(BF16)
    at_h = (row // WIDE == col).astype(BF16)
    out = lax.broadcasted_iota(jnp.int32, (cells, cells), 0)
    inp = lax.broadcasted_iota(jnp.int32, (cells, cells), 1)
    same_h = out // WIDE == inp // WIDE
    same_w = (out % WIDE == inp % WIDE) & (out % WIDE < side)

    def spread(picks, mix, keep, flip):
        left = (dot_cols if flip else dot)(picks, mix).astype(BF16)
        return jnp.where(keep, dot_cols(left, picks), 0.0).astype(BF16)

    forward = jnp.concatenate(
        [spread(at_w, mix_w, same_h, False), spread(at_h, mix_h, same_w, False)], axis=0
    )
    backward = jnp.concatenate(
        [spread(at_w, mix_w, same_h, True), spread(at_h, mix_h, same_w, True)], axis=1
    )
    return forward, backward


def by_image(maps_ref, all_ref):
    side, _, held, features = maps_ref.shape
    empty = jnp.zeros((WIDE - side, held, features), F32)
    for h in range(side):
        lines = jnp.concatenate([maps_ref[h], empty], axis=0)
        all_ref[:, h * WIDE : (h + 1) * WIDE, :] = jnp.swapaxes(lines, 0, 1)


def unpack_weights(tmp, unite_ref, up_ref, down_ref):
    packed_ref = tmp.packed
    shards, height, _ = packed_ref.shape
    part = height // 3
    features = unite_ref.shape[1]
    ups, downs, unites = [], [], []
    for s in range(shards):
        piece = packed_ref[s].astype(F32)
        ups.append(piece[:part])
        downs.append(piece[part : 2 * part])
        for q in range(3):
            unites.append(piece[2 * part :, q * features : (q + 1) * features])
    up_ref[...] = jnp.concatenate(ups, axis=0).astype(BF16)
    down_ref[...] = jnp.concatenate(downs, axis=0).astype(BF16)
    unite_ref[...] = jnp.concatenate(unites, axis=0).astype(BF16)


def pack_grads(unite, up, down, pieces_of, dp):
    features = up.shape[0]
    part = features // dp
    for s in range(dp):
        columns = [
            unite[(3 * s + q) * part : (3 * s + q + 1) * part] for q in range(3)
        ]
        filler = jnp.zeros((part, up.shape[1] - 3 * features), F32)
        piece = jnp.concatenate(
            [
                up[s * part : (s + 1) * part],
                down[s * part : (s + 1) * part],
                jnp.concatenate(columns + [filler], axis=1),
            ],
            axis=0,
        )
        pieces_of(s, piece.astype(BF16))


def pack_image_rows(values, side):
    lines = [values[r : r + side] for r in range(0, values.shape[0], WIDE)]
    half = len(lines) // 2
    return jnp.concatenate(
        [jnp.concatenate(lines[:half], axis=0), jnp.concatenate(lines[half:], axis=0)], axis=1
    )


def hidden_bias(up_bias_ref, layer, place_ref):
    groups = up_bias_ref.shape[1]
    blocks = [up_bias_ref[layer, pl.ds(place_ref[0] ^ j, 1), :] for j in range(groups)]
    return jnp.concatenate(blocks, axis=1)


def mix_image(conv, center, inv_std, bn_gain, bn_bias, mixing, side):
    rows = conv.shape[0]
    ahat = (conv - center) * inv_std
    branch = jnp.where(valid_rows(rows, side), ahat * bn_gain + bn_bias, 0.0).astype(BF16)
    along = dot(mixing, branch).astype(BF16)
    return branch, along[:rows], along[rows:]


def mlp_rows(stream, joined, unite_ref, norm_gain, up_ref, up_bias, down_ref, side):
    rows, features = stream.shape
    united = dot(joined, unite_ref[...])
    resid = stream + united
    mid = jnp.sum(resid, axis=-1, keepdims=True) / features
    deviate = resid - mid
    spread = jnp.sum(deviate * deviate, axis=-1, keepdims=True) / features
    inv_norm = lax.rsqrt(spread + EPSILON)
    uhat = deviate * inv_norm
    normal = (uhat * norm_gain).astype(BF16)
    pre = dot(normal, up_ref[...]) + up_bias
    below = 0.5 + 0.5 * lax.erf(pre * (0.5**0.5))
    slope = below + pre * (jnp.exp(-0.5 * pre * pre) * 0.3989422804014327)
    hidden = (pre * below).astype(BF16)
    mlp = jnp.where(valid_rows(rows, side), dot_cols(hidden, down_ref[...]), 0.0)
    result = resid + mlp
    squares = jnp.concatenate(
        [jnp.sum(v * v, axis=0, keepdims=True) for v in (united, mlp, result)], axis=0
    )
    return SimpleNamespace(
        uhat=uhat,
        inv_norm=inv_norm,
        slope=slope,
        hidden=hidden,
        result=result,
        squares=squares,
    )


def backward_rows(grad, uhat, inv_norm, slope, unite_ref, norm_gain, up_ref, down_ref):
    features = grad.shape[1]
    grad_low = grad.astype(BF16)
    gh = dot(grad_low, down_ref[...])
    gpre = (gh * slope).astype(BF16)
    bias = jnp.sum(gpre.astype(F32), axis=0, keepdims=True)
    gn = dot_cols(gpre, up_ref[...])
    gain = jnp.sum(gn * uhat, axis=0, keepdims=True)
    q = gn * norm_gain
    mean_q = jnp.sum(q, axis=-1, keepdims=True) / features
    mean_qu = jnp.sum(q * uhat, axis=-1, keepdims=True) / features
    gu = grad + inv_norm * (q - mean_q - uhat * mean_qu)
    gc = gu.astype(BF16)
    return SimpleNamespace(
        grad_low=grad_low, gpre=gpre, bias=bias, gain=gain, gu=gu, gc=gc, gj=dot_cols(gc, unite_ref[...])
    )


def backward_mixes(gj, branch, mixing_back):
    features = branch.shape[1]
    both = jnp.concatenate([gj[:, features : 2 * features], gj[:, 2 * features :]], axis=0).astype(BF16)
    return gj[:, :features] + dot(mixing_back, both), dot_cols(both, branch)


def mixing_grads(cross, side):
    cells = side * WIDE
    out = lax.broadcasted_iota(jnp.int32, (cells, cells), 0)
    inp = lax.broadcasted_iota(jnp.int32, (cells, cells), 1)
    width = jnp.where(out // WIDE == inp // WIDE, cross[:cells], 0.0)
    height = jnp.where(out % WIDE == inp % WIDE, cross[cells:], 0.0)
    across, down = None, []
    for v in range(side):
        at = slice(v * WIDE, (v + 1) * WIDE)
        across = add_up(across, width[at])
        down.append(jnp.sum(height[at], axis=0, keepdims=True))
    down = jnp.concatenate(down + [jnp.zeros((WIDE - side, cells), F32)], axis=0)
    parts = []
    for values in (across, down):
        high = values.astype(BF16)
        parts += [high, (values - high.astype(F32)).astype(BF16)]
    row = lax.broadcasted_iota(jnp.int32, (cells, 2 * WIDE), 0)
    col = lax.broadcasted_iota(jnp.int32, (cells, 2 * WIDE), 1)
    picks = (col == jnp.where(col < WIDE, row % WIDE, row // WIDE + WIDE)).astype(BF16)
    sums = dot(jnp.concatenate(parts, axis=0), picks)
    sums = sums[: 2 * WIDE, :WIDE], sums[2 * WIDE :, WIDE:]
    return tuple(value[:WIDE] + value[WIDE:] for value in sums)


def tap_sums(values, stream):
    rows = values.shape[0]
    shifted = three_shifts(stream)
    return jnp.concatenate(
        [
            jnp.sum(values * shifted[j][WIDE * i : WIDE * i + rows], axis=0, keepdims=True)
            for i in range(3)
            for j in range(3)
        ],
        axis=0,
    )


def conv_back_image(gb, ahat, gu, factor, offset_mean, scale_mean, taps, side):
    rows = gb.shape[0]
    valid = valid_rows(rows, side)
    ga = jnp.where(valid, factor * (gb - offset_mean - ahat * scale_mean), 0.0)
    turned = three_shifts(ga)
    summed = gu
    for i in range(3):
        for j in range(3):
            summed = (
                summed
                + turned[2 - j][WIDE * (2 - i) : WIDE * (2 - i) + rows]
                * taps[3 * i + j : 3 * i + j + 1]
            )
    return jnp.where(valid, summed, 0.0), ga


def add_up(total, part):
    return part if total is None else total + part


SMALL_ROWS, SMALL_WIDE = 60, 384
NORM_ROW, SQUARES_ROW, BIAS_ROW, TAPS_ROW = (27, 48), (28, 49), (31, 52), 39
KEPT = ("uhat", "inv_norm", "slope", "hidden")


def stage_forward(layer, ins, weights, weights_of, kept, on_result, *, images, side):
    rows = side * WIDE
    at = [slice(n * rows, (n + 1) * rows) for n in range(images)]
    center, inv_std = whole_moments(ins.moments, images * side * side)
    for n in range(images):
        branch, along_w, along_h = mix_image(
            ins.conv[at[n], :],
            center,
            inv_std,
            ins.batch_gain[layer : layer + 1, :],
            ins.batch_bias[layer : layer + 1, :],
            ins.mixing[...],
            side,
        )
        features = branch.shape[1]
        kept.joined[at[n], 0:features] = branch
        kept.joined[at[n], features : 2 * features] = along_w
        kept.joined[at[n], 2 * features : 3 * features] = along_h
    weights_of()
    up_bias = hidden_bias(ins.up_bias, layer, ins.place)
    found = mlp_rows(
        ins.stream[...],
        kept.joined[...],
        weights[0],
        ins.layer_gain[layer : layer + 1, :],
        weights[1],
        up_bias,
        weights[2],
        side,
    )
    for name in KEPT:
        to = getattr(kept, name)
        to[...] = getattr(found, name).astype(to.dtype)
    for n in range(images):
        on_result(n, found.result[at[n]])
    squares = found.squares
    return center, inv_std, squares


def stage_backward(
    layer, place, grad_of, center, inv_std, conv, par, weights, kept, gb, gu, small, rows_ref, pieces_of,
    dp, *, images, side,
):
    rows = side * WIDE
    features = gb.shape[1]
    grad_low, gpre, gc = rows_ref
    found = backward_rows(
        grad_of(),
        kept.uhat[...],
        kept.inv_norm[...],
        kept.slope[...].astype(F32),
        weights[0],
        par.layer_gain[layer : layer + 1, :],
        weights[1],
        weights[2],
    )
    grad_low[...] = found.grad_low
    gpre[...] = found.gpre
    gc[...] = found.gc
    gu[...] = found.gu.astype(gu.dtype)
    gain, bias = found.gain, found.bias
    offset = scale = cross = None
    for n in range(images):
        at = slice(n * rows, (n + 1) * rows)
        back, pairs = backward_mixes(found.gj[at], kept.joined[at, 0:features], par.mixing_back[...])
        gb[at, :] = back.astype(gb.dtype)
        offset = add_up(offset, jnp.sum(back, axis=0, keepdims=True))
        ahat = (conv[at, :] - center) * inv_std
        scale = add_up(scale, jnp.sum(back * ahat, axis=0, keepdims=True))
        cross = add_up(cross, pairs)
    small[NORM_ROW[layer] : NORM_ROW[layer] + 1, 0:features] = gain
    groups = par.up_bias.shape[1]
    width = bias.shape[1] // groups
    for j in range(groups):
        small[pl.ds(BIAS_ROW[layer] + (place[0] ^ j), 1), 0:width] = bias[:, j * width : (j + 1) * width]
    wide, tall = mixing_grads(cross, side)
    mixes = slice(layer * WIDE, (layer + 1) * WIDE)
    small[mixes, features : features + WIDE] = wide
    small[mixes, features + WIDE : features + 2 * WIDE] = tall
    unite_grad = dot_rows(kept.joined[...], gc[...])
    normal = (kept.uhat[...] * par.layer_gain[layer : layer + 1, :]).astype(BF16)
    up_grad = dot_rows(normal, gpre[...])
    down_grad = dot_rows(grad_low[...], kept.hidden[...])
    pack_grads(unite_grad, up_grad, down_grad, pieces_of, dp)
    return offset, scale


def first_body(ins, outs, tmp, *, images, side):
    place, taps = ins.place, ins.taps
    own, conv, moments = outs.own, outs.conv, outs.moments
    every = tmp.every
    rows = side * WIDE
    by_image(ins.stream, every)
    for n in range(images):
        own[n * rows : (n + 1) * rows, :] = every[place[0] * images + n]
    for n in range(images):
        at = slice(n * rows, (n + 1) * rows)
        conv[at, :] = convolve(own[at, :], taps[:, 0, :], side)
    local_moments(conv, moments, images, side)


def other_body(ins, outs, tmp, *, images, side):
    rows = side * WIDE
    by_image(ins.cotangent, tmp.every)
    for n in range(images):
        outs.cotangent[n * rows : (n + 1) * rows, :] = tmp.every[ins.place[0] * images + n]
    _, groups, width = outs.up_bias.shape
    for j in range(groups):
        outs.up_bias[:, j, :] = ins.up_bias[:, j * width : (j + 1) * width]
    mixes = ins.mix_w[...].astype(F32), ins.mix_h[...].astype(F32)
    for layer in range(ins.mix_w.shape[1]):
        outs.mixing[layer][...], outs.mixing_back[layer][...] = mixing_matrices(
            *(mix[:, layer, :].astype(BF16) for mix in mixes), side
        )


def middle_body(ins, outs, tmp, *, images, side):
    rows = side * WIDE
    weights = tmp.unite, tmp.up, tmp.down
    results = []

    def weights_of():
        unpack_weights(tmp, *weights)

    center, inv_std, squares = stage_forward(
        0, ins, weights, weights_of, outs, lambda n, result: results.append(result), images=images, side=side
    )
    outs.stats[0:1, :] = center
    outs.stats[1:2, :] = inv_std
    outs.squares[...] = squares
    for n, result in enumerate(results):
        at = slice(n * rows, (n + 1) * rows)
        outs.stream1[at, :] = result
        outs.conv1[at, :] = convolve(result, ins.taps[:, 1, :], side)
    local_moments(outs.conv1, outs.moments1, images, side)


def last_body(ins, outs, tmp, *, images, side, dp):
    weights = tmp.unite, tmp.up, tmp.down
    results = []

    def weights_of():
        unpack_weights(tmp, *weights)

    center, inv_std, squares = stage_forward(
        1, ins, weights, weights_of, tmp, lambda n, result: results.append(result), images=images, side=side
    )
    outs.result[...] = pack_image_rows(jnp.concatenate(results, axis=0), side).astype(BF16)
    outs.stats[0:1, :] = center
    outs.stats[1:2, :] = inv_std
    outs.small[...] = jnp.zeros_like(outs.small)
    pieces_of = sort_pieces(ins.place[1], outs)
    offset, scale = stage_backward(
        1, ins.place, lambda: ins.cotangent[...], center, inv_std,
        ins.conv, ins, weights, tmp, outs.gb, outs.gu, outs.small,
        (tmp.grad_low, tmp.gpre, tmp.gc), pieces_of, dp, images=images, side=side,
    )
    features = squares.shape[1]
    outs.small[SQUARES_ROW[1] : SQUARES_ROW[1] + 3, 0:features] = squares
    to_all(outs.sums, 0, offset)
    to_all(outs.sums, 1, scale)


def conv_back(layer, sums, gb, gu, conv, stats, par, totals, *, images, side):
    rows = side * WIDE
    features = gb.shape[1]
    cells = images * side * side * sums.shape[0]
    offset = jnp.sum(sums[:, 0, 0:features], axis=0, keepdims=True)
    scale = jnp.sum(sums[:, 1, 0:features], axis=0, keepdims=True)
    totals[0:1, :] = offset
    totals[1:2, :] = scale
    center, inv_std = stats[0:1, :], stats[1:2, :]
    factor = par.batch_gain[layer : layer + 1, :] * inv_std
    found = []
    for n in range(images):
        at = slice(n * rows, (n + 1) * rows)
        found.append(
            conv_back_image(
                gb[at, :].astype(F32),
                (conv[at, :] - center) * inv_std,
                gu[at, :].astype(F32),
                factor,
                offset / cells,
                scale / cells,
                par.taps[:, layer, :],
                side,
            )
        )
    return found


def taps_body(ins, outs, tmp, *, images, side):
    rows = side * WIDE
    center, inv_std = ins.stats[0:1, :], ins.stats[1:2, :]
    plain = scaled = None
    for n in range(images):
        at = slice(n * rows, (n + 1) * rows)
        stream = ins.stream[at, :]
        valid = valid_rows(rows, side)
        ones = jnp.where(valid, jnp.ones_like(stream), 0.0)
        ahat = jnp.where(valid, (ins.conv[at, :] - center) * inv_std, 0.0)
        plain = add_up(plain, tap_sums(ones, stream))
        scaled = add_up(scaled, tap_sums(ahat, stream))
    outs.plain[...] = plain
    outs.scaled[...] = scaled


def sort_pieces(mine, outs):
    def put(s, piece):
        same = ((mine ^ s) & 1) == 0

        @pl.when(same)
        def _():
            outs.keep[s >> 1] = piece

        @pl.when(jnp.logical_not(same))
        def _():
            outs.give[s >> 1] = piece

    return put


def between_body(ins, outs, tmp, *, images, side, dp):
    weights = tmp.unite, tmp.up, tmp.down
    unpack_weights(tmp, *weights)
    rows = side * WIDE
    features = ins.gb1.shape[1]
    small, sums = tmp.small, outs.sums
    small[...] = ins.small[...]
    grads, kernel = [], None
    found = conv_back(
        1, ins.sums1, ins.gb1, ins.gu1, ins.conv1, ins.stats1, ins, outs.totals1, images=images, side=side
    )
    for n, (grad, ga) in enumerate(found):
        grads.append(grad)
        kernel = add_up(kernel, tap_sums(ga, ins.stream1[n * rows : (n + 1) * rows, :]))
    small[TAPS_ROW : TAPS_ROW + 9, 0:features] = kernel
    stats = ins.stats0
    offset, scale = stage_backward(
        0, ins.place, lambda: jnp.concatenate(grads, axis=0), stats[0:1, :], stats[1:2, :], ins.conv0, ins, weights, ins,
        tmp.gb, tmp.gu, small, (tmp.grad_low, tmp.gpre, tmp.gc), sort_pieces(ins.place[1], outs), dp,
        images=images, side=side,
    )
    kernel = None
    for n in range(images):
        at = slice(n * rows, (n + 1) * rows)
        kernel = add_up(kernel, tap_sums(tmp.gb[at, :], ins.stream0[at, :]))
    for k, values in enumerate((kernel, ins.plain[...], ins.scaled[...])):
        small[9 * k : 9 * k + 9, 0:features] = values
    small[SQUARES_ROW[0] : SQUARES_ROW[0] + 3, 0:features] = ins.squares0[...]
    cells = images * side * side
    center, inv_std = stats[0:1, :], stats[1:2, :]
    grads = []
    for n in range(images):
        at = slice(n * rows, (n + 1) * rows)
        ahat = (ins.conv0[at, :] - center) * inv_std
        factor = ins.batch_gain[0:1, :] * inv_std
        grad, _ = conv_back_image(
            tmp.gb[at, :], ahat, tmp.gu[at, :], factor, offset / cells, scale / cells, ins.taps[:, 0, :], side
        )
        grads.append(grad)
    outs.grad[...] = pack_image_rows(jnp.concatenate(grads, axis=0), side).astype(BF16)
    to_all(sums, 0, offset)
    to_all(sums, 1, scale)
    devices, height, _ = sums.shape
    for g in range(height - 2):
        held = min(devices, SMALL_ROWS - g * devices)
        sums[0:held, 2 + g, :] = small[g * devices : g * devices + held, :]
        if held < devices:
            sums[held:, 2 + g, :] = jnp.zeros((devices - held, SMALL_WIDE), F32)


def final_body(ins, outs, tmp, *, images, side):
    held, rows, features = tmp.every.shape
    sums = ins.sums0
    cells = images * side * side
    devices = sums.shape[0]
    group = held // images
    offset = jnp.sum(sums[:, 0, 0:features], axis=0, keepdims=True)
    scale = jnp.sum(sums[:, 1, 0:features], axis=0, keepdims=True)
    for row, total in enumerate((offset, scale)):
        to = (outs.offset_grad, outs.scale_grad)[row]
        to[0:1, :] = total
        to[1:2, :] = ins.totals1[row : row + 1, :]
    center, inv_std = ins.stats0[0:1, :], ins.stats0[1:2, :]
    factor = ins.batch_gain[0:1, :] * inv_std
    first = ins.place[1] * group

    def apart(row, total):
        own = [sums[first + p, row : row + 1, 0:features] for p in range(group)]
        own = jnp.concatenate([value for value in own for _ in range(images)], axis=0)
        return factor * (total / (cells * devices) - own / cells)

    shift, slant = apart(0, offset), apart(1, scale)
    put_images(ins.place[0], ins.parts, tmp.every, images, side)
    padded, fields = tmp.padded, tmp.fields
    for ref in (padded, fields):
        edge = jnp.zeros((1,) + ref.shape[1:], F32)
        ref[0:1] = edge
        ref[side + 1 : side + 2] = edge
        edge = jnp.zeros((side, 1) + ref.shape[2:], F32)
        ref[1 : side + 1, 0:1] = edge
        ref[1 : side + 1, side + 1 : side + 2] = edge
    padded[1 : side + 1, 1 : side + 1] = ins.stream[...]
    taps = ins.taps[:, 0, :]
    for h in range(side):
        conv = None
        for i in range(3):
            for j in range(3):
                term = padded[h + i, j : j + side] * taps[3 * i + j : 3 * i + j + 1]
                conv = add_up(conv, term)
        fields[h + 1, 1 : side + 1] = shift + (conv - center) * inv_std * slant
    for h in range(side):
        lines = jnp.swapaxes(tmp.every[:, h * WIDE : (h + 1) * WIDE, :], 0, 1)[:side]
        for i in range(3):
            for j in range(3):
                lines = lines - fields[h + 2 - i, 2 - j : 2 - j + side] * taps[3 * i + j : 3 * i + j + 1]
        outs.out[h] = lines


def put_images(place, parts, every, images, side):
    features = every.shape[2]
    for j, part in enumerate(parts):
        packed = part[...].astype(F32)
        lines = packed.shape[0] // side
        for half in range(2):
            values = packed[:, half * features : (half + 1) * features]
            for k in range(lines):
                n, h = divmod(half * lines + k, side)
                every[(place ^ j) * images + n, h * WIDE : h * WIDE + side, :] = values[
                    k * side : (k + 1) * side
                ]


def gather_body(ins, outs, tmp):
    for g in range(outs.message.shape[1]):
        to_all(outs.message, g, jnp.sum(ins.sums0[:, 2 + g, :], axis=0, keepdims=True))


def spread_body(ins, outs, tmp, *, images, side):
    put_images(ins.place[0], ins.parts, tmp.every, images, side)
    for h in range(side):
        outs.out[h] = jnp.swapaxes(tmp.every[:, h * WIDE : (h + 1) * WIDE, :], 0, 1)[:side]


def core_body(ins, outs, tmp):
    apart = isinstance(outs.parts, list)
    for k in range(ins.keep.shape[0]):
        at = (ins.place[1] >> 1) ^ k if apart else k
        to = outs.parts[k] if apart else outs.parts.at[k]
        to[...] = (ins.keep[at].astype(F32) + ins.got[at].astype(F32)).astype(BF16)


def chips_body(ins, outs, tmp):
    groups = len(outs.give)
    for layer, parts in enumerate(ins.parts):
        parts = parts if isinstance(parts, list) else [parts.at[k] for k in range(parts.shape[0])]
        total = parts[0][...].astype(F32)
        for other in parts[1:]:
            total = total + other[...].astype(F32)
        part = total.shape[0] // 3
        width = total.shape[1] // groups
        features = outs.give[0].shape[2] - 2 * width
        for j in range(groups):
            block = jnp.concatenate(
                [
                    total[:part, j * width : (j + 1) * width],
                    total[part : 2 * part, j * width : (j + 1) * width],
                    total[2 * part :, :features],
                ],
                axis=1,
            )
            outs.give[j][layer] = block.astype(BF16)


def weights_body(ins, outs, tmp):
    layers = outs.up_grad.shape[0]
    for layer in range(layers):
        terms = [ref[layer].astype(F32) for ref in ins.got]
        while len(terms) > 1:
            terms = [terms[j] + terms[j + 1] for j in range(0, len(terms), 2)]
        total = terms[0]
        width = outs.up_grad.shape[2]
        features = outs.unite_grad.shape[1]
        outs.up_grad[layer] = total[:, :width]
        outs.down_grad[layer] = total[:, width : 2 * width]
        rest = total[:, 2 * width :]
        rows = jnp.concatenate([rest[:, q * features : (q + 1) * features] for q in range(3)], axis=0)
        outs.unite_grad[layer] = rows.T


def small_body(ins, outs, tmp, *, side, cells, entries):
    got = ins.got
    features = outs.gain_grad.shape[1]
    devices, height, _ = got.shape
    values = tmp.values
    for g in range(height):
        values[g * devices : (g + 1) * devices, :] = got[:, g, :]
    factor = ins.batch_gain[0:1, :] * ins.stats0[1:2, :]
    first = factor * (
        values[0:9, 0:features]
        - ins.offset[0:1, :] / cells * values[9:18, 0:features]
        - ins.scale[0:1, :] / cells * values[18:27, 0:features]
    )
    for k in range(9):
        outs.kernel_grad[k, 0:1, :] = first[k : k + 1]
        outs.kernel_grad[k, 1:2, :] = values[TAPS_ROW + k : TAPS_ROW + k + 1, 0:features]
    width = outs.bias_grad.shape[1]
    for layer in range(2):
        outs.gain_grad[layer : layer + 1, :] = values[NORM_ROW[layer] : NORM_ROW[layer] + 1, 0:features]
        outs.bias_grad[layer : layer + 1, :] = values[pl.ds(BIAS_ROW[layer] + ins.place[0], 1), 0:width]
        rows = slice(layer * WIDE, layer * WIDE + side)
        outs.width_grad[:, layer, :] = values[rows, features : features + side]
        outs.height_grad[:, layer, :] = values[rows, features + WIDE : features + WIDE + side]
        squares = values[SQUARES_ROW[layer] : SQUARES_ROW[layer] + 3, 0:features]
        outs.stream_rms[:, layer : layer + 1] = jnp.sqrt(
            jnp.sum(squares, axis=1, keepdims=True) / entries
        )


def call(body, ins, outs, scratch=None, shards=(), micros=0, vmem=VMEM_LIMIT, **static):
    ins = dict(ins, shards=list(shards))
    operands, in_tree = jax.tree.flatten(ins)
    shapes, out_tree = jax.tree.flatten(
        {name: jax.tree.map(lambda shape: jax.ShapeDtypeStruct(*shape), outs[name], is_leaf=is_shape) for name in outs}
    )
    scratch = dict(scratch or {})
    if shards:
        scratch["packed"] = (len(shards),) + shards[0].shape, shards[0].dtype
    tmp_names = list(scratch)

    def kernel(*refs):
        cut = len(operands), len(operands) + len(shapes)
        given = SimpleNamespace(**jax.tree.unflatten(in_tree, refs[: cut[0]]))
        results = SimpleNamespace(**jax.tree.unflatten(out_tree, refs[cut[0] : cut[1]]))
        tmp = SimpleNamespace(**dict(zip(tmp_names, refs[cut[1] :])))
        for k, shard in enumerate(given.shards):
            tmp.packed[given.place[1] ^ k] = shard[...]
        body(given, results, tmp, **static)

    def space(name):
        return pl.BlockSpec(memory_space=pltpu.SMEM if name == "place" else pltpu.VMEM)

    found = pl.pallas_call(
        kernel,
        out_shape=shapes,
        in_specs=jax.tree.leaves({name: jax.tree.map(lambda _: space(name), ins[name]) for name in ins}),
        out_specs=[space("")] * len(shapes),
        scratch_shapes=[pltpu.VMEM(*scratch[name]) for name in tmp_names],
        compiler_params=pltpu.CompilerParams(vmem_limit_bytes=vmem),
        cost_estimate=pl.CostEstimate(
            flops=int(micros * COST_FLOPS), transcendentals=0, bytes_accessed=int(micros * COST_BYTES)
        ),
    )(*operands)
    return SimpleNamespace(**jax.tree.unflatten(out_tree, found))


def is_shape(value):
    return isinstance(value, tuple)


def swap(values, axis, mask):
    return lax.ppermute(values, axis, [(i, i ^ mask) for i in range(lax.axis_size(axis))])


def after(values, *others):
    return lax.optimization_barrier((values, others))[0]


def per_device(
    inputs,
    conv_weight,
    batch_gain,
    batch_bias,
    mix_width,
    mix_height,
    unite_weight,
    layer_gain,
    up_weight,
    up_bias,
    down_weight,
    cotangent,
):
    held, side, _, features = inputs.shape
    layers = conv_weight.shape[0]
    dp, mp = lax.axis_size("dp"), lax.axis_size("mp")
    devices = dp * mp
    images = held // mp
    cells = side * WIDE
    rows = images * cells
    units = up_bias.shape[1]
    part = features // dp
    both = ("dp", "mp")
    sizes = dict(images=images, side=side)
    place = jnp.stack([lax.axis_index("mp"), lax.axis_index("dp")]).astype(jnp.int32)

    def group_parts(values):
        if isinstance(values, (list, tuple)):
            return [swap(value, "mp", j) if j else value for j, value in enumerate(values)]
        parts = [values]
        for j in range(1, mp):
            step = j & -j
            parts.append(swap(parts[j ^ step], "mp", step))
        return parts

    def share(blocks):
        return lax.all_to_all(blocks, both, 0, 0, tiled=False)

    maps = jnp.transpose(inputs, (1, 2, 0, 3))
    cotangent_maps = jnp.transpose(cotangent, (1, 2, 0, 3))
    taps = jnp.transpose(conv_weight, (1, 0, 2))
    mix_w, mix_h = (jnp.transpose(mix, (1, 0, 2)) for mix in (mix_width, mix_height))
    shared = (devices, 2, features)
    thirds = unite_weight.reshape(layers, 3, part, features)
    thirds = jnp.concatenate([thirds[:, q] for q in range(3)], axis=2)
    thirds = jnp.pad(thirds, ((0, 0), (0, 0), (0, units - 3 * features)))

    def widen(wide, step):
        return jnp.concatenate([wide, swap(wide, "mp", step)], axis=1)

    def over_dp(layer, wide, wait_chips, wait_core):
        piece = after(jnp.concatenate([wide, thirds[layer]], axis=0), *wait_chips)
        shards = [piece] + [swap(piece, "dp", 2 * k) for k in range(1, dp // 2)]
        mates = [swap(after(shard, *wait_core), "dp", 1) for shard in shards]
        return [shard for pair in zip(shards, mates) for shard in pair]

    wide = jnp.concatenate([up_weight[0], down_weight[0]], axis=0)
    wide = near = widen(wide, 1) if mp > 1 else wide
    step = 2
    while step < mp:
        wide = widen(wide, step)
        step *= 2
    found = call(
        first_body,
        dict(place=after(place, near), stream=maps, taps=taps),
        dict(own=((rows, features), F32), conv=((rows, features), F32), moments=(shared, F32)),
        dict(every=((held, cells, features), F32)),
        micros=4,
        **sizes,
    )
    moments0 = share(after(found.moments, wide))
    other = call(
        other_body,
        dict(place=place, cotangent=cotangent_maps, mix_w=mix_w, mix_h=mix_h, up_bias=up_bias),
        dict(
            cotangent=((rows, features), F32),
            up_bias=((layers, mp, units // mp), F32),
            mixing=[((2 * cells, cells), BF16)] * layers,
            mixing_back=[((cells, 2 * cells), BF16)] * layers,
        ),
        dict(every=((held, cells, features), F32)),
        micros=3,
        **sizes,
    )

    packed = [over_dp(0, wide, (found.moments,), (moments0, other.mixing[0]))]
    wide = after(jnp.concatenate([up_weight[1], down_weight[1]], axis=0), wide)
    step = 1
    while step < mp:
        wide = widen(wide, step)
        step *= 2
    wide1 = wide

    own, conv0 = found.own, found.conv
    par = dict(
        place=place,
        taps=taps,
        batch_gain=batch_gain,
        batch_bias=batch_bias,
        layer_gain=layer_gain,
        up_bias=other.up_bias,
    )
    kept = dict(
        joined=((rows, 3 * features), BF16),
        uhat=((rows, features), F32),
        inv_norm=((rows, 1), F32),
        slope=((rows, units), BF16),
        hidden=((rows, units), BF16),
    )
    weight_tmp = dict(
        unite=((3 * features, features), BF16),
        up=((features, units), BF16),
        down=((features, units), BF16),
    )
    back_tmp = dict(
        grad_low=((rows, features), BF16), gpre=((rows, units), BF16), gc=((rows, features), BF16)
    )
    back_outs = dict(gb=((rows, features), F32), gu=((rows, features), F32))
    stats = ((2, features), F32)
    pieces = [((dp // 2, 3 * part, units), BF16)] * 2
    piece = ((3 * part, units), BF16)

    def over_core(values, apart=False):
        return call(
            core_body,
            dict(place=place, keep=values.keep, got=swap(values.give, "dp", 1)),
            dict(parts=[piece] * (dp // 2) if apart else pieces[0]),
            vmem=SMALL_LIMIT,
        ).parts

    def from_chips(parts):
        if isinstance(parts, list):
            return [swap(values, "dp", 2 * k) if k else values for k, values in enumerate(parts)]
        groups = [[2 * q + c for q in range(dp // 2)] for c in range(2)]
        return lax.all_to_all(parts, "dp", 0, 0, axis_index_groups=groups, tiled=False)

    mid = call(
        middle_body,
        dict(
            par,
            moments=moments0,
            conv=conv0,
            stream=own,
            mixing=other.mixing[0],
        ),
        dict(
            kept,
            stream1=((rows, features), F32),
            conv1=((rows, features), F32),
            moments1=(shared, F32),
            stats=stats,
            squares=((3, features), F32),
        ),
        weight_tmp,
        packed[0],
        micros=6,
        **sizes,
    )
    packed.append(over_dp(1, wide1, packed[0][::2], (mid.moments1,)))
    under = call(
        taps_body,
        dict(stream=own, conv=conv0, stats=mid.stats),
        dict(plain=((9, features), F32), scaled=((9, features), F32)),
        micros=2,
        **sizes,
    )
    last = call(
        last_body,
        dict(
            par,
            moments=after(share(mid.moments1), under.plain),
            conv=mid.conv1,
            stream=mid.stream1,
            mixing=other.mixing[1],
            mixing_back=other.mixing_back[1],
            cotangent=other.cotangent,
        ),
        dict(
            gb=((rows, features), BF16),
            gu=((rows, features), BF16),
            result=((images * side * side // 2, 2 * features), BF16),
            stats=stats,
            small=((SMALL_ROWS, SMALL_WIDE), F32),
            sums=(shared, F32),
            keep=pieces[0],
            give=pieces[1],
        ),
        dict(
            dict(kept, slope=((rows, units), F32)),
            **weight_tmp,
            **back_tmp,
        ),
        packed[1],
        micros=10,
        dp=dp,
        **sizes,
    )
    summed1 = over_core(last)
    groups = -(-SMALL_ROWS // devices)
    between = call(
        between_body,
        {
            **par,
            **{name: getattr(mid, name) for name in kept},
            **dict(
                sums1=after(share(last.sums), summed1),
                gb1=last.gb,
                gu1=last.gu,
                conv1=mid.conv1,
                stream1=mid.stream1,
                stats1=last.stats,
                small=last.small,
                stream0=own,
                plain=under.plain,
                scaled=under.scaled,
                conv0=conv0,
                stats0=mid.stats,
                squares0=mid.squares,
                mixing_back=other.mixing_back[0],
            ),
        },
        dict(
            grad=((images * side * side // 2, 2 * features), BF16),
            totals1=stats,
            sums=((devices, 2 + groups, SMALL_WIDE), F32),
            keep=pieces[0],
            give=pieces[1],
        ),
        dict(
            back_tmp,
            **back_outs,
            **weight_tmp,
            small=((SMALL_ROWS, SMALL_WIDE), F32),
        ),
        packed[0],
        micros=10,
        dp=dp,
        **sizes,
    )
    result_parts = [last.result] + [swap(last.result, "mp", 1 << k) for k in range((mp - 1).bit_length())]
    parts1 = from_chips(summed1)
    grad, sums0, give, parts1, near = lax.optimization_barrier(
        (between.grad, between.sums, between.give, parts1, result_parts[1:])
    )
    result_parts = [last.result]
    for j in range(1, mp):
        step = j & -j
        result_parts.append(near[j.bit_length() - 1] if j == step else swap(result_parts[j ^ step], "mp", step))
    sums0 = share(sums0)
    chunk = call(
        gather_body, dict(sums0=sums0), dict(message=((devices, groups, SMALL_WIDE), F32)), vmem=SMALL_LIMIT
    )
    shared_small = share(chunk.message)
    summed0 = over_core(SimpleNamespace(keep=between.keep, give=give), True)
    summed0 = after(summed0, result_parts)
    grad_parts = group_parts(after(grad, summed0))
    cut = call(
        chips_body,
        dict(parts=[from_chips(summed0), parts1]),
        dict(give=[((layers, part, 2 * (units // mp) + 3 * features), BF16)] * mp),
        vmem=SMALL_LIMIT,
    ).give
    grads = call(
        weights_body,
        dict(got=group_parts(after(cut, grad_parts, shared_small))),
        dict(
            up_grad=((layers, part, units // mp), F32),
            down_grad=((layers, part, units // mp), F32),
            unite_grad=((layers, features, 3 * part), F32),
        ),
        vmem=SMALL_LIMIT,
    )
    whole_maps = ((side, side, held, features), F32)
    output = call(
        spread_body,
        dict(place=place, parts=result_parts),
        dict(out=whole_maps),
        dict(every=((held, cells, features), F32)),
        **sizes,
    ).out
    padded = ((side + 2, side + 2, held, features), F32)
    end = call(
        final_body,
        dict(
            place=place,
            parts=grad_parts,
            stream=maps,
            sums0=sums0,
            totals1=between.totals1,
            stats0=mid.stats,
            batch_gain=batch_gain,
            taps=taps,
        ),
        dict(out=whole_maps, offset_grad=stats, scale_grad=stats),
        dict(every=((held, cells, features), F32), padded=padded, fields=padded),
        **sizes,
    )
    outputs = [jnp.transpose(out, (2, 0, 1, 3)) for out in (output, end.out)]
    small = call(
        small_body,
        dict(
            place=place,
            got=shared_small,
            batch_gain=batch_gain,
            stats0=mid.stats,
            offset=end.offset_grad,
            scale=end.scale_grad,
        ),
        dict(
            kernel_grad=((9, layers, features), F32),
            gain_grad=((layers, features), F32),
            bias_grad=((layers, units // mp), F32),
            width_grad=((side, layers, side), F32),
            height_grad=((side, layers, side), F32),
            stream_rms=((3, layers), F32),
        ),
        dict(values=((groups * devices, SMALL_WIDE), F32)),
        vmem=SMALL_LIMIT,
        side=side,
        cells=images * side * side * devices,
        entries=held * side * side * features * dp,
    )
    return (
        *outputs,
        jnp.transpose(small.kernel_grad, (1, 0, 2)),
        end.scale_grad,
        end.offset_grad,
        jnp.transpose(small.width_grad, (1, 0, 2)),
        jnp.transpose(small.height_grad, (1, 0, 2)),
        jnp.transpose(grads.unite_grad, (0, 2, 1)),
        small.gain_grad,
        grads.up_grad,
        small.bias_grad,
        grads.down_grad,
        small.stream_rms.T,
    )


def solution(mesh):
    in_specs = (
        P("dp", None, None, None),
        P(),
        P(),
        P(),
        P(),
        P(),
        P(None, "dp", None),
        P(),
        P(None, "dp", "mp"),
        P(),
        P(None, "dp", "mp"),
        P("dp", None, None, None),
    )
    out_specs = (
        P("dp", None, None, None),
        P("dp", None, None, None),
        P(),
        P(),
        P(),
        P(),
        P(),
        P(None, "dp", None),
        P(),
        P(None, "dp", "mp"),
        P(None, "mp"),
        P(None, "dp", "mp"),
        P(),
    )
    return jax.shard_map(
        per_device, mesh=mesh, in_specs=in_specs, out_specs=out_specs, check_vma=False
    )
```

```python
import functools
from types import SimpleNamespace

import jax
import jax.numpy as jnp
from jax import lax
from jax.experimental import pallas as pl
from jax.experimental.pallas import tpu as pltpu
from jax.sharding import PartitionSpec as P

EPSILON = 1e-05
WIDE = 16
VMEM_LIMIT = 58 * 1024 * 1024
SMALL_LIMIT = 14 * 1024 * 1024
COST_BYTES = 3.0e6
COST_FLOPS = 1.0e10
F32 = jnp.float32
BF16 = jnp.bfloat16


def dot(left, right):
    return lax.dot_general(left, right, (((1,), (0,)), ((), ())), preferred_element_type=F32)


def dot_cols(left, right):
    return lax.dot_general(left, right, (((1,), (1,)), ((), ())), preferred_element_type=F32)


def dot_rows(left, right):
    return lax.dot_general(left, right, (((0,), (0,)), ((), ())), preferred_element_type=F32)


def valid_rows(rows, side):
    return lax.broadcasted_iota(jnp.int32, (rows, 1), 0) % WIDE < side


def three_shifts(image):
    rows, features = image.shape
    empty = jnp.zeros((WIDE, features), image.dtype)
    padded = jnp.concatenate([empty, image, empty], axis=0)
    total = rows + 2 * WIDE
    return pltpu.roll(padded, 1, 0), padded, pltpu.roll(padded, total - 1, 0)


def convolve(image, taps, side):
    rows = image.shape[0]
    shifted = three_shifts(image)
    summed = None
    for i in range(3):
        for j in range(3):
            term = shifted[j][WIDE * i : WIDE * i + rows] * taps[3 * i + j : 3 * i + j + 1]
            summed = term if summed is None else summed + term
    return jnp.where(valid_rows(rows, side), summed, 0.0)


def to_all(message_ref, row, values):
    devices = message_ref.shape[0]
    message_ref[:, row, 0 : values.shape[1]] = jnp.broadcast_to(values, (devices, values.shape[1]))


def local_moments(conv_ref, moments_ref, images, side):
    rows = side * WIDE
    count = images * side * side
    total = None
    for n in range(images):
        part = jnp.sum(conv_ref[n * rows : (n + 1) * rows, :], axis=0, keepdims=True)
        total = part if total is None else total + part
    mean = total / count
    squares = None
    for n in range(images):
        deviate = jnp.where(
            valid_rows(rows, side), conv_ref[n * rows : (n + 1) * rows, :] - mean, 0.0
        )
        part = jnp.sum(deviate * deviate, axis=0, keepdims=True)
        squares = part if squares is None else squares + part
    to_all(moments_ref, 0, mean)
    to_all(moments_ref, 1, squares)


def whole_moments(gathered_ref, count):
    devices = gathered_ref.shape[0]
    means = gathered_ref[:, 0, :]
    squares = gathered_ref[:, 1, :]
    center = jnp.sum(means, axis=0, keepdims=True) / devices
    apart = means - center
    spread = (
        jnp.sum(squares, axis=0, keepdims=True)
        + jnp.sum(apart * apart, axis=0, keepdims=True) * count
    ) / (count * devices)
    return center, lax.rsqrt(spread + EPSILON)


def mixing_matrices(mix_w, mix_h, side):
    cells = side * WIDE
    row = lax.broadcasted_iota(jnp.int32, (cells, side), 0)
    col = lax.broadcasted_iota(jnp.int32, (cells, side), 1)
    at_w = (row % WIDE == col).astype(BF16)
    at_h = (row // WIDE == col).astype(BF16)
    out = lax.broadcasted_iota(jnp.int32, (cells, cells), 0)
    inp = lax.broadcasted_iota(jnp.int32, (cells, cells), 1)
    same_h = out // WIDE == inp // WIDE
    same_w = (out % WIDE == inp % WIDE) & (out % WIDE < side)

    def spread(picks, mix, keep, flip):
        left = (dot_cols if flip else dot)(picks, mix).astype(BF16)
        return jnp.where(keep, dot_cols(left, picks), 0.0).astype(BF16)

    forward = jnp.concatenate(
        [spread(at_w, mix_w, same_h, False), spread(at_h, mix_h, same_w, False)], axis=0
    )
    backward = jnp.concatenate(
        [spread(at_w, mix_w, same_h, True), spread(at_h, mix_h, same_w, True)], axis=1
    )
    return forward, backward


def by_image(maps_ref, all_ref):
    side, _, held, features = maps_ref.shape
    empty = jnp.zeros((WIDE - side, held, features), F32)
    for h in range(side):
        lines = jnp.concatenate([maps_ref[h], empty], axis=0)
        all_ref[:, h * WIDE : (h + 1) * WIDE, :] = jnp.swapaxes(lines, 0, 1)


def unpack_weights(tmp, unite_ref, up_ref, down_ref):
    packed_ref = tmp.packed
    shards, height, _ = packed_ref.shape
    part = height // 3
    features = unite_ref.shape[1]
    ups, downs, unites = [], [], []
    for s in range(shards):
        piece = packed_ref[s].astype(F32)
        ups.append(piece[:part])
        downs.append(piece[part : 2 * part])
        for q in range(3):
            unites.append(piece[2 * part :, q * SMALL_WIDE : q * SMALL_WIDE + features])
    up_ref[...] = jnp.concatenate(ups, axis=0).astype(BF16)
    down_ref[...] = jnp.concatenate(downs, axis=0).astype(BF16)
    unite_ref[...] = jnp.concatenate(unites, axis=0).astype(BF16)


def pack_grads(unite, up, down, mine, outs, dp):
    features = up.shape[0]
    part = features // dp
    beside = jnp.zeros((part, SMALL_WIDE - features), F32)
    filler = jnp.zeros((part, up.shape[1] - 3 * SMALL_WIDE), F32)

    def piece(s):
        columns = []
        for q in range(3):
            columns += [unite[(3 * s + q) * part : (3 * s + q + 1) * part], beside]
        return jnp.concatenate(
            [
                up[s * part : (s + 1) * part],
                down[s * part : (s + 1) * part],
                jnp.concatenate(columns + [filler], axis=1),
            ],
            axis=0,
        )

    first = (mine & 1) == 0
    for k in range(dp // 2):
        pair = piece(2 * k), piece(2 * k + 1)
        outs.keep[k] = jnp.where(first, pair[0], pair[1]).astype(BF16)
        outs.give[k] = jnp.where(first, pair[1], pair[0]).astype(BF16)


def pack_image_rows(values, side):
    lines = [values[r : r + side] for r in range(0, values.shape[0], WIDE)]
    half = len(lines) // 2
    return jnp.concatenate(
        [jnp.concatenate(lines[:half], axis=0), jnp.concatenate(lines[half:], axis=0)], axis=1
    )


def hidden_bias(up_bias_ref, layer, place_ref):
    groups = up_bias_ref.shape[1]
    blocks = [up_bias_ref[layer, pl.ds(place_ref[0] ^ j, 1), :] for j in range(groups)]
    return jnp.concatenate(blocks, axis=1)


def mix_image(conv, center, inv_std, bn_gain, bn_bias, mixing, side):
    rows = conv.shape[0]
    ahat = (conv - center) * inv_std
    branch = jnp.where(valid_rows(rows, side), ahat * bn_gain + bn_bias, 0.0).astype(BF16)
    along = dot(mixing, branch).astype(BF16)
    return branch, along[:rows], along[rows:]


def mlp_rows(stream, joined, unite_ref, norm_gain, up_ref, up_bias, down_ref, side):
    rows, features = stream.shape
    united = dot(joined, unite_ref[...])
    resid = stream + united
    mid = jnp.sum(resid, axis=-1, keepdims=True) / features
    deviate = resid - mid
    spread = jnp.sum(deviate * deviate, axis=-1, keepdims=True) / features
    inv_norm = lax.rsqrt(spread + EPSILON)
    uhat = deviate * inv_norm
    normal = (uhat * norm_gain).astype(BF16)
    pre = dot(normal, up_ref[...]) + up_bias
    below = 0.5 + 0.5 * lax.erf(pre * (0.5**0.5))
    slope = below + pre * (jnp.exp(-0.5 * pre * pre) * 0.3989422804014327)
    hidden = (pre * below).astype(BF16)
    mlp = jnp.where(valid_rows(rows, side), dot_cols(hidden, down_ref[...]), 0.0)
    result = resid + mlp
    squares = jnp.concatenate(
        [jnp.sum(v * v, axis=0, keepdims=True) for v in (united, mlp, result)], axis=0
    )
    return SimpleNamespace(
        uhat=uhat,
        inv_norm=inv_norm,
        slope=slope,
        hidden=hidden,
        result=result,
        squares=squares,
    )


def backward_rows(grad, uhat, inv_norm, slope, unite_ref, norm_gain, up_ref, down_ref):
    features = grad.shape[1]
    grad_low = grad.astype(BF16)
    gh = dot(grad_low, down_ref[...])
    gpre = (gh * slope).astype(BF16)
    bias = jnp.sum(gpre.astype(F32), axis=0, keepdims=True)
    gn = dot_cols(gpre, up_ref[...])
    gain = jnp.sum(gn * uhat, axis=0, keepdims=True)
    q = gn * norm_gain
    mean_q = jnp.sum(q, axis=-1, keepdims=True) / features
    mean_qu = jnp.sum(q * uhat, axis=-1, keepdims=True) / features
    gu = grad + inv_norm * (q - mean_q - uhat * mean_qu)
    gc = gu.astype(BF16)
    return SimpleNamespace(
        grad_low=grad_low, gpre=gpre, bias=bias, gain=gain, gu=gu, gc=gc, gj=dot_cols(gc, unite_ref[...])
    )


def backward_mixes(gj, branch, mixing_back):
    features = branch.shape[1]
    both = jnp.concatenate([gj[:, features : 2 * features], gj[:, 2 * features :]], axis=0).astype(BF16)
    return gj[:, :features] + dot(mixing_back, both), dot_cols(both, branch)


def mixing_grads(cross, side):
    cells = side * WIDE
    out = lax.broadcasted_iota(jnp.int32, (cells, cells), 0)
    inp = lax.broadcasted_iota(jnp.int32, (cells, cells), 1)
    width = jnp.where(out // WIDE == inp // WIDE, cross[:cells], 0.0)
    height = jnp.where(out % WIDE == inp % WIDE, cross[cells:], 0.0)
    across, down = None, []
    for v in range(side):
        at = slice(v * WIDE, (v + 1) * WIDE)
        across = add_up(across, width[at])
        down.append(jnp.sum(height[at], axis=0, keepdims=True))
    down = jnp.concatenate(down + [jnp.zeros((WIDE - side, cells), F32)], axis=0)
    parts = []
    for values in (across, down):
        high = values.astype(BF16)
        parts += [high, (values - high.astype(F32)).astype(BF16)]
    row = lax.broadcasted_iota(jnp.int32, (cells, 2 * WIDE), 0)
    col = lax.broadcasted_iota(jnp.int32, (cells, 2 * WIDE), 1)
    picks = (col == jnp.where(col < WIDE, row % WIDE, row // WIDE + WIDE)).astype(BF16)
    sums = dot(jnp.concatenate(parts, axis=0), picks)
    sums = sums[: 2 * WIDE, :WIDE], sums[2 * WIDE :, WIDE:]
    return tuple(value[:WIDE] + value[WIDE:] for value in sums)


def tap_sums(values, stream):
    rows = values.shape[0]
    shifted = three_shifts(stream)
    return jnp.concatenate(
        [
            jnp.sum(values * shifted[j][WIDE * i : WIDE * i + rows], axis=0, keepdims=True)
            for i in range(3)
            for j in range(3)
        ],
        axis=0,
    )


def conv_back_image(gb, ahat, gu, factor, offset_mean, scale_mean, taps, side):
    rows = gb.shape[0]
    valid = valid_rows(rows, side)
    ga = jnp.where(valid, factor * (gb - offset_mean - ahat * scale_mean), 0.0)
    turned = three_shifts(ga)
    summed = gu
    for i in range(3):
        for j in range(3):
            summed = (
                summed
                + turned[2 - j][WIDE * (2 - i) : WIDE * (2 - i) + rows]
                * taps[3 * i + j : 3 * i + j + 1]
            )
    return jnp.where(valid, summed, 0.0), ga


def add_up(total, part):
    return part if total is None else total + part


SMALL_ROWS, SMALL_WIDE = 60, 384
NORM_ROW, SQUARES_ROW, BIAS_ROW, TAPS_ROW = (27, 48), (28, 49), (31, 52), 39
KEPT = ("uhat", "inv_norm", "slope", "hidden")


def stage_forward(layer, ins, weights, weights_of, kept, on_result, *, images, side):
    rows = side * WIDE
    at = [slice(n * rows, (n + 1) * rows) for n in range(images)]
    center, inv_std = whole_moments(ins.moments, images * side * side)
    for n in range(images):
        branch, along_w, along_h = mix_image(
            ins.conv[at[n], :],
            center,
            inv_std,
            ins.batch_gain[layer : layer + 1, :],
            ins.batch_bias[layer : layer + 1, :],
            ins.mixing[...],
            side,
        )
        features = branch.shape[1]
        kept.joined[at[n], 0:features] = branch
        kept.joined[at[n], features : 2 * features] = along_w
        kept.joined[at[n], 2 * features : 3 * features] = along_h
    weights_of()
    up_bias = hidden_bias(ins.up_bias, layer, ins.place)
    found = mlp_rows(
        ins.stream[...],
        kept.joined[...],
        weights[0],
        ins.layer_gain[layer : layer + 1, :],
        weights[1],
        up_bias,
        weights[2],
        side,
    )
    for name in KEPT:
        to = getattr(kept, name)
        to[...] = getattr(found, name).astype(to.dtype)
    for n in range(images):
        on_result(n, found.result[at[n]])
    squares = found.squares
    return center, inv_std, squares


def stage_backward(
    layer, place, grad_of, center, inv_std, conv, par, weights, kept, gb, gu, small, rows_ref, outs,
    dp, *, images, side,
):
    rows = side * WIDE
    features = gb.shape[1]
    grad_low, gpre, gc = rows_ref
    found = backward_rows(
        grad_of(),
        kept.uhat[...],
        kept.inv_norm[...],
        kept.slope[...].astype(F32),
        weights[0],
        par.layer_gain[layer : layer + 1, :],
        weights[1],
        weights[2],
    )
    grad_low[...] = found.grad_low
    gpre[...] = found.gpre
    gc[...] = found.gc
    gu[...] = found.gu.astype(gu.dtype)
    gain, bias = found.gain, found.bias
    offset = scale = cross = None
    for n in range(images):
        at = slice(n * rows, (n + 1) * rows)
        back, pairs = backward_mixes(found.gj[at], kept.joined[at, 0:features], par.mixing_back[...])
        gb[at, :] = back.astype(gb.dtype)
        offset = add_up(offset, jnp.sum(back, axis=0, keepdims=True))
        ahat = (conv[at, :] - center) * inv_std
        scale = add_up(scale, jnp.sum(back * ahat, axis=0, keepdims=True))
        cross = add_up(cross, pairs)
    small[NORM_ROW[layer] : NORM_ROW[layer] + 1, 0:features] = gain
    groups = par.up_bias.shape[1]
    width = bias.shape[1] // groups
    for j in range(groups):
        small[pl.ds(BIAS_ROW[layer] + (place[0] ^ j), 1), 0:width] = bias[:, j * width : (j + 1) * width]
    wide, tall = mixing_grads(cross, side)
    mixes = slice(layer * WIDE, (layer + 1) * WIDE)
    small[mixes, features : features + WIDE] = wide
    small[mixes, features + WIDE : features + 2 * WIDE] = tall
    unite_grad = dot_rows(kept.joined[...], gc[...])
    normal = (kept.uhat[...] * par.layer_gain[layer : layer + 1, :]).astype(BF16)
    up_grad = dot_rows(normal, gpre[...])
    down_grad = dot_rows(grad_low[...], kept.hidden[...])
    pack_grads(unite_grad, up_grad, down_grad, place[1], outs, dp)
    return offset, scale


def first_body(ins, outs, tmp, *, images, side):
    place, taps = ins.place, ins.taps
    own, conv, moments = outs.own, outs.conv, outs.moments
    every = tmp.every
    rows = side * WIDE
    by_image(ins.stream, every)
    for n in range(images):
        own[n * rows : (n + 1) * rows, :] = every[place[0] * images + n]
    for n in range(images):
        at = slice(n * rows, (n + 1) * rows)
        conv[at, :] = convolve(own[at, :], taps[:, 0, :], side)
    local_moments(conv, moments, images, side)


def other_body(ins, outs, tmp, *, images, side):
    rows = side * WIDE
    by_image(ins.cotangent, tmp.every)
    for n in range(images):
        outs.cotangent[n * rows : (n + 1) * rows, :] = tmp.every[ins.place[0] * images + n]
    _, groups, width = outs.up_bias.shape
    for j in range(groups):
        outs.up_bias[:, j, :] = ins.up_bias[:, j * width : (j + 1) * width]
    mixes = ins.mix_w[...].astype(F32), ins.mix_h[...].astype(F32)
    for layer in range(ins.mix_w.shape[1]):
        outs.mixing[layer][...], outs.mixing_back[layer][...] = mixing_matrices(
            *(mix[:, layer, :].astype(BF16) for mix in mixes), side
        )


def middle_body(ins, outs, tmp, *, images, side):
    rows = side * WIDE
    weights = tmp.unite, tmp.up, tmp.down
    results = []

    def weights_of():
        unpack_weights(tmp, *weights)

    center, inv_std, squares = stage_forward(
        0, ins, weights, weights_of, outs, lambda n, result: results.append(result), images=images, side=side
    )
    outs.stats[0:1, :] = center
    outs.stats[1:2, :] = inv_std
    outs.squares[...] = squares
    for n, result in enumerate(results):
        at = slice(n * rows, (n + 1) * rows)
        outs.stream1[at, :] = result
        outs.conv1[at, :] = convolve(result, ins.taps[:, 1, :], side)
    local_moments(outs.conv1, outs.moments1, images, side)


def last_body(ins, outs, tmp, *, images, side, dp):
    weights = tmp.unite, tmp.up, tmp.down
    results = []

    def weights_of():
        unpack_weights(tmp, *weights)

    center, inv_std, squares = stage_forward(
        1, ins, weights, weights_of, tmp, lambda n, result: results.append(result), images=images, side=side
    )
    outs.result[...] = pack_image_rows(jnp.concatenate(results, axis=0), side).astype(BF16)
    outs.stats[0:1, :] = center
    outs.stats[1:2, :] = inv_std
    outs.small[...] = jnp.zeros_like(outs.small)
    offset, scale = stage_backward(
        1, ins.place, lambda: ins.cotangent[...], center, inv_std,
        ins.conv, ins, weights, tmp, outs.gb, outs.gu, outs.small,
        (tmp.grad_low, tmp.gpre, tmp.gc), outs, dp, images=images, side=side,
    )
    features = squares.shape[1]
    outs.small[SQUARES_ROW[1] : SQUARES_ROW[1] + 3, 0:features] = squares
    to_all(outs.sums, 0, offset)
    to_all(outs.sums, 1, scale)


def conv_back(layer, sums, gb, gu, conv, stats, par, totals, *, images, side):
    rows = side * WIDE
    features = gb.shape[1]
    cells = images * side * side * sums.shape[0]
    offset = jnp.sum(sums[:, 0, 0:features], axis=0, keepdims=True)
    scale = jnp.sum(sums[:, 1, 0:features], axis=0, keepdims=True)
    totals[0:1, :] = offset
    totals[1:2, :] = scale
    center, inv_std = stats[0:1, :], stats[1:2, :]
    factor = par.batch_gain[layer : layer + 1, :] * inv_std
    found = []
    for n in range(images):
        at = slice(n * rows, (n + 1) * rows)
        found.append(
            conv_back_image(
                gb[at, :].astype(F32),
                (conv[at, :] - center) * inv_std,
                gu[at, :].astype(F32),
                factor,
                offset / cells,
                scale / cells,
                par.taps[:, layer, :],
                side,
            )
        )
    return found


def taps_body(ins, outs, tmp, *, images, side):
    rows = side * WIDE
    center, inv_std = ins.stats[0:1, :], ins.stats[1:2, :]
    plain = scaled = None
    for n in range(images):
        at = slice(n * rows, (n + 1) * rows)
        stream = ins.stream[at, :]
        valid = valid_rows(rows, side)
        ones = jnp.where(valid, jnp.ones_like(stream), 0.0)
        ahat = jnp.where(valid, (ins.conv[at, :] - center) * inv_std, 0.0)
        plain = add_up(plain, tap_sums(ones, stream))
        scaled = add_up(scaled, tap_sums(ahat, stream))
    outs.plain[...] = plain
    outs.scaled[...] = scaled


def between_body(ins, outs, tmp, *, images, side, dp):
    weights = tmp.unite, tmp.up, tmp.down
    unpack_weights(tmp, *weights)
    rows = side * WIDE
    features = ins.gb1.shape[1]
    small, sums = tmp.small, outs.sums
    small[...] = ins.small[...]
    grads, kernel = [], None
    found = conv_back(
        1, ins.sums1, ins.gb1, ins.gu1, ins.conv1, ins.stats1, ins, outs.totals1, images=images, side=side
    )
    for n, (grad, ga) in enumerate(found):
        grads.append(grad)
        kernel = add_up(kernel, tap_sums(ga, ins.stream1[n * rows : (n + 1) * rows, :]))
    small[TAPS_ROW : TAPS_ROW + 9, 0:features] = kernel
    stats = ins.stats0
    offset, scale = stage_backward(
        0, ins.place, lambda: jnp.concatenate(grads, axis=0), stats[0:1, :], stats[1:2, :], ins.conv0, ins, weights, ins,
        tmp.gb, tmp.gu, small, (tmp.grad_low, tmp.gpre, tmp.gc), outs, dp,
        images=images, side=side,
    )
    kernel = None
    for n in range(images):
        at = slice(n * rows, (n + 1) * rows)
        kernel = add_up(kernel, tap_sums(tmp.gb[at, :], ins.stream0[at, :]))
    for k, values in enumerate((kernel, ins.plain[...], ins.scaled[...])):
        small[9 * k : 9 * k + 9, 0:features] = values
    small[SQUARES_ROW[0] : SQUARES_ROW[0] + 3, 0:features] = ins.squares0[...]
    cells = images * side * side
    center, inv_std = stats[0:1, :], stats[1:2, :]
    grads = []
    for n in range(images):
        at = slice(n * rows, (n + 1) * rows)
        ahat = (ins.conv0[at, :] - center) * inv_std
        factor = ins.batch_gain[0:1, :] * inv_std
        grad, _ = conv_back_image(
            tmp.gb[at, :], ahat, tmp.gu[at, :], factor, offset / cells, scale / cells, ins.taps[:, 0, :], side
        )
        grads.append(grad)
    outs.grad[...] = pack_image_rows(jnp.concatenate(grads, axis=0), side).astype(BF16)
    to_all(sums, 0, offset)
    to_all(sums, 1, scale)
    devices, height, _ = sums.shape
    for g in range(height - 2):
        held = min(devices, SMALL_ROWS - g * devices)
        sums[0:held, 2 + g, :] = small[g * devices : g * devices + held, :]
        if held < devices:
            sums[held:, 2 + g, :] = jnp.zeros((devices - held, SMALL_WIDE), F32)


def final_body(ins, outs, tmp, *, images, side):
    held, rows, features = tmp.every.shape
    sums = ins.sums0
    cells = images * side * side
    devices = sums.shape[0]
    group = held // images
    offset = jnp.sum(sums[:, 0, 0:features], axis=0, keepdims=True)
    scale = jnp.sum(sums[:, 1, 0:features], axis=0, keepdims=True)
    for row, total in enumerate((offset, scale)):
        to = (outs.offset_grad, outs.scale_grad)[row]
        to[0:1, :] = total
        to[1:2, :] = ins.totals1[row : row + 1, :]
    center, inv_std = ins.stats0[0:1, :], ins.stats0[1:2, :]
    factor = ins.batch_gain[0:1, :] * inv_std
    first = ins.place[1] * group

    def apart(row, total):
        own = [sums[first + p, row : row + 1, 0:features] for p in range(group)]
        own = jnp.concatenate([value for value in own for _ in range(images)], axis=0)
        return factor * (total / (cells * devices) - own / cells)

    shift, slant = apart(0, offset), apart(1, scale)
    put_images(ins.place[0], ins.parts, tmp.every, images, side)
    padded, fields = tmp.padded, tmp.fields
    for ref in (padded, fields):
        edge = jnp.zeros((1,) + ref.shape[1:], F32)
        ref[0:1] = edge
        ref[side + 1 : side + 2] = edge
        edge = jnp.zeros((side, 1) + ref.shape[2:], F32)
        ref[1 : side + 1, 0:1] = edge
        ref[1 : side + 1, side + 1 : side + 2] = edge
    padded[1 : side + 1, 1 : side + 1] = ins.stream[...]
    taps = ins.taps[:, 0, :]
    for h in range(side):
        conv = None
        for i in range(3):
            for j in range(3):
                term = padded[h + i, j : j + side] * taps[3 * i + j : 3 * i + j + 1]
                conv = add_up(conv, term)
        fields[h + 1, 1 : side + 1] = shift + (conv - center) * inv_std * slant
    for h in range(side):
        lines = jnp.swapaxes(tmp.every[:, h * WIDE : (h + 1) * WIDE, :], 0, 1)[:side]
        for i in range(3):
            for j in range(3):
                lines = lines - fields[h + 2 - i, 2 - j : 2 - j + side] * taps[3 * i + j : 3 * i + j + 1]
        outs.out[h] = lines


def put_images(place, parts, every, images, side):
    features = every.shape[2]
    for j, part in enumerate(parts):
        packed = part[...].astype(F32)
        lines = packed.shape[0] // side
        for half in range(2):
            values = packed[:, half * features : (half + 1) * features]
            for k in range(lines):
                n, h = divmod(half * lines + k, side)
                every[(place ^ j) * images + n, h * WIDE : h * WIDE + side, :] = values[
                    k * side : (k + 1) * side
                ]


def gather_body(ins, outs, tmp):
    for g in range(outs.message.shape[1]):
        to_all(outs.message, g, jnp.sum(ins.sums0[:, 2 + g, :], axis=0, keepdims=True))


def spread_body(ins, outs, tmp, *, images, side):
    put_images(ins.place[0], ins.parts, tmp.every, images, side)
    for h in range(side):
        outs.out[h] = jnp.swapaxes(tmp.every[:, h * WIDE : (h + 1) * WIDE, :], 0, 1)[:side]


def core_body(ins, outs, tmp):
    apart = isinstance(outs.parts, list)
    for k in range(ins.keep.shape[0]):
        at = (ins.place[1] >> 1) ^ k if apart else k
        to = outs.parts[k] if apart else outs.parts.at[k]
        to[...] = (ins.keep[at].astype(F32) + ins.got[at].astype(F32)).astype(BF16)


def chips_body(ins, outs, tmp):
    groups = len(outs.give)
    for layer, parts in enumerate(ins.parts):
        parts = parts if isinstance(parts, list) else [parts.at[k] for k in range(parts.shape[0])]
        total = parts[0][...].astype(F32)
        for other in parts[1:]:
            total = total + other[...].astype(F32)
        part = total.shape[0] // 3
        width = total.shape[1] // groups
        features = outs.give[0].shape[2] - 2 * width
        for j in range(groups):
            block = jnp.concatenate(
                [
                    total[:part, j * width : (j + 1) * width],
                    total[part : 2 * part, j * width : (j + 1) * width],
                    *[
                        total[2 * part :, q * SMALL_WIDE : q * SMALL_WIDE + features // 3]
                        for q in range(3)
                    ],
                ],
                axis=1,
            )
            outs.give[j][layer] = block.astype(BF16)


def weights_body(ins, outs, tmp):
    layers = outs.up_grad.shape[0]
    for layer in range(layers):
        terms = [ref[layer].astype(F32) for ref in ins.got]
        while len(terms) > 1:
            terms = [terms[j] + terms[j + 1] for j in range(0, len(terms), 2)]
        total = terms[0]
        width = outs.up_grad.shape[2]
        features = outs.unite_grad.shape[1]
        outs.up_grad[layer] = total[:, :width]
        outs.down_grad[layer] = total[:, width : 2 * width]
        rest = total[:, 2 * width :]
        rows = jnp.concatenate([rest[:, q * features : (q + 1) * features] for q in range(3)], axis=0)
        outs.unite_grad[layer] = rows.T


def small_body(ins, outs, tmp, *, side, cells, entries):
    got = ins.got
    features = outs.gain_grad.shape[1]
    devices, height, _ = got.shape
    values = tmp.values
    for g in range(height):
        values[g * devices : (g + 1) * devices, :] = got[:, g, :]
    factor = ins.batch_gain[0:1, :] * ins.stats0[1:2, :]
    first = factor * (
        values[0:9, 0:features]
        - ins.offset[0:1, :] / cells * values[9:18, 0:features]
        - ins.scale[0:1, :] / cells * values[18:27, 0:features]
    )
    for k in range(9):
        outs.kernel_grad[k, 0:1, :] = first[k : k + 1]
        outs.kernel_grad[k, 1:2, :] = values[TAPS_ROW + k : TAPS_ROW + k + 1, 0:features]
    width = outs.bias_grad.shape[1]
    for layer in range(2):
        outs.gain_grad[layer : layer + 1, :] = values[NORM_ROW[layer] : NORM_ROW[layer] + 1, 0:features]
        outs.bias_grad[layer : layer + 1, :] = values[pl.ds(BIAS_ROW[layer] + ins.place[0], 1), 0:width]
        rows = slice(layer * WIDE, layer * WIDE + side)
        outs.width_grad[:, layer, :] = values[rows, features : features + side]
        outs.height_grad[:, layer, :] = values[rows, features + WIDE : features + WIDE + side]
        squares = values[SQUARES_ROW[layer] : SQUARES_ROW[layer] + 3, 0:features]
        outs.stream_rms[:, layer : layer + 1] = jnp.sqrt(
            jnp.sum(squares, axis=1, keepdims=True) / entries
        )


def call(body, ins, outs, scratch=None, shards=(), micros=0, vmem=VMEM_LIMIT, **static):
    ins = dict(ins, shards=list(shards))
    operands, in_tree = jax.tree.flatten(ins)
    shapes, out_tree = jax.tree.flatten(
        {name: jax.tree.map(lambda shape: jax.ShapeDtypeStruct(*shape), outs[name], is_leaf=is_shape) for name in outs}
    )
    scratch = dict(scratch or {})
    if shards:
        scratch["packed"] = (len(shards),) + shards[0].shape, shards[0].dtype
    tmp_names = list(scratch)

    def kernel(*refs):
        cut = len(operands), len(operands) + len(shapes)
        given = SimpleNamespace(**jax.tree.unflatten(in_tree, refs[: cut[0]]))
        results = SimpleNamespace(**jax.tree.unflatten(out_tree, refs[cut[0] : cut[1]]))
        tmp = SimpleNamespace(**dict(zip(tmp_names, refs[cut[1] :])))
        for k, shard in enumerate(given.shards):
            tmp.packed[given.place[1] ^ k] = shard[...]
        body(given, results, tmp, **static)

    def space(name):
        return pl.BlockSpec(memory_space=pltpu.SMEM if name == "place" else pltpu.VMEM)

    found = pl.pallas_call(
        kernel,
        out_shape=shapes,
        in_specs=jax.tree.leaves({name: jax.tree.map(lambda _: space(name), ins[name]) for name in ins}),
        out_specs=[space("")] * len(shapes),
        scratch_shapes=[pltpu.VMEM(*scratch[name]) for name in tmp_names],
        compiler_params=pltpu.CompilerParams(vmem_limit_bytes=vmem),
        cost_estimate=pl.CostEstimate(
            flops=int(micros * COST_FLOPS), transcendentals=0, bytes_accessed=int(micros * COST_BYTES)
        ),
    )(*operands)
    return SimpleNamespace(**jax.tree.unflatten(out_tree, found))


def is_shape(value):
    return isinstance(value, tuple)


def swap(values, axis, mask):
    return lax.ppermute(values, axis, [(i, i ^ mask) for i in range(lax.axis_size(axis))])


def after(values, *others):
    return lax.optimization_barrier((values, others))[0]


def per_device(
    inputs,
    conv_weight,
    batch_gain,
    batch_bias,
    mix_width,
    mix_height,
    unite_weight,
    layer_gain,
    up_weight,
    up_bias,
    down_weight,
    cotangent,
):
    held, side, _, features = inputs.shape
    layers = conv_weight.shape[0]
    dp, mp = lax.axis_size("dp"), lax.axis_size("mp")
    devices = dp * mp
    images = held // mp
    cells = side * WIDE
    rows = images * cells
    units = up_bias.shape[1]
    part = features // dp
    both = ("dp", "mp")
    sizes = dict(images=images, side=side)
    place = jnp.stack([lax.axis_index("mp"), lax.axis_index("dp")]).astype(jnp.int32)

    def group_parts(values):
        if isinstance(values, (list, tuple)):
            return [swap(value, "mp", j) if j else value for j, value in enumerate(values)]
        parts = [values]
        for j in range(1, mp):
            step = j & -j
            parts.append(swap(parts[j ^ step], "mp", step))
        return parts

    def share(blocks):
        return lax.all_to_all(blocks, both, 0, 0, tiled=False)

    maps = jnp.transpose(inputs, (1, 2, 0, 3))
    cotangent_maps = jnp.transpose(cotangent, (1, 2, 0, 3))
    taps = jnp.transpose(conv_weight, (1, 0, 2))
    mix_w, mix_h = (jnp.transpose(mix, (1, 0, 2)) for mix in (mix_width, mix_height))
    shared = (devices, 2, features)
    thirds = unite_weight.reshape(layers, 3, part, features)
    beside = [(0, 0), (0, 0), (0, SMALL_WIDE - features)]
    thirds = jnp.concatenate([jnp.pad(thirds[:, q], beside) for q in range(3)], axis=2)
    thirds = jnp.pad(thirds, ((0, 0), (0, 0), (0, units - 3 * SMALL_WIDE)))

    def widen(wide, step):
        return jnp.concatenate([wide, swap(wide, "mp", step)], axis=1)

    def over_dp(layer, wide, wait_chips, wait_core):
        piece = after(jnp.concatenate([wide, thirds[layer]], axis=0), *wait_chips)
        shards = [piece] + [swap(piece, "dp", 2 * k) for k in range(1, dp // 2)]
        mates = [swap(after(shard, *wait_core), "dp", 1) for shard in shards]
        return [shard for pair in zip(shards, mates) for shard in pair]

    wide = jnp.concatenate([up_weight[0], down_weight[0]], axis=0)
    wide = near = widen(wide, 1) if mp > 1 else wide
    step = 2
    while step < mp:
        wide = widen(wide, step)
        step *= 2
    found = call(
        first_body,
        dict(place=after(place, near), stream=maps, taps=taps),
        dict(own=((rows, features), F32), conv=((rows, features), F32), moments=(shared, F32)),
        dict(every=((held, cells, features), F32)),
        micros=4,
        **sizes,
    )
    moments0 = share(after(found.moments, wide))
    other = call(
        other_body,
        dict(place=place, cotangent=cotangent_maps, mix_w=mix_w, mix_h=mix_h, up_bias=up_bias),
        dict(
            cotangent=((rows, features), F32),
            up_bias=((layers, mp, units // mp), F32),
            mixing=[((2 * cells, cells), BF16)] * layers,
            mixing_back=[((cells, 2 * cells), BF16)] * layers,
        ),
        dict(every=((held, cells, features), F32)),
        micros=3,
        **sizes,
    )

    packed = [over_dp(0, wide, (found.moments,), (moments0, other.mixing[0]))]
    wide = after(jnp.concatenate([up_weight[1], down_weight[1]], axis=0), wide)
    step = 1
    while step < mp:
        wide = widen(wide, step)
        step *= 2
    wide1 = wide

    own, conv0 = found.own, found.conv
    par = dict(
        place=place,
        taps=taps,
        batch_gain=batch_gain,
        batch_bias=batch_bias,
        layer_gain=layer_gain,
        up_bias=other.up_bias,
    )
    kept = dict(
        joined=((rows, 3 * features), BF16),
        uhat=((rows, features), F32),
        inv_norm=((rows, 1), F32),
        slope=((rows, units), BF16),
        hidden=((rows, units), BF16),
    )
    weight_tmp = dict(
        unite=((3 * features, features), BF16),
        up=((features, units), BF16),
        down=((features, units), BF16),
    )
    back_tmp = dict(
        grad_low=((rows, features), BF16), gpre=((rows, units), BF16), gc=((rows, features), BF16)
    )
    back_outs = dict(gb=((rows, features), F32), gu=((rows, features), F32))
    stats = ((2, features), F32)
    pieces = [((dp // 2, 3 * part, units), BF16)] * 2
    piece = ((3 * part, units), BF16)

    def over_core(values, apart=False):
        return call(
            core_body,
            dict(place=place, keep=values.keep, got=swap(values.give, "dp", 1)),
            dict(parts=[piece] * (dp // 2) if apart else pieces[0]),
            vmem=SMALL_LIMIT,
        ).parts

    def from_chips(parts):
        if isinstance(parts, list):
            return [swap(values, "dp", 2 * k) if k else values for k, values in enumerate(parts)]
        groups = [[2 * q + c for q in range(dp // 2)] for c in range(2)]
        return lax.all_to_all(parts, "dp", 0, 0, axis_index_groups=groups, tiled=False)

    mid = call(
        middle_body,
        dict(
            par,
            moments=moments0,
            conv=conv0,
            stream=own,
            mixing=other.mixing[0],
        ),
        dict(
            kept,
            stream1=((rows, features), F32),
            conv1=((rows, features), F32),
            moments1=(shared, F32),
            stats=stats,
            squares=((3, features), F32),
        ),
        weight_tmp,
        packed[0],
        micros=6,
        **sizes,
    )
    packed.append(over_dp(1, wide1, packed[0][::2], (mid.moments1,)))
    under = call(
        taps_body,
        dict(stream=own, conv=conv0, stats=mid.stats),
        dict(plain=((9, features), F32), scaled=((9, features), F32)),
        micros=2,
        **sizes,
    )
    last = call(
        last_body,
        dict(
            par,
            moments=after(share(mid.moments1), under.plain),
            conv=mid.conv1,
            stream=mid.stream1,
            mixing=other.mixing[1],
            mixing_back=other.mixing_back[1],
            cotangent=other.cotangent,
        ),
        dict(
            gb=((rows, features), BF16),
            gu=((rows, features), BF16),
            result=((images * side * side // 2, 2 * features), BF16),
            stats=stats,
            small=((SMALL_ROWS, SMALL_WIDE), F32),
            sums=(shared, F32),
            keep=pieces[0],
            give=pieces[1],
        ),
        dict(
            dict(kept, slope=((rows, units), F32)),
            **weight_tmp,
            **back_tmp,
        ),
        packed[1],
        micros=10,
        dp=dp,
        **sizes,
    )
    summed1 = over_core(last)
    groups = -(-SMALL_ROWS // devices)
    between = call(
        between_body,
        {
            **par,
            **{name: getattr(mid, name) for name in kept},
            **dict(
                sums1=after(share(last.sums), summed1),
                gb1=last.gb,
                gu1=last.gu,
                conv1=mid.conv1,
                stream1=mid.stream1,
                stats1=last.stats,
                small=last.small,
                stream0=own,
                plain=under.plain,
                scaled=under.scaled,
                conv0=conv0,
                stats0=mid.stats,
                squares0=mid.squares,
                mixing_back=other.mixing_back[0],
            ),
        },
        dict(
            grad=((images * side * side // 2, 2 * features), BF16),
            totals1=stats,
            sums=((devices, 2 + groups, SMALL_WIDE), F32),
            keep=pieces[0],
            give=pieces[1],
        ),
        dict(
            back_tmp,
            **back_outs,
            **weight_tmp,
            small=((SMALL_ROWS, SMALL_WIDE), F32),
        ),
        packed[0],
        micros=10,
        dp=dp,
        **sizes,
    )
    result_parts = [last.result] + [swap(last.result, "mp", 1 << k) for k in range((mp - 1).bit_length())]
    parts1 = from_chips(summed1)
    grad, sums0, give, parts1, near = lax.optimization_barrier(
        (between.grad, between.sums, between.give, parts1, result_parts[1:])
    )
    result_parts = [last.result]
    for j in range(1, mp):
        step = j & -j
        result_parts.append(near[j.bit_length() - 1] if j == step else swap(result_parts[j ^ step], "mp", step))
    sums0 = share(sums0)
    chunk = call(
        gather_body, dict(sums0=sums0), dict(message=((devices, groups, SMALL_WIDE), F32)), vmem=SMALL_LIMIT
    )
    shared_small = share(chunk.message)
    summed0 = over_core(SimpleNamespace(keep=between.keep, give=give), True)
    summed0 = after(summed0, result_parts)
    grad_parts = group_parts(after(grad, summed0))
    cut = call(
        chips_body,
        dict(parts=[from_chips(summed0), parts1]),
        dict(give=[((layers, part, 2 * (units // mp) + 3 * features), BF16)] * mp),
        vmem=SMALL_LIMIT,
    ).give
    grads = call(
        weights_body,
        dict(got=group_parts(after(cut, grad_parts, shared_small))),
        dict(
            up_grad=((layers, part, units // mp), F32),
            down_grad=((layers, part, units // mp), F32),
            unite_grad=((layers, features, 3 * part), F32),
        ),
        vmem=SMALL_LIMIT,
    )
    whole_maps = ((side, side, held, features), F32)
    output = call(
        spread_body,
        dict(place=place, parts=result_parts),
        dict(out=whole_maps),
        dict(every=((held, cells, features), F32)),
        **sizes,
    ).out
    padded = ((side + 2, side + 2, held, features), F32)
    end = call(
        final_body,
        dict(
            place=place,
            parts=grad_parts,
            stream=maps,
            sums0=sums0,
            totals1=between.totals1,
            stats0=mid.stats,
            batch_gain=batch_gain,
            taps=taps,
        ),
        dict(out=whole_maps, offset_grad=stats, scale_grad=stats),
        dict(every=((held, cells, features), F32), padded=padded, fields=padded),
        **sizes,
    )
    outputs = [jnp.transpose(out, (2, 0, 1, 3)) for out in (output, end.out)]
    small = call(
        small_body,
        dict(
            place=place,
            got=shared_small,
            batch_gain=batch_gain,
            stats0=mid.stats,
            offset=end.offset_grad,
            scale=end.scale_grad,
        ),
        dict(
            kernel_grad=((9, layers, features), F32),
            gain_grad=((layers, features), F32),
            bias_grad=((layers, units // mp), F32),
            width_grad=((side, layers, side), F32),
            height_grad=((side, layers, side), F32),
            stream_rms=((3, layers), F32),
        ),
        dict(values=((groups * devices, SMALL_WIDE), F32)),
        vmem=SMALL_LIMIT,
        side=side,
        cells=images * side * side * devices,
        entries=held * side * side * features * dp,
    )
    return (
        *outputs,
        jnp.transpose(small.kernel_grad, (1, 0, 2)),
        end.scale_grad,
        end.offset_grad,
        jnp.transpose(small.width_grad, (1, 0, 2)),
        jnp.transpose(small.height_grad, (1, 0, 2)),
        jnp.transpose(grads.unite_grad, (0, 2, 1)),
        small.gain_grad,
        grads.up_grad,
        small.bias_grad,
        grads.down_grad,
        small.stream_rms.T,
    )


def solution(mesh):
    in_specs = (
        P("dp", None, None, None),
        P(),
        P(),
        P(),
        P(),
        P(),
        P(None, "dp", None),
        P(),
        P(None, "dp", "mp"),
        P(),
        P(None, "dp", "mp"),
        P("dp", None, None, None),
    )
    out_specs = (
        P("dp", None, None, None),
        P("dp", None, None, None),
        P(),
        P(),
        P(),
        P(),
        P(),
        P(None, "dp", None),
        P(),
        P(None, "dp", "mp"),
        P(None, "mp"),
        P(None, "dp", "mp"),
        P(),
    )
    return jax.shard_map(
        per_device, mesh=mesh, in_specs=in_specs, out_specs=out_specs, check_vma=False
    )
```

```python
import functools
from types import SimpleNamespace

import jax
import jax.numpy as jnp
from jax import lax
from jax.experimental import pallas as pl
from jax.experimental.pallas import tpu as pltpu
from jax.sharding import PartitionSpec as P

EPSILON = 1e-05
WIDE = 16
VMEM_LIMIT = 58 * 1024 * 1024
SMALL_LIMIT = 14 * 1024 * 1024
COST_BYTES = 3.0e6
COST_FLOPS = 1.0e10
F32 = jnp.float32
BF16 = jnp.bfloat16


def dot(left, right):
    return lax.dot_general(left, right, (((1,), (0,)), ((), ())), preferred_element_type=F32)


def dot_cols(left, right):
    return lax.dot_general(left, right, (((1,), (1,)), ((), ())), preferred_element_type=F32)


def dot_rows(left, right):
    return lax.dot_general(left, right, (((0,), (0,)), ((), ())), preferred_element_type=F32)


def valid_rows(rows, side):
    return lax.broadcasted_iota(jnp.int32, (rows, 1), 0) % WIDE < side


def three_shifts(image):
    rows, features = image.shape
    empty = jnp.zeros((WIDE, features), image.dtype)
    padded = jnp.concatenate([empty, image, empty], axis=0)
    total = rows + 2 * WIDE
    return pltpu.roll(padded, 1, 0), padded, pltpu.roll(padded, total - 1, 0)


def convolve(image, taps, side):
    rows = image.shape[0]
    shifted = three_shifts(image)
    summed = None
    for i in range(3):
        for j in range(3):
            term = shifted[j][WIDE * i : WIDE * i + rows] * taps[3 * i + j : 3 * i + j + 1]
            summed = term if summed is None else summed + term
    return jnp.where(valid_rows(rows, side), summed, 0.0)


def to_all(message_ref, row, values):
    devices = message_ref.shape[0]
    message_ref[:, row, 0 : values.shape[1]] = jnp.broadcast_to(values, (devices, values.shape[1]))


def local_moments(conv_ref, moments_ref, images, side):
    rows = side * WIDE
    count = images * side * side
    total = None
    for n in range(images):
        part = jnp.sum(conv_ref[n * rows : (n + 1) * rows, :], axis=0, keepdims=True)
        total = part if total is None else total + part
    mean = total / count
    squares = None
    for n in range(images):
        deviate = jnp.where(
            valid_rows(rows, side), conv_ref[n * rows : (n + 1) * rows, :] - mean, 0.0
        )
        part = jnp.sum(deviate * deviate, axis=0, keepdims=True)
        squares = part if squares is None else squares + part
    to_all(moments_ref, 0, mean)
    to_all(moments_ref, 1, squares)


def whole_moments(gathered_ref, count):
    devices = gathered_ref.shape[0]
    means = gathered_ref[:, 0, :]
    squares = gathered_ref[:, 1, :]
    center = jnp.sum(means, axis=0, keepdims=True) / devices
    apart = means - center
    spread = (
        jnp.sum(squares, axis=0, keepdims=True)
        + jnp.sum(apart * apart, axis=0, keepdims=True) * count
    ) / (count * devices)
    return center, lax.rsqrt(spread + EPSILON)


def mixing_matrices(mix_w, mix_h, side):
    cells = side * WIDE
    row = lax.broadcasted_iota(jnp.int32, (cells, side), 0)
    col = lax.broadcasted_iota(jnp.int32, (cells, side), 1)
    at_w = (row % WIDE == col).astype(BF16)
    at_h = (row // WIDE == col).astype(BF16)
    out = lax.broadcasted_iota(jnp.int32, (cells, cells), 0)
    inp = lax.broadcasted_iota(jnp.int32, (cells, cells), 1)
    same_h = out // WIDE == inp // WIDE
    same_w = (out % WIDE == inp % WIDE) & (out % WIDE < side)

    def spread(picks, mix, keep, flip):
        left = (dot_cols if flip else dot)(picks, mix).astype(BF16)
        return jnp.where(keep, dot_cols(left, picks), 0.0).astype(BF16)

    forward = jnp.concatenate(
        [spread(at_w, mix_w, same_h, False), spread(at_h, mix_h, same_w, False)], axis=0
    )
    backward = jnp.concatenate(
        [spread(at_w, mix_w, same_h, True), spread(at_h, mix_h, same_w, True)], axis=1
    )
    return forward, backward


def by_image(maps_ref, all_ref):
    side, _, held, features = maps_ref.shape
    empty = jnp.zeros((WIDE - side, held, features), F32)
    for h in range(side):
        lines = jnp.concatenate([maps_ref[h], empty], axis=0)
        all_ref[:, h * WIDE : (h + 1) * WIDE, :] = jnp.swapaxes(lines, 0, 1)


def unpack_weights(tmp, unite_ref, up_ref, down_ref):
    packed_ref = tmp.packed
    shards, height, _ = packed_ref.shape
    part = height // 3
    features = unite_ref.shape[1]
    ups, downs, unites = [], [], []
    for s in range(shards):
        piece = packed_ref[s].astype(F32)
        ups.append(piece[:part])
        downs.append(piece[part : 2 * part])
        for q in range(3):
            unites.append(piece[2 * part :, q * SMALL_WIDE : q * SMALL_WIDE + features])
    up_ref[...] = jnp.concatenate(ups, axis=0).astype(BF16)
    down_ref[...] = jnp.concatenate(downs, axis=0).astype(BF16)
    unite_ref[...] = jnp.concatenate(unites, axis=0).astype(BF16)


def pack_grads(unite, up, down, mine, outs, dp):
    features = up.shape[0]
    part = features // dp
    beside = jnp.zeros((part, SMALL_WIDE - features), F32)
    filler = jnp.zeros((part, up.shape[1] - 3 * SMALL_WIDE), F32)

    def piece(s):
        columns = []
        for q in range(3):
            columns += [unite[(3 * s + q) * part : (3 * s + q + 1) * part], beside]
        return jnp.concatenate(
            [
                up[s * part : (s + 1) * part],
                down[s * part : (s + 1) * part],
                jnp.concatenate(columns + [filler], axis=1),
            ],
            axis=0,
        )

    first = (mine & 1) == 0
    for k in range(dp // 2):
        pair = piece(2 * k), piece(2 * k + 1)
        outs.keep[k] = jnp.where(first, pair[0], pair[1]).astype(BF16)
        outs.give[k] = jnp.where(first, pair[1], pair[0]).astype(BF16)


def pack_image_rows(values, side):
    lines = [values[r : r + side] for r in range(0, values.shape[0], WIDE)]
    half = len(lines) // 2
    return jnp.concatenate(
        [jnp.concatenate(lines[:half], axis=0), jnp.concatenate(lines[half:], axis=0)], axis=1
    )


def hidden_bias(up_bias_ref, layer, place_ref):
    groups = up_bias_ref.shape[1]
    blocks = [up_bias_ref[layer, pl.ds(place_ref[0] ^ j, 1), :] for j in range(groups)]
    return jnp.concatenate(blocks, axis=1)


def mix_image(conv, center, inv_std, bn_gain, bn_bias, mixing, side):
    rows = conv.shape[0]
    ahat = (conv - center) * inv_std
    branch = jnp.where(valid_rows(rows, side), ahat * bn_gain + bn_bias, 0.0).astype(BF16)
    along = dot(mixing, branch).astype(BF16)
    return branch, along[:rows], along[rows:]


def mlp_rows(stream, joined, unite_ref, norm_gain, up_ref, up_bias, down_ref, side):
    rows, features = stream.shape
    united = dot(joined, unite_ref[...])
    resid = stream + united
    mid = jnp.sum(resid, axis=-1, keepdims=True) / features
    deviate = resid - mid
    spread = jnp.sum(deviate * deviate, axis=-1, keepdims=True) / features
    inv_norm = lax.rsqrt(spread + EPSILON)
    uhat = deviate * inv_norm
    normal = (uhat * norm_gain).astype(BF16)
    pre = dot(normal, up_ref[...]) + up_bias
    below = 0.5 + 0.5 * lax.erf(pre * (0.5**0.5))
    slope = below + pre * (jnp.exp(-0.5 * pre * pre) * 0.3989422804014327)
    hidden = (pre * below).astype(BF16)
    mlp = jnp.where(valid_rows(rows, side), dot_cols(hidden, down_ref[...]), 0.0)
    result = resid + mlp
    squares = jnp.concatenate(
        [jnp.sum(v * v, axis=0, keepdims=True) for v in (united, mlp, result)], axis=0
    )
    return SimpleNamespace(
        uhat=uhat,
        inv_norm=inv_norm,
        slope=slope,
        hidden=hidden,
        result=result,
        squares=squares,
    )


def backward_rows(grad, uhat, inv_norm, slope, unite_ref, norm_gain, up_ref, down_ref):
    features = grad.shape[1]
    grad_low = grad.astype(BF16)
    gh = dot(grad_low, down_ref[...])
    gpre = (gh * slope).astype(BF16)
    bias = jnp.sum(gpre.astype(F32), axis=0, keepdims=True)
    gn = dot_cols(gpre, up_ref[...])
    gain = jnp.sum(gn * uhat, axis=0, keepdims=True)
    q = gn * norm_gain
    mean_q = jnp.sum(q, axis=-1, keepdims=True) / features
    mean_qu = jnp.sum(q * uhat, axis=-1, keepdims=True) / features
    gu = grad + inv_norm * (q - mean_q - uhat * mean_qu)
    gc = gu.astype(BF16)
    return SimpleNamespace(
        grad_low=grad_low, gpre=gpre, bias=bias, gain=gain, gu=gu, gc=gc, gj=dot_cols(gc, unite_ref[...])
    )


def backward_mixes(gj, branch, mixing_back):
    features = branch.shape[1]
    both = jnp.concatenate([gj[:, features : 2 * features], gj[:, 2 * features :]], axis=0).astype(BF16)
    return gj[:, :features] + dot(mixing_back, both), dot_cols(both, branch)


def mixing_grads(cross, side):
    cells = side * WIDE
    out = lax.broadcasted_iota(jnp.int32, (cells, cells), 0)
    inp = lax.broadcasted_iota(jnp.int32, (cells, cells), 1)
    width = jnp.where(out // WIDE == inp // WIDE, cross[:cells], 0.0)
    height = jnp.where(out % WIDE == inp % WIDE, cross[cells:], 0.0)
    across, down = None, []
    for v in range(side):
        at = slice(v * WIDE, (v + 1) * WIDE)
        across = add_up(across, width[at])
        down.append(jnp.sum(height[at], axis=0, keepdims=True))
    down = jnp.concatenate(down + [jnp.zeros((WIDE - side, cells), F32)], axis=0)
    parts = []
    for values in (across, down):
        high = values.astype(BF16)
        parts += [high, (values - high.astype(F32)).astype(BF16)]
    row = lax.broadcasted_iota(jnp.int32, (cells, 2 * WIDE), 0)
    col = lax.broadcasted_iota(jnp.int32, (cells, 2 * WIDE), 1)
    picks = (col == jnp.where(col < WIDE, row % WIDE, row // WIDE + WIDE)).astype(BF16)
    sums = dot(jnp.concatenate(parts, axis=0), picks)
    sums = sums[: 2 * WIDE, :WIDE], sums[2 * WIDE :, WIDE:]
    return tuple(value[:WIDE] + value[WIDE:] for value in sums)


def tap_sums(values, stream):
    rows = values.shape[0]
    shifted = three_shifts(stream)
    return jnp.concatenate(
        [
            jnp.sum(values * shifted[j][WIDE * i : WIDE * i + rows], axis=0, keepdims=True)
            for i in range(3)
            for j in range(3)
        ],
        axis=0,
    )


def conv_back_image(gb, ahat, gu, factor, offset_mean, scale_mean, taps, side):
    rows = gb.shape[0]
    valid = valid_rows(rows, side)
    ga = jnp.where(valid, factor * (gb - offset_mean - ahat * scale_mean), 0.0)
    turned = three_shifts(ga)
    summed = gu
    for i in range(3):
        for j in range(3):
            summed = (
                summed
                + turned[2 - j][WIDE * (2 - i) : WIDE * (2 - i) + rows]
                * taps[3 * i + j : 3 * i + j + 1]
            )
    return jnp.where(valid, summed, 0.0), ga


def add_up(total, part):
    return part if total is None else total + part


SMALL_ROWS, SMALL_WIDE = 60, 384
NORM_ROW, SQUARES_ROW, BIAS_ROW, TAPS_ROW = (27, 48), (28, 49), (31, 52), 39
KEPT = ("uhat", "inv_norm", "slope", "hidden")


def stage_forward(layer, ins, weights, weights_of, kept, on_result, *, images, side):
    rows = side * WIDE
    at = [slice(n * rows, (n + 1) * rows) for n in range(images)]
    center, inv_std = whole_moments(ins.moments, images * side * side)
    for n in range(images):
        branch, along_w, along_h = mix_image(
            ins.conv[at[n], :],
            center,
            inv_std,
            ins.batch_gain[layer : layer + 1, :],
            ins.batch_bias[layer : layer + 1, :],
            ins.mixing[...],
            side,
        )
        features = branch.shape[1]
        kept.joined[at[n], 0:features] = branch
        kept.joined[at[n], features : 2 * features] = along_w
        kept.joined[at[n], 2 * features : 3 * features] = along_h
    weights_of()
    up_bias = hidden_bias(ins.up_bias, layer, ins.place)
    found = mlp_rows(
        ins.stream[...],
        kept.joined[...],
        weights[0],
        ins.layer_gain[layer : layer + 1, :],
        weights[1],
        up_bias,
        weights[2],
        side,
    )
    for name in KEPT:
        to = getattr(kept, name)
        to[...] = getattr(found, name).astype(to.dtype)
    for n in range(images):
        on_result(n, found.result[at[n]])
    squares = found.squares
    return center, inv_std, squares


def stage_backward(
    layer, place, grad_of, center, inv_std, conv, par, weights, kept, gb, gu, small, rows_ref, outs,
    dp, *, images, side,
):
    rows = side * WIDE
    features = gb.shape[1]
    grad_low, gpre, gc = rows_ref
    found = backward_rows(
        grad_of(),
        kept.uhat[...],
        kept.inv_norm[...],
        kept.slope[...].astype(F32),
        weights[0],
        par.layer_gain[layer : layer + 1, :],
        weights[1],
        weights[2],
    )
    grad_low[...] = found.grad_low
    gpre[...] = found.gpre
    gc[...] = found.gc
    gu[...] = found.gu.astype(gu.dtype)
    gain, bias = found.gain, found.bias
    offset = scale = cross = None
    for n in range(images):
        at = slice(n * rows, (n + 1) * rows)
        back, pairs = backward_mixes(found.gj[at], kept.joined[at, 0:features], par.mixing_back[...])
        gb[at, :] = back.astype(gb.dtype)
        offset = add_up(offset, jnp.sum(back, axis=0, keepdims=True))
        ahat = (conv[at, :] - center) * inv_std
        scale = add_up(scale, jnp.sum(back * ahat, axis=0, keepdims=True))
        cross = add_up(cross, pairs)
    small[NORM_ROW[layer] : NORM_ROW[layer] + 1, 0:features] = gain
    groups = par.up_bias.shape[1]
    width = bias.shape[1] // groups
    for j in range(groups):
        small[pl.ds(BIAS_ROW[layer] + (place[0] ^ j), 1), 0:width] = bias[:, j * width : (j + 1) * width]
    wide, tall = mixing_grads(cross, side)
    mixes = slice(layer * WIDE, (layer + 1) * WIDE)
    small[mixes, features : features + WIDE] = wide
    small[mixes, features + WIDE : features + 2 * WIDE] = tall
    unite_grad = dot_rows(kept.joined[...], gc[...])
    normal = (kept.uhat[...] * par.layer_gain[layer : layer + 1, :]).astype(BF16)
    up_grad = dot_rows(normal, gpre[...])
    down_grad = dot_rows(grad_low[...], kept.hidden[...])
    pack_grads(unite_grad, up_grad, down_grad, place[1], outs, dp)
    return offset, scale


def first_body(ins, outs, tmp, *, images, side):
    place, taps = ins.place, ins.taps
    own, conv, moments = outs.own, outs.conv, outs.moments
    every = tmp.every
    rows = side * WIDE
    by_image(ins.stream, every)
    for n in range(images):
        own[n * rows : (n + 1) * rows, :] = every[place[0] * images + n]
    for n in range(images):
        at = slice(n * rows, (n + 1) * rows)
        conv[at, :] = convolve(own[at, :], taps[:, 0, :], side)
    local_moments(conv, moments, images, side)


def other_body(ins, outs, tmp, *, images, side):
    rows = side * WIDE
    by_image(ins.cotangent, tmp.every)
    for n in range(images):
        outs.cotangent[n * rows : (n + 1) * rows, :] = tmp.every[ins.place[0] * images + n]
    _, groups, width = outs.up_bias.shape
    for j in range(groups):
        outs.up_bias[:, j, :] = ins.up_bias[:, j * width : (j + 1) * width]
    mixes = ins.mix_w[...].astype(F32), ins.mix_h[...].astype(F32)
    for layer in range(ins.mix_w.shape[1]):
        outs.mixing[layer][...], outs.mixing_back[layer][...] = mixing_matrices(
            *(mix[:, layer, :].astype(BF16) for mix in mixes), side
        )


def middle_body(ins, outs, tmp, *, images, side):
    rows = side * WIDE
    weights = tmp.unite, tmp.up, tmp.down
    results = []

    def weights_of():
        unpack_weights(tmp, *weights)

    center, inv_std, squares = stage_forward(
        0, ins, weights, weights_of, outs, lambda n, result: results.append(result), images=images, side=side
    )
    outs.stats[0:1, :] = center
    outs.stats[1:2, :] = inv_std
    outs.squares[...] = squares
    for n, result in enumerate(results):
        at = slice(n * rows, (n + 1) * rows)
        outs.stream1[at, :] = result
        outs.conv1[at, :] = convolve(result, ins.taps[:, 1, :], side)
    local_moments(outs.conv1, outs.moments1, images, side)


def last_body(ins, outs, tmp, *, images, side, dp):
    weights = tmp.unite, tmp.up, tmp.down
    results = []

    def weights_of():
        unpack_weights(tmp, *weights)

    center, inv_std, squares = stage_forward(
        1, ins, weights, weights_of, tmp, lambda n, result: results.append(result), images=images, side=side
    )
    outs.result[...] = pack_image_rows(jnp.concatenate(results, axis=0), side).astype(BF16)
    outs.stats[0:1, :] = center
    outs.stats[1:2, :] = inv_std
    outs.small[...] = jnp.zeros_like(outs.small)
    offset, scale = stage_backward(
        1, ins.place, lambda: ins.cotangent[...], center, inv_std,
        ins.conv, ins, weights, tmp, outs.gb, outs.gu, outs.small,
        (tmp.grad_low, tmp.gpre, tmp.gc), outs, dp, images=images, side=side,
    )
    features = squares.shape[1]
    outs.small[SQUARES_ROW[1] : SQUARES_ROW[1] + 3, 0:features] = squares
    to_all(outs.sums, 0, offset)
    to_all(outs.sums, 1, scale)


def conv_back(layer, sums, gb, gu, conv, stats, par, totals, *, images, side):
    rows = side * WIDE
    features = gb.shape[1]
    cells = images * side * side * sums.shape[0]
    offset = jnp.sum(sums[:, 0, 0:features], axis=0, keepdims=True)
    scale = jnp.sum(sums[:, 1, 0:features], axis=0, keepdims=True)
    totals[0:1, :] = offset
    totals[1:2, :] = scale
    center, inv_std = stats[0:1, :], stats[1:2, :]
    factor = par.batch_gain[layer : layer + 1, :] * inv_std
    found = []
    for n in range(images):
        at = slice(n * rows, (n + 1) * rows)
        found.append(
            conv_back_image(
                gb[at, :].astype(F32),
                (conv[at, :] - center) * inv_std,
                gu[at, :].astype(F32),
                factor,
                offset / cells,
                scale / cells,
                par.taps[:, layer, :],
                side,
            )
        )
    return found


def taps_body(ins, outs, tmp, *, images, side):
    rows = side * WIDE
    center, inv_std = ins.stats[0:1, :], ins.stats[1:2, :]
    plain = scaled = None
    for n in range(images):
        at = slice(n * rows, (n + 1) * rows)
        stream = ins.stream[at, :]
        valid = valid_rows(rows, side)
        ones = jnp.where(valid, jnp.ones_like(stream), 0.0)
        ahat = jnp.where(valid, (ins.conv[at, :] - center) * inv_std, 0.0)
        plain = add_up(plain, tap_sums(ones, stream))
        scaled = add_up(scaled, tap_sums(ahat, stream))
    outs.plain[...] = plain
    outs.scaled[...] = scaled


def between_body(ins, outs, tmp, *, images, side, dp):
    weights = tmp.unite, tmp.up, tmp.down
    unpack_weights(tmp, *weights)
    rows = side * WIDE
    features = ins.gb1.shape[1]
    small, sums = tmp.small, outs.sums
    small[...] = ins.small[...]
    grads, kernel = [], None
    found = conv_back(
        1, ins.sums1, ins.gb1, ins.gu1, ins.conv1, ins.stats1, ins, outs.totals1, images=images, side=side
    )
    for n, (grad, ga) in enumerate(found):
        grads.append(grad)
        kernel = add_up(kernel, tap_sums(ga, ins.stream1[n * rows : (n + 1) * rows, :]))
    small[TAPS_ROW : TAPS_ROW + 9, 0:features] = kernel
    stats = ins.stats0
    offset, scale = stage_backward(
        0, ins.place, lambda: jnp.concatenate(grads, axis=0), stats[0:1, :], stats[1:2, :], ins.conv0, ins, weights, ins,
        tmp.gb, tmp.gu, small, (tmp.grad_low, tmp.gpre, tmp.gc), outs, dp,
        images=images, side=side,
    )
    kernel = None
    for n in range(images):
        at = slice(n * rows, (n + 1) * rows)
        kernel = add_up(kernel, tap_sums(tmp.gb[at, :], ins.stream0[at, :]))
    for k, values in enumerate((kernel, ins.plain[...], ins.scaled[...])):
        small[9 * k : 9 * k + 9, 0:features] = values
    small[SQUARES_ROW[0] : SQUARES_ROW[0] + 3, 0:features] = ins.squares0[...]
    cells = images * side * side
    center, inv_std = stats[0:1, :], stats[1:2, :]
    grads = []
    for n in range(images):
        at = slice(n * rows, (n + 1) * rows)
        ahat = (ins.conv0[at, :] - center) * inv_std
        factor = ins.batch_gain[0:1, :] * inv_std
        grad, _ = conv_back_image(
            tmp.gb[at, :], ahat, tmp.gu[at, :], factor, offset / cells, scale / cells, ins.taps[:, 0, :], side
        )
        grads.append(grad)
    outs.grad[...] = pack_image_rows(jnp.concatenate(grads, axis=0), side).astype(BF16)
    to_all(sums, 0, offset)
    to_all(sums, 1, scale)
    devices, height, _ = sums.shape
    for g in range(height - 2):
        held = min(devices, SMALL_ROWS - g * devices)
        sums[0:held, 2 + g, :] = small[g * devices : g * devices + held, :]
        if held < devices:
            sums[held:, 2 + g, :] = jnp.zeros((devices - held, SMALL_WIDE), F32)


def final_body(ins, outs, tmp, *, images, side):
    held, rows, features = tmp.every.shape
    sums = ins.sums0
    cells = images * side * side
    devices = sums.shape[0]
    group = held // images
    offset = jnp.sum(sums[:, 0, 0:features], axis=0, keepdims=True)
    scale = jnp.sum(sums[:, 1, 0:features], axis=0, keepdims=True)
    for row, total in enumerate((offset, scale)):
        to = (outs.offset_grad, outs.scale_grad)[row]
        to[0:1, :] = total
        to[1:2, :] = ins.totals1[row : row + 1, :]
    center, inv_std = ins.stats0[0:1, :], ins.stats0[1:2, :]
    factor = ins.batch_gain[0:1, :] * inv_std
    first = ins.place[1] * group

    def apart(row, total):
        own = [sums[first + p, row : row + 1, 0:features] for p in range(group)]
        own = jnp.concatenate([value for value in own for _ in range(images)], axis=0)
        return factor * (total / (cells * devices) - own / cells)

    shift, slant = apart(0, offset), apart(1, scale)
    put_images(ins.place[0], ins.parts, tmp.every, images, side)
    padded, fields = tmp.padded, tmp.fields
    for ref in (padded, fields):
        edge = jnp.zeros((1,) + ref.shape[1:], F32)
        ref[0:1] = edge
        ref[side + 1 : side + 2] = edge
        edge = jnp.zeros((side, 1) + ref.shape[2:], F32)
        ref[1 : side + 1, 0:1] = edge
        ref[1 : side + 1, side + 1 : side + 2] = edge
    padded[1 : side + 1, 1 : side + 1] = ins.stream[...]
    taps = ins.taps[:, 0, :]
    for h in range(side):
        conv = None
        for i in range(3):
            for j in range(3):
                term = padded[h + i, j : j + side] * taps[3 * i + j : 3 * i + j + 1]
                conv = add_up(conv, term)
        fields[h + 1, 1 : side + 1] = shift + (conv - center) * inv_std * slant
    for h in range(side):
        lines = jnp.swapaxes(tmp.every[:, h * WIDE : (h + 1) * WIDE, :], 0, 1)[:side]
        for i in range(3):
            for j in range(3):
                lines = lines - fields[h + 2 - i, 2 - j : 2 - j + side] * taps[3 * i + j : 3 * i + j + 1]
        outs.out[h] = lines


def put_images(place, parts, every, images, side):
    features = every.shape[2]
    for j, part in enumerate(parts):
        packed = part[...].astype(F32)
        lines = packed.shape[0] // side
        for half in range(2):
            values = packed[:, half * features : (half + 1) * features]
            for k in range(lines):
                n, h = divmod(half * lines + k, side)
                every[(place ^ j) * images + n, h * WIDE : h * WIDE + side, :] = values[
                    k * side : (k + 1) * side
                ]


def gather_body(ins, outs, tmp):
    for g in range(outs.message.shape[1]):
        to_all(outs.message, g, jnp.sum(ins.sums0[:, 2 + g, :], axis=0, keepdims=True))


def spread_body(ins, outs, tmp, *, images, side):
    put_images(ins.place[0], ins.parts, tmp.every, images, side)
    for h in range(side):
        outs.out[h] = jnp.swapaxes(tmp.every[:, h * WIDE : (h + 1) * WIDE, :], 0, 1)[:side]


def core_body(ins, outs, tmp):
    apart = isinstance(outs.parts, list)
    for k in range(ins.keep.shape[0]):
        at = (ins.place[1] >> 1) ^ k if apart else k
        to = outs.parts[k] if apart else outs.parts.at[k]
        to[...] = (ins.keep[at].astype(F32) + ins.got[at].astype(F32)).astype(BF16)


def chips_body(ins, outs, tmp):
    groups = len(outs.give)
    for layer, parts in enumerate(ins.parts):
        parts = parts if isinstance(parts, list) else [parts.at[k] for k in range(parts.shape[0])]
        total = parts[0][...].astype(F32)
        for other in parts[1:]:
            total = total + other[...].astype(F32)
        part = total.shape[0] // 3
        width = total.shape[1] // groups
        features = outs.give[0].shape[2] - 2 * width
        for j in range(groups):
            block = jnp.concatenate(
                [
                    total[:part, j * width : (j + 1) * width],
                    total[part : 2 * part, j * width : (j + 1) * width],
                    *[
                        total[2 * part :, q * SMALL_WIDE : q * SMALL_WIDE + features // 3]
                        for q in range(3)
                    ],
                ],
                axis=1,
            )
            outs.give[j][layer] = block.astype(BF16)


def weights_body(ins, outs, tmp):
    layers = outs.up_grad.shape[0]
    for layer in range(layers):
        terms = [ref[layer].astype(F32) for ref in ins.got]
        while len(terms) > 1:
            terms = [terms[j] + terms[j + 1] for j in range(0, len(terms), 2)]
        total = terms[0]
        width = outs.up_grad.shape[2]
        features = outs.unite_grad.shape[1]
        outs.up_grad[layer] = total[:, :width]
        outs.down_grad[layer] = total[:, width : 2 * width]
        rest = total[:, 2 * width :]
        rows = jnp.concatenate([rest[:, q * features : (q + 1) * features] for q in range(3)], axis=0)
        outs.unite_grad[layer] = rows.T


def small_body(ins, outs, tmp, *, side, cells, entries):
    got = ins.got
    features = outs.gain_grad.shape[1]
    devices, height, _ = got.shape
    values = tmp.values
    for g in range(height):
        values[g * devices : (g + 1) * devices, :] = got[:, g, :]
    factor = ins.batch_gain[0:1, :] * ins.stats0[1:2, :]
    first = factor * (
        values[0:9, 0:features]
        - ins.offset[0:1, :] / cells * values[9:18, 0:features]
        - ins.scale[0:1, :] / cells * values[18:27, 0:features]
    )
    for k in range(9):
        outs.kernel_grad[k, 0:1, :] = first[k : k + 1]
        outs.kernel_grad[k, 1:2, :] = values[TAPS_ROW + k : TAPS_ROW + k + 1, 0:features]
    width = outs.bias_grad.shape[1]
    for layer in range(2):
        outs.gain_grad[layer : layer + 1, :] = values[NORM_ROW[layer] : NORM_ROW[layer] + 1, 0:features]
        outs.bias_grad[layer : layer + 1, :] = values[pl.ds(BIAS_ROW[layer] + ins.place[0], 1), 0:width]
        rows = slice(layer * WIDE, layer * WIDE + side)
        outs.width_grad[:, layer, :] = values[rows, features : features + side]
        outs.height_grad[:, layer, :] = values[rows, features + WIDE : features + WIDE + side]
        squares = values[SQUARES_ROW[layer] : SQUARES_ROW[layer] + 3, 0:features]
        outs.stream_rms[:, layer : layer + 1] = jnp.sqrt(
            jnp.sum(squares, axis=1, keepdims=True) / entries
        )


def call(body, ins, outs, scratch=None, shards=(), micros=0, vmem=VMEM_LIMIT, **static):
    ins = dict(ins, shards=list(shards))
    operands, in_tree = jax.tree.flatten(ins)
    shapes, out_tree = jax.tree.flatten(
        {name: jax.tree.map(lambda shape: jax.ShapeDtypeStruct(*shape), outs[name], is_leaf=is_shape) for name in outs}
    )
    scratch = dict(scratch or {})
    if shards:
        scratch["packed"] = (len(shards),) + shards[0].shape, shards[0].dtype
    tmp_names = list(scratch)

    def kernel(*refs):
        cut = len(operands), len(operands) + len(shapes)
        given = SimpleNamespace(**jax.tree.unflatten(in_tree, refs[: cut[0]]))
        results = SimpleNamespace(**jax.tree.unflatten(out_tree, refs[cut[0] : cut[1]]))
        tmp = SimpleNamespace(**dict(zip(tmp_names, refs[cut[1] :])))
        for k, shard in enumerate(given.shards):
            tmp.packed[given.place[1] ^ k] = shard[...]
        body(given, results, tmp, **static)

    def space(name):
        return pl.BlockSpec(memory_space=pltpu.SMEM if name == "place" else pltpu.VMEM)

    found = pl.pallas_call(
        kernel,
        out_shape=shapes,
        in_specs=jax.tree.leaves({name: jax.tree.map(lambda _: space(name), ins[name]) for name in ins}),
        out_specs=[space("")] * len(shapes),
        scratch_shapes=[pltpu.VMEM(*scratch[name]) for name in tmp_names],
        compiler_params=pltpu.CompilerParams(vmem_limit_bytes=vmem),
        cost_estimate=pl.CostEstimate(
            flops=int(micros * COST_FLOPS), transcendentals=0, bytes_accessed=int(micros * COST_BYTES)
        ),
    )(*operands)
    return SimpleNamespace(**jax.tree.unflatten(out_tree, found))


def is_shape(value):
    return isinstance(value, tuple)


def swap(values, axis, mask):
    return lax.ppermute(values, axis, [(i, i ^ mask) for i in range(lax.axis_size(axis))])


def after(values, *others):
    return lax.optimization_barrier((values, others))[0]


def per_device(
    inputs,
    conv_weight,
    batch_gain,
    batch_bias,
    mix_width,
    mix_height,
    unite_weight,
    layer_gain,
    up_weight,
    up_bias,
    down_weight,
    cotangent,
):
    held, side, _, features = inputs.shape
    layers = conv_weight.shape[0]
    dp, mp = lax.axis_size("dp"), lax.axis_size("mp")
    devices = dp * mp
    images = held // mp
    cells = side * WIDE
    rows = images * cells
    units = up_bias.shape[1]
    part = features // dp
    both = ("dp", "mp")
    sizes = dict(images=images, side=side)
    place = jnp.stack([lax.axis_index("mp"), lax.axis_index("dp")]).astype(jnp.int32)

    def group_parts(values):
        if isinstance(values, (list, tuple)):
            far_first = {j: swap(values[j], "mp", j) for j in range(mp - 1, 0, -1)}
            return [far_first.get(j, value) for j, value in enumerate(values)]
        parts = [values]
        for j in range(1, mp):
            step = j & -j
            parts.append(swap(parts[j ^ step], "mp", step))
        return parts

    def share(blocks):
        return lax.all_to_all(blocks, both, 0, 0, tiled=False)

    maps = jnp.transpose(inputs, (1, 2, 0, 3))
    cotangent_maps = jnp.transpose(cotangent, (1, 2, 0, 3))
    taps = jnp.transpose(conv_weight, (1, 0, 2))
    mix_w, mix_h = (jnp.transpose(mix, (1, 0, 2)) for mix in (mix_width, mix_height))
    shared = (devices, 2, features)
    thirds = unite_weight.reshape(layers, 3, part, features)
    beside = [(0, 0), (0, 0), (0, SMALL_WIDE - features)]
    thirds = jnp.concatenate([jnp.pad(thirds[:, q], beside) for q in range(3)], axis=2)
    thirds = jnp.pad(thirds, ((0, 0), (0, 0), (0, units - 3 * SMALL_WIDE)))

    def widen(wide, step):
        return jnp.concatenate([wide, swap(wide, "mp", step)], axis=1)

    def over_dp(layer, wide, wait_chips, wait_core):
        piece = after(jnp.concatenate([wide, thirds[layer]], axis=0), *wait_chips)
        shards = [piece] + [swap(piece, "dp", 2 * k) for k in range(1, dp // 2)]
        mates = [swap(after(shard, *wait_core), "dp", 1) for shard in shards]
        return [shard for pair in zip(shards, mates) for shard in pair]

    wide = jnp.concatenate([up_weight[0], down_weight[0]], axis=0)
    wide = near = widen(wide, 1) if mp > 1 else wide
    step = 2
    while step < mp:
        wide = widen(wide, step)
        step *= 2
    found = call(
        first_body,
        dict(place=after(place, near), stream=maps, taps=taps),
        dict(own=((rows, features), F32), conv=((rows, features), F32), moments=(shared, F32)),
        dict(every=((held, cells, features), F32)),
        micros=4,
        **sizes,
    )
    moments0 = share(after(found.moments, wide))
    other = call(
        other_body,
        dict(place=place, cotangent=cotangent_maps, mix_w=mix_w, mix_h=mix_h, up_bias=up_bias),
        dict(
            cotangent=((rows, features), F32),
            up_bias=((layers, mp, units // mp), F32),
            mixing=[((2 * cells, cells), BF16)] * layers,
            mixing_back=[((cells, 2 * cells), BF16)] * layers,
        ),
        dict(every=((held, cells, features), F32)),
        micros=3,
        **sizes,
    )

    packed = [over_dp(0, wide, (found.moments,), (moments0, other.mixing[0]))]
    wide = after(jnp.concatenate([up_weight[1], down_weight[1]], axis=0), wide)
    step = 1
    while step < mp:
        wide = widen(wide, step)
        step *= 2
    wide1 = wide

    own, conv0 = found.own, found.conv
    par = dict(
        place=place,
        taps=taps,
        batch_gain=batch_gain,
        batch_bias=batch_bias,
        layer_gain=layer_gain,
        up_bias=other.up_bias,
    )
    kept = dict(
        joined=((rows, 3 * features), BF16),
        uhat=((rows, features), F32),
        inv_norm=((rows, 1), F32),
        slope=((rows, units), BF16),
        hidden=((rows, units), BF16),
    )
    weight_tmp = dict(
        unite=((3 * features, features), BF16),
        up=((features, units), BF16),
        down=((features, units), BF16),
    )
    back_tmp = dict(
        grad_low=((rows, features), BF16), gpre=((rows, units), BF16), gc=((rows, features), BF16)
    )
    back_outs = dict(gb=((rows, features), F32), gu=((rows, features), F32))
    stats = ((2, features), F32)
    pieces = [((dp // 2, 3 * part, units), BF16)] * 2
    piece = ((3 * part, units), BF16)

    def over_core(values, apart=False):
        return call(
            core_body,
            dict(place=place, keep=values.keep, got=swap(values.give, "dp", 1)),
            dict(parts=[piece] * (dp // 2) if apart else pieces[0]),
            vmem=SMALL_LIMIT,
        ).parts

    def from_chips(parts):
        if isinstance(parts, list):
            return [swap(values, "dp", 2 * k) if k else values for k, values in enumerate(parts)]
        groups = [[2 * q + c for q in range(dp // 2)] for c in range(2)]
        return lax.all_to_all(parts, "dp", 0, 0, axis_index_groups=groups, tiled=False)

    mid = call(
        middle_body,
        dict(
            par,
            moments=moments0,
            conv=conv0,
            stream=own,
            mixing=other.mixing[0],
        ),
        dict(
            kept,
            stream1=((rows, features), F32),
            conv1=((rows, features), F32),
            moments1=(shared, F32),
            stats=stats,
            squares=((3, features), F32),
        ),
        weight_tmp,
        packed[0],
        micros=6,
        **sizes,
    )
    packed.append(over_dp(1, wide1, packed[0][::2], (mid.moments1,)))
    under = call(
        taps_body,
        dict(stream=own, conv=conv0, stats=mid.stats),
        dict(plain=((9, features), F32), scaled=((9, features), F32)),
        micros=2,
        **sizes,
    )
    last = call(
        last_body,
        dict(
            par,
            moments=after(share(mid.moments1), under.plain),
            conv=mid.conv1,
            stream=mid.stream1,
            mixing=other.mixing[1],
            mixing_back=other.mixing_back[1],
            cotangent=other.cotangent,
        ),
        dict(
            gb=((rows, features), BF16),
            gu=((rows, features), BF16),
            result=((images * side * side // 2, 2 * features), BF16),
            stats=stats,
            small=((SMALL_ROWS, SMALL_WIDE), F32),
            sums=(shared, F32),
            keep=pieces[0],
            give=pieces[1],
        ),
        dict(
            dict(kept, slope=((rows, units), F32)),
            **weight_tmp,
            **back_tmp,
        ),
        packed[1],
        micros=10,
        dp=dp,
        **sizes,
    )
    summed1 = over_core(last)
    groups = -(-SMALL_ROWS // devices)
    between = call(
        between_body,
        {
            **par,
            **{name: getattr(mid, name) for name in kept},
            **dict(
                sums1=after(share(last.sums), summed1),
                gb1=last.gb,
                gu1=last.gu,
                conv1=mid.conv1,
                stream1=mid.stream1,
                stats1=last.stats,
                small=last.small,
                stream0=own,
                plain=under.plain,
                scaled=under.scaled,
                conv0=conv0,
                stats0=mid.stats,
                squares0=mid.squares,
                mixing_back=other.mixing_back[0],
            ),
        },
        dict(
            grad=((images * side * side // 2, 2 * features), BF16),
            totals1=stats,
            sums=((devices, 2 + groups, SMALL_WIDE), F32),
            keep=pieces[0],
            give=pieces[1],
        ),
        dict(
            back_tmp,
            **back_outs,
            **weight_tmp,
            small=((SMALL_ROWS, SMALL_WIDE), F32),
        ),
        packed[0],
        micros=10,
        dp=dp,
        **sizes,
    )
    result_parts = [last.result] + [swap(last.result, "mp", 1 << k) for k in range((mp - 1).bit_length())]
    parts1 = from_chips(summed1)
    grad, sums0, give, parts1, near = lax.optimization_barrier(
        (between.grad, between.sums, between.give, parts1, result_parts[1:])
    )
    result_parts = [last.result]
    for j in range(1, mp):
        step = j & -j
        result_parts.append(near[j.bit_length() - 1] if j == step else swap(result_parts[j ^ step], "mp", step))
    sums0 = share(sums0)
    chunk = call(
        gather_body, dict(sums0=sums0), dict(message=((devices, groups, SMALL_WIDE), F32)), vmem=SMALL_LIMIT
    )
    shared_small = share(chunk.message)
    summed0 = over_core(SimpleNamespace(keep=between.keep, give=give), True)
    summed0 = after(summed0, result_parts)
    grad_parts = group_parts(after(grad, summed0))
    cut = call(
        chips_body,
        dict(parts=[from_chips(summed0), parts1]),
        dict(give=[((layers, part, 2 * (units // mp) + 3 * features), BF16)] * mp),
        vmem=SMALL_LIMIT,
    ).give
    grads = call(
        weights_body,
        dict(got=group_parts(after(cut, grad_parts, shared_small))),
        dict(
            up_grad=((layers, part, units // mp), F32),
            down_grad=((layers, part, units // mp), F32),
            unite_grad=((layers, features, 3 * part), F32),
        ),
        vmem=SMALL_LIMIT,
    )
    whole_maps = ((side, side, held, features), F32)
    output = call(
        spread_body,
        dict(place=place, parts=result_parts),
        dict(out=whole_maps),
        dict(every=((held, cells, features), F32)),
        **sizes,
    ).out
    padded = ((side + 2, side + 2, held, features), F32)
    end = call(
        final_body,
        dict(
            place=place,
            parts=grad_parts,
            stream=maps,
            sums0=sums0,
            totals1=between.totals1,
            stats0=mid.stats,
            batch_gain=batch_gain,
            taps=taps,
        ),
        dict(out=whole_maps, offset_grad=stats, scale_grad=stats),
        dict(every=((held, cells, features), F32), padded=padded, fields=padded),
        vmem=36 * 1024 * 1024,
        **sizes,
    )
    outputs = [jnp.transpose(out, (2, 0, 1, 3)) for out in (output, end.out)]
    small = call(
        small_body,
        dict(
            place=place,
            got=shared_small,
            batch_gain=batch_gain,
            stats0=mid.stats,
            offset=end.offset_grad,
            scale=end.scale_grad,
        ),
        dict(
            kernel_grad=((9, layers, features), F32),
            gain_grad=((layers, features), F32),
            bias_grad=((layers, units // mp), F32),
            width_grad=((side, layers, side), F32),
            height_grad=((side, layers, side), F32),
            stream_rms=((3, layers), F32),
        ),
        dict(values=((groups * devices, SMALL_WIDE), F32)),
        vmem=SMALL_LIMIT,
        side=side,
        cells=images * side * side * devices,
        entries=held * side * side * features * dp,
    )
    return (
        *outputs,
        jnp.transpose(small.kernel_grad, (1, 0, 2)),
        end.scale_grad,
        end.offset_grad,
        jnp.transpose(small.width_grad, (1, 0, 2)),
        jnp.transpose(small.height_grad, (1, 0, 2)),
        jnp.transpose(grads.unite_grad, (0, 2, 1)),
        small.gain_grad,
        grads.up_grad,
        small.bias_grad,
        grads.down_grad,
        small.stream_rms.T,
    )


def solution(mesh):
    in_specs = (
        P("dp", None, None, None),
        P(),
        P(),
        P(),
        P(),
        P(),
        P(None, "dp", None),
        P(),
        P(None, "dp", "mp"),
        P(),
        P(None, "dp", "mp"),
        P("dp", None, None, None),
    )
    out_specs = (
        P("dp", None, None, None),
        P("dp", None, None, None),
        P(),
        P(),
        P(),
        P(),
        P(),
        P(None, "dp", None),
        P(),
        P(None, "dp", "mp"),
        P(None, "mp"),
        P(None, "dp", "mp"),
        P(),
    )
    return jax.shard_map(
        per_device, mesh=mesh, in_specs=in_specs, out_specs=out_specs, check_vma=False
    )
```

```python
import functools
from types import SimpleNamespace

import jax
import jax.numpy as jnp
from jax import lax
from jax.experimental import pallas as pl
from jax.experimental.pallas import tpu as pltpu
from jax.sharding import PartitionSpec as P

EPSILON = 1e-05
WIDE = 16
VMEM_LIMIT = 58 * 1024 * 1024
SMALL_LIMIT = 14 * 1024 * 1024
COST_BYTES = 3.0e6
COST_FLOPS = 1.0e10
F32 = jnp.float32
BF16 = jnp.bfloat16


def dot(left, right):
    return lax.dot_general(left, right, (((1,), (0,)), ((), ())), preferred_element_type=F32)


def dot_cols(left, right):
    return lax.dot_general(left, right, (((1,), (1,)), ((), ())), preferred_element_type=F32)


def dot_rows(left, right):
    return lax.dot_general(left, right, (((0,), (0,)), ((), ())), preferred_element_type=F32)


def valid_rows(rows, side):
    return lax.broadcasted_iota(jnp.int32, (rows, 1), 0) % WIDE < side


def three_shifts(image):
    rows, features = image.shape
    empty = jnp.zeros((WIDE, features), image.dtype)
    padded = jnp.concatenate([empty, image, empty], axis=0)
    total = rows + 2 * WIDE
    return pltpu.roll(padded, 1, 0), padded, pltpu.roll(padded, total - 1, 0)


def convolve(image, taps, side):
    rows = image.shape[0]
    shifted = three_shifts(image)
    summed = None
    for i in range(3):
        for j in range(3):
            term = shifted[j][WIDE * i : WIDE * i + rows] * taps[3 * i + j : 3 * i + j + 1]
            summed = term if summed is None else summed + term
    return jnp.where(valid_rows(rows, side), summed, 0.0)


def to_all(message_ref, row, values):
    devices = message_ref.shape[0]
    message_ref[:, row, 0 : values.shape[1]] = jnp.broadcast_to(values, (devices, values.shape[1]))


def local_moments(conv_ref, moments_ref, images, side):
    rows = side * WIDE
    count = images * side * side
    total = None
    for n in range(images):
        part = jnp.sum(conv_ref[n * rows : (n + 1) * rows, :], axis=0, keepdims=True)
        total = part if total is None else total + part
    mean = total / count
    squares = None
    for n in range(images):
        deviate = jnp.where(
            valid_rows(rows, side), conv_ref[n * rows : (n + 1) * rows, :] - mean, 0.0
        )
        part = jnp.sum(deviate * deviate, axis=0, keepdims=True)
        squares = part if squares is None else squares + part
    to_all(moments_ref, 0, mean)
    to_all(moments_ref, 1, squares)


def whole_moments(gathered_ref, count):
    devices = gathered_ref.shape[0]
    means = gathered_ref[:, 0, :]
    squares = gathered_ref[:, 1, :]
    center = jnp.sum(means, axis=0, keepdims=True) / devices
    apart = means - center
    spread = (
        jnp.sum(squares, axis=0, keepdims=True)
        + jnp.sum(apart * apart, axis=0, keepdims=True) * count
    ) / (count * devices)
    return center, lax.rsqrt(spread + EPSILON)


def mixing_matrices(mix_w, mix_h, side):
    cells = side * WIDE
    row = lax.broadcasted_iota(jnp.int32, (cells, side), 0)
    col = lax.broadcasted_iota(jnp.int32, (cells, side), 1)
    at_w = (row % WIDE == col).astype(BF16)
    at_h = (row // WIDE == col).astype(BF16)
    out = lax.broadcasted_iota(jnp.int32, (cells, cells), 0)
    inp = lax.broadcasted_iota(jnp.int32, (cells, cells), 1)
    same_h = out // WIDE == inp // WIDE
    same_w = (out % WIDE == inp % WIDE) & (out % WIDE < side)

    def spread(picks, mix, keep, flip):
        left = (dot_cols if flip else dot)(picks, mix).astype(BF16)
        return jnp.where(keep, dot_cols(left, picks), 0.0).astype(BF16)

    forward = jnp.concatenate(
        [spread(at_w, mix_w, same_h, False), spread(at_h, mix_h, same_w, False)], axis=0
    )
    backward = jnp.concatenate(
        [spread(at_w, mix_w, same_h, True), spread(at_h, mix_h, same_w, True)], axis=1
    )
    return forward, backward


def by_image(maps_ref, all_ref):
    side, _, held, features = maps_ref.shape
    empty = jnp.zeros((WIDE - side, held, features), F32)
    for h in range(side):
        lines = jnp.concatenate([maps_ref[h], empty], axis=0)
        all_ref[:, h * WIDE : (h + 1) * WIDE, :] = jnp.swapaxes(lines, 0, 1)


def unpack_weights(tmp, unite_ref, up_ref, down_ref):
    packed_ref = tmp.packed
    shards, height, _ = packed_ref.shape
    part = height // 3
    features = unite_ref.shape[1]
    ups, downs, unites = [], [], []
    for s in range(shards):
        piece = packed_ref[s].astype(F32)
        ups.append(piece[:part])
        downs.append(piece[part : 2 * part])
        for q in range(3):
            unites.append(piece[2 * part :, q * SMALL_WIDE : q * SMALL_WIDE + features])
    up_ref[...] = jnp.concatenate(ups, axis=0).astype(BF16)
    down_ref[...] = jnp.concatenate(downs, axis=0).astype(BF16)
    unite_ref[...] = jnp.concatenate(unites, axis=0).astype(BF16)


def pack_grads(unite, up, down, mine, outs, dp):
    features = up.shape[0]
    part = features // dp
    beside = jnp.zeros((part, SMALL_WIDE - features), F32)
    filler = jnp.zeros((part, up.shape[1] - 3 * SMALL_WIDE), F32)

    def piece(s):
        columns = []
        for q in range(3):
            columns += [unite[(3 * s + q) * part : (3 * s + q + 1) * part], beside]
        return jnp.concatenate(
            [
                up[s * part : (s + 1) * part],
                down[s * part : (s + 1) * part],
                jnp.concatenate(columns + [filler], axis=1),
            ],
            axis=0,
        )

    first = (mine & 1) == 0
    for k in range(dp // 2):
        pair = piece(2 * k), piece(2 * k + 1)
        outs.keep[k] = jnp.where(first, pair[0], pair[1]).astype(BF16)
        outs.give[k] = jnp.where(first, pair[1], pair[0]).astype(BF16)


def pack_image_rows(values, side):
    lines = [values[r : r + side] for r in range(0, values.shape[0], WIDE)]
    half = len(lines) // 2
    return jnp.concatenate(
        [jnp.concatenate(lines[:half], axis=0), jnp.concatenate(lines[half:], axis=0)], axis=1
    )


def hidden_bias(up_bias_ref, layer, place_ref):
    groups = up_bias_ref.shape[1]
    blocks = [up_bias_ref[layer, pl.ds(place_ref[0] ^ j, 1), :] for j in range(groups)]
    return jnp.concatenate(blocks, axis=1)


def mix_image(conv, center, inv_std, bn_gain, bn_bias, mixing, side):
    rows = conv.shape[0]
    ahat = (conv - center) * inv_std
    branch = jnp.where(valid_rows(rows, side), ahat * bn_gain + bn_bias, 0.0).astype(BF16)
    along = dot(mixing, branch).astype(BF16)
    return branch, along[:rows], along[rows:]


def mlp_rows(stream, joined, unite_ref, norm_gain, up_ref, up_bias, down_ref, side):
    rows, features = stream.shape
    united = dot(joined, unite_ref[...])
    resid = stream + united
    mid = jnp.sum(resid, axis=-1, keepdims=True) / features
    deviate = resid - mid
    spread = jnp.sum(deviate * deviate, axis=-1, keepdims=True) / features
    inv_norm = lax.rsqrt(spread + EPSILON)
    uhat = deviate * inv_norm
    normal = (uhat * norm_gain).astype(BF16)
    pre = dot(normal, up_ref[...]) + up_bias
    below = 0.5 + 0.5 * lax.erf(pre * (0.5**0.5))
    slope = below + pre * (jnp.exp(-0.5 * pre * pre) * 0.3989422804014327)
    hidden = (pre * below).astype(BF16)
    mlp = jnp.where(valid_rows(rows, side), dot_cols(hidden, down_ref[...]), 0.0)
    result = resid + mlp
    squares = jnp.concatenate(
        [jnp.sum(v * v, axis=0, keepdims=True) for v in (united, mlp, result)], axis=0
    )
    return SimpleNamespace(
        uhat=uhat,
        inv_norm=inv_norm,
        slope=slope,
        hidden=hidden,
        result=result,
        squares=squares,
    )


def backward_rows(grad, uhat, inv_norm, slope, unite_ref, norm_gain, up_ref, down_ref):
    features = grad.shape[1]
    grad_low = grad.astype(BF16)
    gh = dot(grad_low, down_ref[...])
    gpre = (gh * slope).astype(BF16)
    bias = jnp.sum(gpre.astype(F32), axis=0, keepdims=True)
    gn = dot_cols(gpre, up_ref[...])
    gain = jnp.sum(gn * uhat, axis=0, keepdims=True)
    q = gn * norm_gain
    mean_q = jnp.sum(q, axis=-1, keepdims=True) / features
    mean_qu = jnp.sum(q * uhat, axis=-1, keepdims=True) / features
    gu = grad + inv_norm * (q - mean_q - uhat * mean_qu)
    gc = gu.astype(BF16)
    return SimpleNamespace(
        grad_low=grad_low, gpre=gpre, bias=bias, gain=gain, gu=gu, gc=gc, gj=dot_cols(gc, unite_ref[...])
    )


def backward_mixes(gj, branch, mixing_back):
    features = branch.shape[1]
    both = jnp.concatenate([gj[:, features : 2 * features], gj[:, 2 * features :]], axis=0).astype(BF16)
    return gj[:, :features] + dot(mixing_back, both), dot_cols(both, branch)


def mixing_grads(cross, side):
    cells = side * WIDE
    out = lax.broadcasted_iota(jnp.int32, (cells, cells), 0)
    inp = lax.broadcasted_iota(jnp.int32, (cells, cells), 1)
    width = jnp.where(out // WIDE == inp // WIDE, cross[:cells], 0.0)
    height = jnp.where(out % WIDE == inp % WIDE, cross[cells:], 0.0)
    across, down = None, []
    for v in range(side):
        at = slice(v * WIDE, (v + 1) * WIDE)
        across = add_up(across, width[at])
        down.append(jnp.sum(height[at], axis=0, keepdims=True))
    down = jnp.concatenate(down + [jnp.zeros((WIDE - side, cells), F32)], axis=0)
    parts = []
    for values in (across, down):
        high = values.astype(BF16)
        parts += [high, (values - high.astype(F32)).astype(BF16)]
    row = lax.broadcasted_iota(jnp.int32, (cells, 2 * WIDE), 0)
    col = lax.broadcasted_iota(jnp.int32, (cells, 2 * WIDE), 1)
    picks = (col == jnp.where(col < WIDE, row % WIDE, row // WIDE + WIDE)).astype(BF16)
    sums = dot(jnp.concatenate(parts, axis=0), picks)
    sums = sums[: 2 * WIDE, :WIDE], sums[2 * WIDE :, WIDE:]
    return tuple(value[:WIDE] + value[WIDE:] for value in sums)


def tap_sums(values, stream):
    rows = values.shape[0]
    shifted = three_shifts(stream)
    return jnp.concatenate(
        [
            jnp.sum(values * shifted[j][WIDE * i : WIDE * i + rows], axis=0, keepdims=True)
            for i in range(3)
            for j in range(3)
        ],
        axis=0,
    )


def conv_back_image(gb, ahat, gu, factor, offset_mean, scale_mean, taps, side):
    rows = gb.shape[0]
    valid = valid_rows(rows, side)
    ga = jnp.where(valid, factor * (gb - offset_mean - ahat * scale_mean), 0.0)
    turned = three_shifts(ga)
    summed = gu
    for i in range(3):
        for j in range(3):
            summed = (
                summed
                + turned[2 - j][WIDE * (2 - i) : WIDE * (2 - i) + rows]
                * taps[3 * i + j : 3 * i + j + 1]
            )
    return jnp.where(valid, summed, 0.0), ga


def add_up(total, part):
    return part if total is None else total + part


SMALL_ROWS, SMALL_WIDE = 60, 384
NORM_ROW, SQUARES_ROW, BIAS_ROW, TAPS_ROW = (27, 48), (28, 49), (31, 52), 39
KEPT = ("uhat", "inv_norm", "slope", "hidden")


def stage_forward(layer, ins, weights, weights_of, kept, on_result, *, images, side):
    rows = side * WIDE
    at = [slice(n * rows, (n + 1) * rows) for n in range(images)]
    center, inv_std = whole_moments(ins.moments, images * side * side)
    for n in range(images):
        branch, along_w, along_h = mix_image(
            ins.conv[at[n], :],
            center,
            inv_std,
            ins.batch_gain[layer : layer + 1, :],
            ins.batch_bias[layer : layer + 1, :],
            ins.mixing[...],
            side,
        )
        features = branch.shape[1]
        kept.joined[at[n], 0:features] = branch
        kept.joined[at[n], features : 2 * features] = along_w
        kept.joined[at[n], 2 * features : 3 * features] = along_h
    weights_of()
    up_bias = hidden_bias(ins.up_bias, layer, ins.place)
    found = mlp_rows(
        ins.stream[...],
        kept.joined[...],
        weights[0],
        ins.layer_gain[layer : layer + 1, :],
        weights[1],
        up_bias,
        weights[2],
        side,
    )
    for name in KEPT:
        to = getattr(kept, name)
        to[...] = getattr(found, name).astype(to.dtype)
    for n in range(images):
        on_result(n, found.result[at[n]])
    squares = found.squares
    return center, inv_std, squares


def stage_backward(
    layer, place, grad_of, center, inv_std, conv, par, weights, kept, gb, gu, small, rows_ref, outs,
    dp, *, images, side,
):
    rows = side * WIDE
    features = gb.shape[1]
    grad_low, gpre, gc = rows_ref
    found = backward_rows(
        grad_of(),
        kept.uhat[...],
        kept.inv_norm[...],
        kept.slope[...].astype(F32),
        weights[0],
        par.layer_gain[layer : layer + 1, :],
        weights[1],
        weights[2],
    )
    grad_low[...] = found.grad_low
    gpre[...] = found.gpre
    gc[...] = found.gc
    gu[...] = found.gu.astype(gu.dtype)
    gain, bias = found.gain, found.bias
    offset = scale = cross = None
    for n in range(images):
        at = slice(n * rows, (n + 1) * rows)
        back, pairs = backward_mixes(found.gj[at], kept.joined[at, 0:features], par.mixing_back[...])
        gb[at, :] = back.astype(gb.dtype)
        offset = add_up(offset, jnp.sum(back, axis=0, keepdims=True))
        ahat = (conv[at, :] - center) * inv_std
        scale = add_up(scale, jnp.sum(back * ahat, axis=0, keepdims=True))
        cross = add_up(cross, pairs)
    small[NORM_ROW[layer] : NORM_ROW[layer] + 1, 0:features] = gain
    groups = par.up_bias.shape[1]
    width = bias.shape[1] // groups
    for j in range(groups):
        small[pl.ds(BIAS_ROW[layer] + (place[0] ^ j), 1), 0:width] = bias[:, j * width : (j + 1) * width]
    wide, tall = mixing_grads(cross, side)
    mixes = slice(layer * WIDE, (layer + 1) * WIDE)
    small[mixes, features : features + WIDE] = wide
    small[mixes, features + WIDE : features + 2 * WIDE] = tall
    unite_grad = dot_rows(kept.joined[...], gc[...])
    normal = (kept.uhat[...] * par.layer_gain[layer : layer + 1, :]).astype(BF16)
    up_grad = dot_rows(normal, gpre[...])
    down_grad = dot_rows(grad_low[...], kept.hidden[...])
    pack_grads(unite_grad, up_grad, down_grad, place[1], outs, dp)
    return offset, scale


def first_body(ins, outs, tmp, *, images, side):
    place, taps = ins.place, ins.taps
    own, conv, moments = outs.own, outs.conv, outs.moments
    every = tmp.every
    rows = side * WIDE
    by_image(ins.stream, every)
    for n in range(images):
        own[n * rows : (n + 1) * rows, :] = every[place[0] * images + n]
    for n in range(images):
        at = slice(n * rows, (n + 1) * rows)
        conv[at, :] = convolve(own[at, :], taps[:, 0, :], side)
    local_moments(conv, moments, images, side)


def other_body(ins, outs, tmp, *, images, side):
    rows = side * WIDE
    by_image(ins.cotangent, tmp.every)
    for n in range(images):
        outs.cotangent[n * rows : (n + 1) * rows, :] = tmp.every[ins.place[0] * images + n]
    _, groups, width = outs.up_bias.shape
    for j in range(groups):
        outs.up_bias[:, j, :] = ins.up_bias[:, j * width : (j + 1) * width]
    mixes = ins.mix_w[...].astype(F32), ins.mix_h[...].astype(F32)
    for layer in range(ins.mix_w.shape[1]):
        outs.mixing[layer][...], outs.mixing_back[layer][...] = mixing_matrices(
            *(mix[:, layer, :].astype(BF16) for mix in mixes), side
        )


def middle_body(ins, outs, tmp, *, images, side):
    rows = side * WIDE
    weights = tmp.unite, tmp.up, tmp.down
    results = []

    def weights_of():
        unpack_weights(tmp, *weights)

    center, inv_std, squares = stage_forward(
        0, ins, weights, weights_of, outs, lambda n, result: results.append(result), images=images, side=side
    )
    outs.stats[0:1, :] = center
    outs.stats[1:2, :] = inv_std
    outs.squares[...] = squares
    for n, result in enumerate(results):
        at = slice(n * rows, (n + 1) * rows)
        outs.stream1[at, :] = result
        outs.conv1[at, :] = convolve(result, ins.taps[:, 1, :], side)
    local_moments(outs.conv1, outs.moments1, images, side)


def last_body(ins, outs, tmp, *, images, side, dp):
    weights = tmp.unite, tmp.up, tmp.down
    results = []

    def weights_of():
        unpack_weights(tmp, *weights)

    center, inv_std, squares = stage_forward(
        1, ins, weights, weights_of, tmp, lambda n, result: results.append(result), images=images, side=side
    )
    outs.result[...] = pack_image_rows(jnp.concatenate(results, axis=0), side).astype(BF16)
    outs.stats[0:1, :] = center
    outs.stats[1:2, :] = inv_std
    outs.small[...] = jnp.zeros_like(outs.small)
    offset, scale = stage_backward(
        1, ins.place, lambda: ins.cotangent[...], center, inv_std,
        ins.conv, ins, weights, tmp, outs.gb, outs.gu, outs.small,
        (tmp.grad_low, tmp.gpre, tmp.gc), outs, dp, images=images, side=side,
    )
    features = squares.shape[1]
    outs.small[SQUARES_ROW[1] : SQUARES_ROW[1] + 3, 0:features] = squares
    to_all(outs.sums, 0, offset)
    to_all(outs.sums, 1, scale)


def conv_back(layer, sums, gb, gu, conv, stats, par, totals, *, images, side):
    rows = side * WIDE
    features = gb.shape[1]
    cells = images * side * side * sums.shape[0]
    offset = jnp.sum(sums[:, 0, 0:features], axis=0, keepdims=True)
    scale = jnp.sum(sums[:, 1, 0:features], axis=0, keepdims=True)
    totals[0:1, :] = offset
    totals[1:2, :] = scale
    center, inv_std = stats[0:1, :], stats[1:2, :]
    factor = par.batch_gain[layer : layer + 1, :] * inv_std
    found = []
    for n in range(images):
        at = slice(n * rows, (n + 1) * rows)
        found.append(
            conv_back_image(
                gb[at, :].astype(F32),
                (conv[at, :] - center) * inv_std,
                gu[at, :].astype(F32),
                factor,
                offset / cells,
                scale / cells,
                par.taps[:, layer, :],
                side,
            )
        )
    return found


def taps_body(ins, outs, tmp, *, images, side):
    rows = side * WIDE
    center, inv_std = ins.stats[0:1, :], ins.stats[1:2, :]
    plain = scaled = None
    for n in range(images):
        at = slice(n * rows, (n + 1) * rows)
        stream = ins.stream[at, :]
        valid = valid_rows(rows, side)
        ones = jnp.where(valid, jnp.ones_like(stream), 0.0)
        ahat = jnp.where(valid, (ins.conv[at, :] - center) * inv_std, 0.0)
        plain = add_up(plain, tap_sums(ones, stream))
        scaled = add_up(scaled, tap_sums(ahat, stream))
    outs.plain[...] = plain
    outs.scaled[...] = scaled


def between_body(ins, outs, tmp, *, images, side, dp):
    weights = tmp.unite, tmp.up, tmp.down
    unpack_weights(tmp, *weights)
    rows = side * WIDE
    features = ins.gb1.shape[1]
    small, sums = tmp.small, outs.sums
    small[...] = ins.small[...]
    grads, kernel = [], None
    found = conv_back(
        1, ins.sums1, ins.gb1, ins.gu1, ins.conv1, ins.stats1, ins, outs.totals1, images=images, side=side
    )
    for n, (grad, ga) in enumerate(found):
        grads.append(grad)
        kernel = add_up(kernel, tap_sums(ga, ins.stream1[n * rows : (n + 1) * rows, :]))
    small[TAPS_ROW : TAPS_ROW + 9, 0:features] = kernel
    stats = ins.stats0
    offset, scale = stage_backward(
        0, ins.place, lambda: jnp.concatenate(grads, axis=0), stats[0:1, :], stats[1:2, :], ins.conv0, ins, weights, ins,
        tmp.gb, tmp.gu, small, (tmp.grad_low, tmp.gpre, tmp.gc), outs, dp,
        images=images, side=side,
    )
    kernel = None
    for n in range(images):
        at = slice(n * rows, (n + 1) * rows)
        kernel = add_up(kernel, tap_sums(tmp.gb[at, :], ins.stream0[at, :]))
    for k, values in enumerate((kernel, ins.plain[...], ins.scaled[...])):
        small[9 * k : 9 * k + 9, 0:features] = values
    small[SQUARES_ROW[0] : SQUARES_ROW[0] + 3, 0:features] = ins.squares0[...]
    cells = images * side * side
    center, inv_std = stats[0:1, :], stats[1:2, :]
    grads = []
    for n in range(images):
        at = slice(n * rows, (n + 1) * rows)
        ahat = (ins.conv0[at, :] - center) * inv_std
        factor = ins.batch_gain[0:1, :] * inv_std
        grad, _ = conv_back_image(
            tmp.gb[at, :], ahat, tmp.gu[at, :], factor, offset / cells, scale / cells, ins.taps[:, 0, :], side
        )
        grads.append(grad)
    outs.grad[...] = pack_image_rows(jnp.concatenate(grads, axis=0), side).astype(BF16)
    to_all(sums, 0, offset)
    to_all(sums, 1, scale)
    devices, height, _ = sums.shape
    for g in range(height - 2):
        held = min(devices, SMALL_ROWS - g * devices)
        sums[0:held, 2 + g, :] = small[g * devices : g * devices + held, :]
        if held < devices:
            sums[held:, 2 + g, :] = jnp.zeros((devices - held, SMALL_WIDE), F32)


def final_body(ins, outs, tmp, *, images, side):
    held, rows, features = tmp.every.shape
    sums = ins.sums0
    cells = images * side * side
    devices = sums.shape[0]
    group = held // images
    offset = jnp.sum(sums[:, 0, 0:features], axis=0, keepdims=True)
    scale = jnp.sum(sums[:, 1, 0:features], axis=0, keepdims=True)
    for row, total in enumerate((offset, scale)):
        to = (outs.offset_grad, outs.scale_grad)[row]
        to[0:1, :] = total
        to[1:2, :] = ins.totals1[row : row + 1, :]
    center, inv_std = ins.stats0[0:1, :], ins.stats0[1:2, :]
    factor = ins.batch_gain[0:1, :] * inv_std
    first = ins.place[1] * group

    def apart(row, total):
        own = [sums[first + p, row : row + 1, 0:features] for p in range(group)]
        own = jnp.concatenate([value for value in own for _ in range(images)], axis=0)
        return factor * (total / (cells * devices) - own / cells)

    shift, slant = apart(0, offset), apart(1, scale)
    put_images(ins.place[0], ins.parts, tmp.every, images, side)
    padded, fields = tmp.padded, tmp.fields
    for ref in (padded, fields):
        edge = jnp.zeros((1,) + ref.shape[1:], F32)
        ref[0:1] = edge
        ref[side + 1 : side + 2] = edge
        edge = jnp.zeros((side, 1) + ref.shape[2:], F32)
        ref[1 : side + 1, 0:1] = edge
        ref[1 : side + 1, side + 1 : side + 2] = edge
    padded[1 : side + 1, 1 : side + 1] = ins.stream[...]
    taps = ins.taps[:, 0, :]
    for h in range(side):
        conv = None
        for i in range(3):
            for j in range(3):
                term = padded[h + i, j : j + side] * taps[3 * i + j : 3 * i + j + 1]
                conv = add_up(conv, term)
        fields[h + 1, 1 : side + 1] = shift + (conv - center) * inv_std * slant
    for h in range(side):
        lines = jnp.swapaxes(tmp.every[:, h * WIDE : (h + 1) * WIDE, :], 0, 1)[:side]
        for i in range(3):
            for j in range(3):
                lines = lines - fields[h + 2 - i, 2 - j : 2 - j + side] * taps[3 * i + j : 3 * i + j + 1]
        outs.out[h] = lines


def put_images(place, parts, every, images, side):
    features = every.shape[2]
    for j, part in enumerate(parts):
        packed = part[...].astype(F32)
        lines = packed.shape[0] // side
        for half in range(2):
            values = packed[:, half * features : (half + 1) * features]
            for k in range(lines):
                n, h = divmod(half * lines + k, side)
                every[(place ^ j) * images + n, h * WIDE : h * WIDE + side, :] = values[
                    k * side : (k + 1) * side
                ]


def gather_body(ins, outs, tmp):
    for g in range(outs.message.shape[1]):
        to_all(outs.message, g, jnp.sum(ins.sums0[:, 2 + g, :], axis=0, keepdims=True))


def spread_body(ins, outs, tmp, *, images, side):
    put_images(ins.place[0], ins.parts, tmp.every, images, side)
    for h in range(side):
        outs.out[h] = jnp.swapaxes(tmp.every[:, h * WIDE : (h + 1) * WIDE, :], 0, 1)[:side]


def core_body(ins, outs, tmp):
    apart = isinstance(outs.parts, list)
    for k in range(ins.keep.shape[0]):
        at = (ins.place[1] >> 1) ^ k if apart else k
        to = outs.parts[k] if apart else outs.parts.at[k]
        to[...] = (ins.keep[at].astype(F32) + ins.got[at].astype(F32)).astype(BF16)


def chips_body(ins, outs, tmp):
    groups = len(outs.give)
    blocks = [[] for _ in range(groups)]
    for parts in ins.parts:
        parts = parts if isinstance(parts, list) else [parts.at[k] for k in range(parts.shape[0])]
        total = parts[0][...].astype(F32)
        for other in parts[1:]:
            total = total + other[...].astype(F32)
        part = total.shape[0] // 3
        width = total.shape[1] // groups
        features = outs.give[0].shape[1] // len(ins.parts) - 2 * width
        for j in range(groups):
            block = jnp.concatenate(
                [
                    total[:part, j * width : (j + 1) * width],
                    total[part : 2 * part, j * width : (j + 1) * width],
                    *[
                        total[2 * part :, q * SMALL_WIDE : q * SMALL_WIDE + features // 3]
                        for q in range(3)
                    ],
                ],
                axis=1,
            )
            blocks[j].append(block)
    for give, block in zip(outs.give, blocks):
        give[...] = jnp.concatenate(block, axis=1).astype(BF16)


def weights_body(ins, outs, tmp):
    layers = outs.up_grad.shape[0]
    for layer in range(layers):
        size = ins.got[0].shape[1] // layers
        terms = [ref[:, layer * size : (layer + 1) * size].astype(F32) for ref in ins.got]
        while len(terms) > 1:
            terms = [terms[j] + terms[j + 1] for j in range(0, len(terms), 2)]
        total = terms[0]
        width = outs.up_grad.shape[2]
        features = outs.unite_grad.shape[1]
        outs.up_grad[layer] = total[:, :width]
        outs.down_grad[layer] = total[:, width : 2 * width]
        rest = total[:, 2 * width :]
        rows = jnp.concatenate([rest[:, q * features : (q + 1) * features] for q in range(3)], axis=0)
        outs.unite_grad[layer] = rows.T


def small_body(ins, outs, tmp, *, side, cells, entries):
    got = ins.got
    features = outs.gain_grad.shape[1]
    devices, height, _ = got.shape
    values = tmp.values
    for g in range(height):
        values[g * devices : (g + 1) * devices, :] = got[:, g, :]
    factor = ins.batch_gain[0:1, :] * ins.stats0[1:2, :]
    first = factor * (
        values[0:9, 0:features]
        - ins.offset[0:1, :] / cells * values[9:18, 0:features]
        - ins.scale[0:1, :] / cells * values[18:27, 0:features]
    )
    for k in range(9):
        outs.kernel_grad[k, 0:1, :] = first[k : k + 1]
        outs.kernel_grad[k, 1:2, :] = values[TAPS_ROW + k : TAPS_ROW + k + 1, 0:features]
    width = outs.bias_grad.shape[1]
    for layer in range(2):
        outs.gain_grad[layer : layer + 1, :] = values[NORM_ROW[layer] : NORM_ROW[layer] + 1, 0:features]
        outs.bias_grad[layer : layer + 1, :] = values[pl.ds(BIAS_ROW[layer] + ins.place[0], 1), 0:width]
        rows = slice(layer * WIDE, layer * WIDE + side)
        outs.width_grad[:, layer, :] = values[rows, features : features + side]
        outs.height_grad[:, layer, :] = values[rows, features + WIDE : features + WIDE + side]
        squares = values[SQUARES_ROW[layer] : SQUARES_ROW[layer] + 3, 0:features]
        outs.stream_rms[:, layer : layer + 1] = jnp.sqrt(
            jnp.sum(squares, axis=1, keepdims=True) / entries
        )


def call(body, ins, outs, scratch=None, shards=(), micros=0, vmem=VMEM_LIMIT, **static):
    ins = dict(ins, shards=list(shards))
    operands, in_tree = jax.tree.flatten(ins)
    shapes, out_tree = jax.tree.flatten(
        {name: jax.tree.map(lambda shape: jax.ShapeDtypeStruct(*shape), outs[name], is_leaf=is_shape) for name in outs}
    )
    scratch = dict(scratch or {})
    if shards:
        scratch["packed"] = (len(shards),) + shards[0].shape, shards[0].dtype
    tmp_names = list(scratch)

    def kernel(*refs):
        cut = len(operands), len(operands) + len(shapes)
        given = SimpleNamespace(**jax.tree.unflatten(in_tree, refs[: cut[0]]))
        results = SimpleNamespace(**jax.tree.unflatten(out_tree, refs[cut[0] : cut[1]]))
        tmp = SimpleNamespace(**dict(zip(tmp_names, refs[cut[1] :])))
        for k, shard in enumerate(given.shards):
            tmp.packed[given.place[1] ^ k] = shard[...]
        body(given, results, tmp, **static)

    def space(name):
        return pl.BlockSpec(memory_space=pltpu.SMEM if name == "place" else pltpu.VMEM)

    found = pl.pallas_call(
        kernel,
        out_shape=shapes,
        in_specs=jax.tree.leaves({name: jax.tree.map(lambda _: space(name), ins[name]) for name in ins}),
        out_specs=[space("")] * len(shapes),
        scratch_shapes=[pltpu.VMEM(*scratch[name]) for name in tmp_names],
        compiler_params=pltpu.CompilerParams(vmem_limit_bytes=vmem),
        cost_estimate=pl.CostEstimate(
            flops=int(micros * COST_FLOPS), transcendentals=0, bytes_accessed=int(micros * COST_BYTES)
        ),
    )(*operands)
    return SimpleNamespace(**jax.tree.unflatten(out_tree, found))


def is_shape(value):
    return isinstance(value, tuple)


def swap(values, axis, mask):
    return lax.ppermute(values, axis, [(i, i ^ mask) for i in range(lax.axis_size(axis))])


def after(values, *others):
    return lax.optimization_barrier((values, others))[0]


def per_device(
    inputs,
    conv_weight,
    batch_gain,
    batch_bias,
    mix_width,
    mix_height,
    unite_weight,
    layer_gain,
    up_weight,
    up_bias,
    down_weight,
    cotangent,
):
    held, side, _, features = inputs.shape
    layers = conv_weight.shape[0]
    dp, mp = lax.axis_size("dp"), lax.axis_size("mp")
    devices = dp * mp
    images = held // mp
    cells = side * WIDE
    rows = images * cells
    units = up_bias.shape[1]
    part = features // dp
    both = ("dp", "mp")
    sizes = dict(images=images, side=side)
    place = jnp.stack([lax.axis_index("mp"), lax.axis_index("dp")]).astype(jnp.int32)

    def group_parts(values):
        if isinstance(values, (list, tuple)):
            far_first = {j: swap(values[j], "mp", j) for j in range(mp - 1, 0, -1)}
            return [far_first.get(j, value) for j, value in enumerate(values)]
        parts = [values]
        for j in range(1, mp):
            step = j & -j
            parts.append(swap(parts[j ^ step], "mp", step))
        return parts

    def share(blocks):
        return lax.all_to_all(blocks, both, 0, 0, tiled=False)

    maps = jnp.transpose(inputs, (1, 2, 0, 3))
    cotangent_maps = jnp.transpose(cotangent, (1, 2, 0, 3))
    taps = jnp.transpose(conv_weight, (1, 0, 2))
    mix_w, mix_h = (jnp.transpose(mix, (1, 0, 2)) for mix in (mix_width, mix_height))
    shared = (devices, 2, features)
    thirds = unite_weight.reshape(layers, 3, part, features)
    beside = [(0, 0), (0, 0), (0, SMALL_WIDE - features)]
    thirds = jnp.concatenate([jnp.pad(thirds[:, q], beside) for q in range(3)], axis=2)
    thirds = jnp.pad(thirds, ((0, 0), (0, 0), (0, units - 3 * SMALL_WIDE)))

    def widen(wide, step):
        return jnp.concatenate([wide, swap(wide, "mp", step)], axis=1)

    def over_dp(layer, wide, wait_chips, wait_core):
        piece = after(jnp.concatenate([wide, thirds[layer]], axis=0), *wait_chips)
        shards = [piece] + [swap(piece, "dp", 2 * k) for k in range(1, dp // 2)]
        mates = [swap(after(shard, *wait_core), "dp", 1) for shard in shards]
        return [shard for pair in zip(shards, mates) for shard in pair]

    wide = jnp.concatenate([up_weight[0], down_weight[0]], axis=0)
    wide = near = widen(wide, 1) if mp > 1 else wide
    step = 2
    while step < mp:
        wide = widen(wide, step)
        step *= 2
    found = call(
        first_body,
        dict(place=after(place, near), stream=maps, taps=taps),
        dict(own=((rows, features), F32), conv=((rows, features), F32), moments=(shared, F32)),
        dict(every=((held, cells, features), F32)),
        micros=4,
        **sizes,
    )
    moments0 = share(after(found.moments, wide))
    other = call(
        other_body,
        dict(place=place, cotangent=cotangent_maps, mix_w=mix_w, mix_h=mix_h, up_bias=up_bias),
        dict(
            cotangent=((rows, features), F32),
            up_bias=((layers, mp, units // mp), F32),
            mixing=[((2 * cells, cells), BF16)] * layers,
            mixing_back=[((cells, 2 * cells), BF16)] * layers,
        ),
        dict(every=((held, cells, features), F32)),
        micros=3,
        **sizes,
    )

    packed = [over_dp(0, wide, (found.moments,), (moments0, other.mixing[0]))]
    wide = after(jnp.concatenate([up_weight[1], down_weight[1]], axis=0), wide)
    step = 1
    while step < mp:
        wide = widen(wide, step)
        step *= 2
    wide1 = wide

    own, conv0 = found.own, found.conv
    par = dict(
        place=place,
        taps=taps,
        batch_gain=batch_gain,
        batch_bias=batch_bias,
        layer_gain=layer_gain,
        up_bias=other.up_bias,
    )
    kept = dict(
        joined=((rows, 3 * features), BF16),
        uhat=((rows, features), F32),
        inv_norm=((rows, 1), F32),
        slope=((rows, units), BF16),
        hidden=((rows, units), BF16),
    )
    weight_tmp = dict(
        unite=((3 * features, features), BF16),
        up=((features, units), BF16),
        down=((features, units), BF16),
    )
    back_tmp = dict(
        grad_low=((rows, features), BF16), gpre=((rows, units), BF16), gc=((rows, features), BF16)
    )
    back_outs = dict(gb=((rows, features), F32), gu=((rows, features), F32))
    stats = ((2, features), F32)
    pieces = [((dp // 2, 3 * part, units), BF16)] * 2
    piece = ((3 * part, units), BF16)

    def over_core(values, apart=False):
        return call(
            core_body,
            dict(place=place, keep=values.keep, got=swap(values.give, "dp", 1)),
            dict(parts=[piece] * (dp // 2) if apart else pieces[0]),
            vmem=SMALL_LIMIT,
        ).parts

    def from_chips(parts):
        if isinstance(parts, list):
            return [swap(values, "dp", 2 * k) if k else values for k, values in enumerate(parts)]
        groups = [[2 * q + c for q in range(dp // 2)] for c in range(2)]
        return lax.all_to_all(parts, "dp", 0, 0, axis_index_groups=groups, tiled=False)

    mid = call(
        middle_body,
        dict(
            par,
            moments=moments0,
            conv=conv0,
            stream=own,
            mixing=other.mixing[0],
        ),
        dict(
            kept,
            stream1=((rows, features), F32),
            conv1=((rows, features), F32),
            moments1=(shared, F32),
            stats=stats,
            squares=((3, features), F32),
        ),
        weight_tmp,
        packed[0],
        micros=6,
        **sizes,
    )
    packed.append(over_dp(1, wide1, packed[0][::2], (mid.moments1,)))
    under = call(
        taps_body,
        dict(stream=own, conv=conv0, stats=mid.stats),
        dict(plain=((9, features), F32), scaled=((9, features), F32)),
        micros=2,
        **sizes,
    )
    last = call(
        last_body,
        dict(
            par,
            moments=after(share(mid.moments1), under.plain),
            conv=mid.conv1,
            stream=mid.stream1,
            mixing=other.mixing[1],
            mixing_back=other.mixing_back[1],
            cotangent=other.cotangent,
        ),
        dict(
            gb=((rows, features), BF16),
            gu=((rows, features), BF16),
            result=((images * side * side // 2, 2 * features), BF16),
            stats=stats,
            small=((SMALL_ROWS, SMALL_WIDE), F32),
            sums=(shared, F32),
            keep=pieces[0],
            give=pieces[1],
        ),
        dict(
            dict(kept, slope=((rows, units), F32)),
            **weight_tmp,
            **back_tmp,
        ),
        packed[1],
        micros=10,
        dp=dp,
        **sizes,
    )
    summed1 = over_core(last)
    groups = -(-SMALL_ROWS // devices)
    between = call(
        between_body,
        {
            **par,
            **{name: getattr(mid, name) for name in kept},
            **dict(
                sums1=after(share(last.sums), summed1),
                gb1=last.gb,
                gu1=last.gu,
                conv1=mid.conv1,
                stream1=mid.stream1,
                stats1=last.stats,
                small=last.small,
                stream0=own,
                plain=under.plain,
                scaled=under.scaled,
                conv0=conv0,
                stats0=mid.stats,
                squares0=mid.squares,
                mixing_back=other.mixing_back[0],
            ),
        },
        dict(
            grad=((images * side * side // 2, 2 * features), BF16),
            totals1=stats,
            sums=((devices, 2 + groups, SMALL_WIDE), F32),
            keep=pieces[0],
            give=pieces[1],
        ),
        dict(
            back_tmp,
            **back_outs,
            **weight_tmp,
            small=((SMALL_ROWS, SMALL_WIDE), F32),
        ),
        packed[0],
        micros=10,
        dp=dp,
        **sizes,
    )
    result_parts = [last.result] + [swap(last.result, "mp", 1 << k) for k in range((mp - 1).bit_length())]
    parts1 = from_chips(summed1)
    grad, sums0, give, parts1, near = lax.optimization_barrier(
        (between.grad, between.sums, between.give, parts1, result_parts[1:])
    )
    result_parts = [last.result]
    for j in range(1, mp):
        step = j & -j
        result_parts.append(near[j.bit_length() - 1] if j == step else swap(result_parts[j ^ step], "mp", step))
    sums0 = share(sums0)
    chunk = call(
        gather_body, dict(sums0=sums0), dict(message=((devices, groups, SMALL_WIDE), F32)), vmem=SMALL_LIMIT
    )
    shared_small = share(chunk.message)
    summed0 = over_core(SimpleNamespace(keep=between.keep, give=give), True)
    summed0 = after(summed0, result_parts)
    grad_parts = group_parts(after(grad, summed0))
    cut = call(
        chips_body,
        dict(parts=[from_chips(summed0), parts1]),
        dict(give=[((part, layers * (2 * (units // mp) + 3 * features)), BF16)] * mp),
        vmem=SMALL_LIMIT,
    ).give
    grads = call(
        weights_body,
        dict(got=group_parts(after(cut, grad_parts, shared_small))),
        dict(
            up_grad=((layers, part, units // mp), F32),
            down_grad=((layers, part, units // mp), F32),
            unite_grad=((layers, features, 3 * part), F32),
        ),
        vmem=SMALL_LIMIT,
    )
    whole_maps = ((side, side, held, features), F32)
    output = call(
        spread_body,
        dict(place=place, parts=result_parts),
        dict(out=whole_maps),
        dict(every=((held, cells, features), F32)),
        **sizes,
    ).out
    padded = ((side + 2, side + 2, held, features), F32)
    end = call(
        final_body,
        dict(
            place=place,
            parts=grad_parts,
            stream=maps,
            sums0=sums0,
            totals1=between.totals1,
            stats0=mid.stats,
            batch_gain=batch_gain,
            taps=taps,
        ),
        dict(out=whole_maps, offset_grad=stats, scale_grad=stats),
        dict(every=((held, cells, features), F32), padded=padded, fields=padded),
        vmem=36 * 1024 * 1024,
        **sizes,
    )
    outputs = [jnp.transpose(out, (2, 0, 1, 3)) for out in (output, end.out)]
    small = call(
        small_body,
        dict(
            place=place,
            got=shared_small,
            batch_gain=batch_gain,
            stats0=mid.stats,
            offset=end.offset_grad,
            scale=end.scale_grad,
        ),
        dict(
            kernel_grad=((9, layers, features), F32),
            gain_grad=((layers, features), F32),
            bias_grad=((layers, units // mp), F32),
            width_grad=((side, layers, side), F32),
            height_grad=((side, layers, side), F32),
            stream_rms=((3, layers), F32),
        ),
        dict(values=((groups * devices, SMALL_WIDE), F32)),
        vmem=SMALL_LIMIT,
        side=side,
        cells=images * side * side * devices,
        entries=held * side * side * features * dp,
    )
    return (
        *outputs,
        jnp.transpose(small.kernel_grad, (1, 0, 2)),
        end.scale_grad,
        end.offset_grad,
        jnp.transpose(small.width_grad, (1, 0, 2)),
        jnp.transpose(small.height_grad, (1, 0, 2)),
        jnp.transpose(grads.unite_grad, (0, 2, 1)),
        small.gain_grad,
        grads.up_grad,
        small.bias_grad,
        grads.down_grad,
        small.stream_rms.T,
    )


def solution(mesh):
    in_specs = (
        P("dp", None, None, None),
        P(),
        P(),
        P(),
        P(),
        P(),
        P(None, "dp", None),
        P(),
        P(None, "dp", "mp"),
        P(),
        P(None, "dp", "mp"),
        P("dp", None, None, None),
    )
    out_specs = (
        P("dp", None, None, None),
        P("dp", None, None, None),
        P(),
        P(),
        P(),
        P(),
        P(),
        P(None, "dp", None),
        P(),
        P(None, "dp", "mp"),
        P(None, "mp"),
        P(None, "dp", "mp"),
        P(),
    )
    return jax.shard_map(
        per_device, mesh=mesh, in_specs=in_specs, out_specs=out_specs, check_vma=False
    )
```
